256 devices in a mesh: tile: 32 (over y, x, core), sta: 8 (over z).
Axes of the slice: x: 4, y: 4, z: 8, core: 2. Of those that a mesh axis runs over, the one named last changes fastest.
Arguments:
- waves: bfloat16 [2048, 3, 64, 1024], P('tile', None, 'sta'), may hold values from -6 to 6
- station_mask: int32 [2048, 64], P('tile', 'sta'), may hold values 0 or 1
- pair_local: int32 [32, 32, 8], P('tile'), may hold values from 0 to 63
- pair_remote: int32 [32, 32, 8], P('tile'), may hold values from 0 to 63
- pair_count: int32 [32, 32], P('tile'), may hold values from 0 to 8, as said below
Outputs:
- station_coef: bfloat16 [32, 32, 8, 64, 128], P('tile', None, None, 'sta')
- stack: float32 [32, 32, 8, 128], P('tile', None, None, 'sta')
The draws below stay inside these ranges and needn't reach their ends.
Inputs may be any that keep to these rules, and one draw needn't show every extreme that they name: `pair_count`: in every draw some tile has exactly 8 live slots toward some partner tile; a quarter of the tiles are dense on average.
All inputs are finite; a program needn't handle non-finite values. No bound on the sum of `station_mask` on one device may be relied on, other than what follows from the above.
Results may differ from the reference program's by a relative error of at most 0.015.
Values may be sent and summed in bfloat16 or wider, within the bound.
No kernel may reach another device: no remote copies, remote signals or barrier semaphores. Data moves between devices by JAX's collectives and lax.ppermute only.
A program may use at most 128 MiB of HBM per device.

```python
import math
import jax
import jax.numpy as jnp
from jax import lax

SAMPLES = 1024
BAND = 256
LAGS = 128
STATIONS = 64
EV_DEV = 64
PEER_CAP = 8
TILES = 32
EVENTS = 2048


def draw_pair_count(key, part):
    key = jax.random.fold_in(key, 11)
    keys = jax.random.split(key, 5)
    dense = jax.random.randint(keys[0], (TILES, 1), 0, 4) == 0
    high = jax.random.randint(keys[1], (TILES, TILES), PEER_CAP // 2, PEER_CAP + 1)
    lower = jax.random.randint(keys[2], (TILES, TILES), 0, PEER_CAP // 4 + 1)
    counts = jnp.where(dense, high, lower)
    row_pick = jax.random.randint(keys[3], (), 0, TILES)
    col_pick = jax.random.randint(keys[4], (), 0, TILES)
    return counts.at[row_pick, col_pick].set(PEER_CAP).astype(jnp.int32)


def touch_ends(drawn, stream_key, smallest, top_value):
    spot = [jax.random.randint(jax.random.fold_in(stream_key, axis), (), 0, length) for axis, length in enumerate(drawn.shape)]
    main_axis = drawn.shape.index(max(drawn.shape))
    beside = spot[:main_axis] + [(spot[main_axis] + 1) % drawn.shape[main_axis]] + spot[main_axis + 1:]
    return drawn.at[tuple(spot)].set(smallest).at[tuple(beside)].set(top_value)


def level_of(rng, extent, cuts, least, largest):
    def one(axis_at, shards_of):
        draws = jax.random.uniform(jax.random.fold_in(jax.random.fold_in(rng, 6), axis_at), (shards_of,), jnp.float32, least / len(cuts), largest / len(cuts))
        return jnp.repeat(jnp.exp(draws), extent[axis_at] // shards_of).reshape((-1,) + (1,) * (len(extent) - axis_at - 1))

    factor_of = one(*cuts[0])
    for cut in cuts[1:]:
        factor_of = factor_of * one(*cut)
    return factor_of


def scatter_about(key, dims, scale, bound, cuts=(), kind=jnp.bfloat16):
    entries = scale * jax.random.normal(key, dims, jnp.float32)
    if cuts:
        entries = entries * level_of(key, dims, cuts, -0.22, 0.18)
    return jnp.clip(entries, -bound, bound).astype(kind)


def setup_inputs(seed: int = 0) -> dict:
    key_of = jax.random.split(jax.random.key(seed), 6)
    waves = scatter_about(key_of[0], (EVENTS, 3, STATIONS, SAMPLES), 1.0, 6.0, ((0, 32), (2, 8)))
    station_mask = touch_ends((jax.random.randint(key_of[1], (EVENTS, STATIONS), 0, 8) < 7).astype(jnp.int32), jax.random.fold_in(key_of[1], 1), 0, 1)
    pair_local = touch_ends(jax.random.randint(key_of[2], (TILES, TILES, PEER_CAP), 0, EV_DEV), jax.random.fold_in(key_of[2], 1), 0, EV_DEV - 1).astype(jnp.int32)
    pair_remote = touch_ends(jax.random.randint(key_of[3], (TILES, TILES, PEER_CAP), 0, EV_DEV), jax.random.fold_in(key_of[3], 1), 0, EV_DEV - 1).astype(jnp.int32)
    pair_count = draw_pair_count(jax.random.fold_in(key_of[5], 71), 0)
    return {"waves": waves, "station_mask": station_mask, "pair_local": pair_local, "pair_remote": pair_remote, "pair_count": pair_count}


def forward_table(width, band):
    times = jnp.arange(width, dtype=jnp.int32)[:, None]
    bins = jnp.arange(1, band + 1, dtype=jnp.int32)[None, :]
    phase = (times * bins % width).astype(jnp.float32) * (2.0 * math.pi / width)
    return jnp.concatenate([jnp.cos(phase), -jnp.sin(phase)], 1).astype(jnp.bfloat16)

def inverse_table(width, band, count):
    bins = jnp.arange(1, band + 1, dtype=jnp.int32)[:, None]
    shifts = jnp.arange(count, dtype=jnp.int32)[None, :] - count // 2
    phase = (bins * shifts % width).astype(jnp.float32) * (2.0 * math.pi / width)
    return jnp.concatenate([jnp.cos(phase), -jnp.sin(phase)], 0).astype(jnp.bfloat16)

def spectra_of(windows, forward):
    shape = windows.shape
    flat = jnp.dot(windows.reshape(-1, shape[-1]), forward, preferred_element_type=jnp.float32)
    return flat.astype(jnp.bfloat16).reshape(shape[:-1] + (forward.shape[1],))

def energy_of(spectra, width):
    values = spectra.astype(jnp.float32)
    return 2.0 / width * lax.optimization_barrier(jnp.sum(values * values, axis=(1, 3)))

def coefficients(spectra_a, spectra_b, valid, lag_table, width):
    half = spectra_a.shape[-1] // 2
    first = spectra_a.astype(jnp.float32)
    second = spectra_b.astype(jnp.float32)
    real_a, imag_a = (first[..., :half], first[..., half:])
    real_b, imag_b = (second[..., :half], second[..., half:])
    real_part = lax.optimization_barrier(jnp.sum(real_a * real_b + imag_a * imag_b, axis=1))
    imag_part = lax.optimization_barrier(jnp.sum(imag_a * real_b - real_a * imag_b, axis=1))
    cross = jnp.concatenate([real_part, imag_part], -1).astype(jnp.bfloat16)
    pairs, stations = (cross.shape[0], cross.shape[1])
    corr = jnp.dot(cross.reshape(-1, 2 * half), lag_table, preferred_element_type=jnp.float32)
    corr = corr.reshape(pairs, stations, -1) * (2.0 / width)
    scale = lax.rsqrt(energy_of(spectra_a, width) * energy_of(spectra_b, width) + 1e-06)
    return corr * (scale * valid)[..., None]

def reference(waves, station_mask, pair_local, pair_remote, pair_count):
    forward = forward_table(SAMPLES, BAND)
    lag_table = inverse_table(SAMPLES, BAND, LAGS)
    blocks = waves.reshape(TILES, EV_DEV, 3, STATIONS, SAMPLES)
    all_spectra = lax.map(lambda events_block: spectra_of(events_block, forward), blocks)
    all_spectra = all_spectra.reshape(EVENTS, 3, STATIONS, 2 * BAND)
    masks = station_mask.astype(jnp.float32)

    def one_tile(tile_index):
        own_rows = tile_index * EV_DEV + pair_local[tile_index].reshape(-1)
        far_rows = (jnp.arange(TILES, dtype=jnp.int32)[:, None] * EV_DEV + pair_remote[tile_index]).reshape(-1)
        live_slot = (jnp.arange(PEER_CAP, dtype=jnp.int32)[None, :] < pair_count[tile_index][:, None]).reshape(-1)
        valid = live_slot.astype(jnp.float32)[:, None] * masks[own_rows] * masks[far_rows]
        coef = coefficients(all_spectra[own_rows], all_spectra[far_rows], valid, lag_table, SAMPLES)
        return (coef.astype(jnp.bfloat16).reshape(TILES, PEER_CAP, STATIONS, LAGS), lax.optimization_barrier(jnp.sum(coef, axis=1)).reshape(TILES, PEER_CAP, LAGS))
    station_coef, stack = lax.map(one_tile, jnp.arange(TILES, dtype=jnp.int32))
    return (station_coef, stack)
```

```python
import functools
import math

import jax
import jax.numpy as jnp
import ml_dtypes
import numpy as np
from jax import lax
from jax.experimental import pallas as pl
from jax.experimental.pallas import tpu as pltpu
from jax.sharding import PartitionSpec as P

BAND = 256
LAGS = 128
SLOTS = 8
SIDE = 4
LANES = 128
ROWS = 48
EVENT_BLOCK = 16
SCALE_WIDTH = 1024.0
VMEM = pl.BlockSpec(memory_space=pltpu.VMEM)
SMEM = pl.BlockSpec(memory_space=pltpu.SMEM)
PARAMS = pltpu.CompilerParams(vmem_limit_bytes=48 * 1024 * 1024)


def forward_table(width):
    phase = np.arange(width)[:, None] * np.arange(1, BAND + 1)[None, :] % width * (2.0 * math.pi / width)
    return np.concatenate([np.cos(phase), -np.sin(phase)], 1).astype(ml_dtypes.bfloat16)


def lag_table(width):
    phase = np.arange(1, BAND + 1)[:, None] * (np.arange(LAGS)[None, :] - LAGS // 2) % width
    phase = phase * (2.0 * math.pi / width)
    table = np.concatenate([np.cos(phase), -np.sin(phase)], 0).astype(ml_dtypes.bfloat16)
    low_re, high_re, low_im, high_im = (table[i * LANES : (i + 1) * LANES] for i in range(4))
    return np.concatenate(
        [np.concatenate([low_re, high_re], 1), np.concatenate([low_im, high_im], 1)], 0
    )


def spectra_kernel(waves_ref, mask_ref, table_ref, first_ref, second_ref, power1_ref, power2_ref):
    events = mask_ref.shape[0]
    flat = jnp.dot(waves_ref[...], table_ref[...], preferred_element_type=jnp.float32)
    flat = flat.reshape(events, 3, 8, 4 * LANES) * mask_ref[...][:, None, :, :1]
    part = [flat[..., i * LANES : (i + 1) * LANES].reshape(events * 3, 8, LANES) for i in range(4)]
    turned = [pltpu.roll(value, 4, 1) for value in part]
    low = lax.broadcasted_iota(jnp.int32, part[0].shape, 1) < 4
    halves = (
        (jnp.where(low, part[0], turned[1]), jnp.where(low, part[2], turned[3])),
        (jnp.where(low, turned[0], part[1]), jnp.where(low, turned[2], part[3])),
    )
    for (real, imag), out_ref, power_ref in zip(
        halves, (first_ref, second_ref), (power1_ref, power2_ref)
    ):
        packed = jnp.concatenate([real, imag], 1).astype(jnp.bfloat16)
        out_ref[...] = packed.reshape(events, ROWS, LANES)
        values = packed.astype(jnp.float32).reshape(events, 3, 2, 8, LANES)
        total = jnp.sum(values * values, axis=(1, 2))
        total = jnp.sum(total, axis=-1, keepdims=True)
        total = (total + pltpu.roll(jnp.broadcast_to(total, (events, 8, LANES)), 4, 1)) * (
            2.0 / SCALE_WIDTH
        )
        power_ref[...] = total


def own_spectra(waves, mask, table):
    events = waves.shape[0]
    flat = waves.reshape(-1, waves.shape[-1])
    block = EVENT_BLOCK
    half = jax.ShapeDtypeStruct((events, ROWS, LANES), jnp.bfloat16)
    power = jax.ShapeDtypeStruct((events, 8, LANES), jnp.float32)
    spec = lambda shape: pl.BlockSpec(shape, lambda i: (i, 0, 0))
    return pl.pallas_call(
        spectra_kernel,
        grid=(events // block,),
        in_specs=[
            pl.BlockSpec((block * 24, flat.shape[-1]), lambda i: (i, 0)),
            spec((block, 8, LANES)),
            pl.BlockSpec(table.shape, lambda i: (0, 0)),
        ],
        out_specs=[spec((block, ROWS, LANES))] * 2 + [spec((block, 8, LANES))] * 2,
        out_shape=[half, half, power, power],
        compiler_params=PARAMS,
        name="spectra",
    )(flat, mask, table)


def tile_of(y, x, core):
    return (lax.rem(y + SIDE, SIDE) * SIDE + lax.rem(x + SIDE, SIDE)) * 2 + core


def pack_kernel(along_x, shifts, place_ref, *refs):
    asked, held = refs[: len(shifts)], refs[len(shifts) : len(shifts) + SIDE]
    outs = refs[len(shifts) + SIDE :]
    y, x, core = place_ref[0], place_ref[1], place_ref[2]
    for number in range(len(shifts)):
        for other in range(2):
            out_ref = outs[number * 2 + other]
            for step in range(SIDE):
                tile = tile_of(y, x - step, core) if along_x else tile_of(y - step, x, core)
                base = other * 256 + tile * SLOTS
                for slot in range(SLOTS):
                    out_ref[step * SLOTS + slot] = held[step][asked[number][base + slot]]


def pack(along_x, shifts, place, asked, held):
    block = jax.ShapeDtypeStruct((SIDE * SLOTS, ROWS, LANES), jnp.bfloat16)
    return pl.pallas_call(
        functools.partial(pack_kernel, along_x, shifts),
        in_specs=[SMEM] * (1 + len(shifts)) + [VMEM] * SIDE,
        out_specs=[VMEM] * (2 * len(shifts)),
        out_shape=[block] * (2 * len(shifts)),
        compiler_params=PARAMS,
        name="pack",
    )(place, *asked, *held)


def pair_kernel(blocks, place_ref, local_ref, count_ref, table_ref, *refs):
    own, power = refs[:2], refs[2:4]
    partner = refs[4 : 4 + len(blocks)]
    _, out_ref, cross_ref, energy_ref, factor_ref = refs[4 + len(blocks) :]
    y, x, core = place_ref[0], place_ref[1], place_ref[2]
    for (half, shift, other), partner_ref in zip(blocks, partner):
        from_core = lax.rem(core + other, 2)

        def tile_at(step):
            if half == 0:
                return tile_of(y - shift, x - step, from_core)
            return tile_of(y - step, x - shift, from_core)

        def one_tile(step, carry):
            tile = tile_at(step)
            live = count_ref[tile]
            for slot in range(SLOTS):
                event = local_ref[tile * SLOTS + slot]
                first = own[half][event].astype(jnp.float32).reshape(3, 2, 8, LANES)
                row = step * SLOTS + slot
                second = partner_ref[row].astype(jnp.float32).reshape(3, 2, 8, LANES)
                real = jnp.sum(first * second, axis=(0, 1))
                imag = jnp.sum(first[:, 1] * second[:, 0] - first[:, 0] * second[:, 1], axis=0)
                cross = jnp.concatenate([real, imag], -1)
                cross_ref[pl.ds(pl.multiple_of(row * 8, 8), 8), :] = cross
                energy_ref[row] = jnp.sum(second * second, axis=(0, 1))
                alive = jnp.where(slot < live, jnp.float32(2.0 / SCALE_WIDTH), jnp.float32(0))
                factor_ref[0, row] = power[half][event]
                factor_ref[1, row] = jnp.full((8, LANES), alive, jnp.float32)
            return carry

        lax.fori_loop(0, SIDE, one_tile, 0)
        rows = SIDE * SLOTS
        corr = jnp.dot(
            cross_ref[...].astype(jnp.bfloat16), table_ref[...], preferred_element_type=jnp.float32
        ).reshape(rows, 8, 2 * LANES)
        low = lax.broadcasted_iota(jnp.int32, (rows, 8, LANES), 1) < 4
        corr = jnp.where(low, corr[..., :LANES], corr[..., LANES:])
        corr = corr + pltpu.roll(corr, 4, 1)
        energy = jnp.broadcast_to(
            jnp.sum(energy_ref[...], axis=-1, keepdims=True), (rows, 8, LANES)
        )
        energy = (energy + pltpu.roll(energy, 4, 1)) * (2.0 / SCALE_WIDTH)
        corr = corr * (lax.rsqrt(factor_ref[0] * energy + 1e-06) * factor_ref[1])
        for step in range(SIDE):
            at = pl.ds(pl.multiple_of(tile_at(jnp.int32(step)) * SLOTS, SLOTS), SLOTS)
            out_ref[at, 4 * half : 4 * half + 4, :] = corr[
                step * SLOTS : (step + 1) * SLOTS, 4 * half : 4 * half + 4
            ]


def pairs(blocks, place, local, count, table, own, power, partner, total):
    rows = SIDE * SLOTS
    return pl.pallas_call(
        functools.partial(pair_kernel, blocks),
        in_specs=[SMEM] * 3 + [VMEM] * (6 + len(blocks)),
        out_specs=VMEM,
        out_shape=jax.ShapeDtypeStruct(total.shape, total.dtype),
        input_output_aliases={8 + len(blocks): 0},
        scratch_shapes=[
            pltpu.VMEM((rows * 8, 2 * LANES), jnp.float32),
            pltpu.VMEM((rows, 8, LANES), jnp.float32),
            pltpu.VMEM((2, rows, 8, LANES), jnp.float32),
        ],
        compiler_params=PARAMS,
        name="pairs",
    )(place, local, count, table, *own, *power, *partner, total)


def hop(value, dy, dx, dcore):
    moves = []
    for y in range(SIDE):
        for x in range(SIDE):
            for core in range(2):
                target = ((y + dy) % SIDE * SIDE + (x + dx) % SIDE) * 2 + (core + dcore) % 2
                moves.append(((y * SIDE + x) * 2 + core, target))
    return lax.ppermute(value, "tile", moves)


def on_device(waves, station_mask, pair_local, pair_remote, pair_count):
    width = waves.shape[-1]
    events, stations = station_mask.shape
    groups = lax.axis_size("sta")
    here = lax.axis_index("tile")
    place = jnp.stack([here // (2 * SIDE), here // 2 % SIDE, here % 2]).astype(jnp.int32)
    local, count = pair_local.reshape(-1), pair_count.reshape(-1)

    wanted = pair_remote.reshape(-1)
    wanted = jnp.concatenate([wanted, hop(wanted, 0, 0, 1)])
    asked_y = [wanted] + [hop(wanted, SIDE - k, 0, 0) for k in range(1, SIDE)]
    asked_x = [wanted] + [hop(wanted, 0, SIDE - k, 0) for k in range(1, SIDE)]

    mask = jnp.broadcast_to(station_mask.astype(jnp.float32)[..., None], (events, stations, LANES))
    own = own_spectra(waves, mask, jnp.asarray(forward_table(width)))
    own, power = own[:2], own[2:]

    held = (
        [own[0]] + [hop(own[0], 0, k, 0) for k in range(1, SIDE)],
        [own[1]] + [hop(own[1], k, 0, 0) for k in range(1, SIDE)],
    )
    asked = (asked_y, asked_x)
    partner = {}
    away = (1, 3, 2)
    for half in range(2):
        sent = pack(half == 0, away, place, [asked[half][m] for m in away], held[half])
        for number, m in enumerate(away):
            for other in range(2):
                shift = (m, 0) if half == 0 else (0, m)
                partner[half, m, other] = hop(sent[2 * number + other], *shift, other)
    for half in range(2):
        near = pack(half == 0, (0,), place, [wanted], held[half])
        partner[half, 0, 0] = near[0]
        partner[half, 0, 1] = hop(near[1], 0, 0, 1)

    table = jnp.asarray(lag_table(width))
    total = jnp.zeros((events * 4, stations, LAGS), jnp.float32)
    for m in (0,) + away:
        blocks = tuple((half, m, other) for half in range(2) for other in range(2))
        total = pairs(
            blocks, place, local, count, table, own, power, [partner[b] for b in blocks], total
        )

    tiles = pair_remote.shape[1]
    station_coef = total.astype(jnp.bfloat16).reshape(1, tiles, SLOTS, stations, LAGS)
    partial_stack = jnp.sum(total, axis=1).T
    parts = lax.all_to_all(partial_stack, "sta", split_axis=0, concat_axis=0, tiled=True)
    stack = jnp.sum(parts.reshape(groups, LAGS // groups, -1), axis=0).T
    return (station_coef, stack.reshape(1, tiles, SLOTS, LAGS // groups))


def solution(mesh):
    placed = (
        P("tile", None, "sta", None),
        P("tile", "sta"),
        P("tile", None, None),
        P("tile", None, None),
        P("tile", None),
    )
    return jax.shard_map(
        on_device,
        mesh=mesh,
        in_specs=placed,
        out_specs=(P("tile", None, None, "sta", None), P("tile", None, None, "sta")),
        check_vma=False,
    )
```

```python
import functools
import math

import jax
import jax.numpy as jnp
import ml_dtypes
import numpy as np
from jax import lax
from jax.experimental import pallas as pl
from jax.experimental.pallas import tpu as pltpu
from jax.sharding import PartitionSpec as P

BAND = 256
LAGS = 128
SLOTS = 8
SIDE = 4
LANES = 128
ROWS = 48
EVENT_BLOCK = 16
BLOCK_ROWS = EVENT_BLOCK * ROWS + 16
HALF_BLOCKS = 2
SCALE_WIDTH = 1024.0
VMEM = pl.BlockSpec(memory_space=pltpu.VMEM)
ANY = pl.BlockSpec(memory_space=pl.ANY)
SMEM = pl.BlockSpec(memory_space=pltpu.SMEM)
PARAMS = pltpu.CompilerParams(vmem_limit_bytes=60 * 1024 * 1024)


def forward_table(width):
    phase = np.arange(width)[:, None] * np.arange(1, BAND + 1)[None, :] % width * (2.0 * math.pi / width)
    return np.concatenate([np.cos(phase), -np.sin(phase)], 1).astype(ml_dtypes.bfloat16)


def lag_table(width):
    phase = np.arange(1, BAND + 1)[:, None] * (np.arange(LAGS)[None, :] - LAGS // 2) % width
    phase = phase * (2.0 * math.pi / width)
    table = np.concatenate([np.cos(phase), -np.sin(phase)], 0).astype(ml_dtypes.bfloat16)
    low_re, high_re, low_im, high_im = (table[i * LANES : (i + 1) * LANES] for i in range(4))
    return np.concatenate(
        [np.concatenate([low_re, high_re], 1), np.concatenate([low_im, high_im], 1)], 0
    )


def spectra_kernel(waves_ref, mask_ref, table_ref, asked_ref, *outs):
    events = mask_ref.shape[0]
    flat = jnp.dot(waves_ref[...], table_ref[...], preferred_element_type=jnp.float32)
    flat = flat.reshape(events, 3, 8, 4 * LANES) * mask_ref[...][:, None, :, :1]
    part = [flat[..., i * LANES : (i + 1) * LANES].reshape(events * 3, 8, LANES) for i in range(4)]
    turned = [pltpu.roll(value, 4, 1) for value in part]
    low = lax.broadcasted_iota(jnp.int32, part[0].shape, 1) < 4
    halves = (
        (jnp.where(low, part[0], turned[1]), jnp.where(low, part[2], turned[3])),
        (jnp.where(low, turned[0], part[1]), jnp.where(low, turned[2], part[3])),
    )
    for (real, imag), out_ref, power_ref in zip(halves, outs[:2], outs[2:]):
        packed = jnp.concatenate([real, imag], 1).astype(jnp.bfloat16)
        out_ref[: events * ROWS, :] = packed.reshape(events * ROWS, LANES)
        out_ref[events * ROWS :, :] = asked_ref[...]
        values = packed.astype(jnp.float32).reshape(events, 3, 2, 8, LANES)
        total = jnp.sum(values * values, axis=(1, 2))
        total = jnp.broadcast_to(jnp.sum(total, axis=-1, keepdims=True), (events, 8, LANES))
        power_ref[...] = (total + pltpu.roll(total, 4, 1)) * (2.0 / SCALE_WIDTH)


def own_spectra(waves, mask, table, asked):
    events = waves.shape[0]
    flat = waves.reshape(-1, waves.shape[-1])
    block = EVENT_BLOCK
    half = jax.ShapeDtypeStruct((events // block * BLOCK_ROWS, LANES), jnp.bfloat16)
    power = jax.ShapeDtypeStruct((events, 8, LANES), jnp.float32)
    spec = pl.BlockSpec((block, 8, LANES), lambda i: (i, 0, 0))
    return pl.pallas_call(
        spectra_kernel,
        grid=(events // block,),
        in_specs=[
            pl.BlockSpec((block * 24, flat.shape[-1]), lambda i: (i, 0)),
            spec,
            pl.BlockSpec(table.shape, lambda i: (0, 0)),
            pl.BlockSpec(asked.shape, lambda i: (0, 0)),
        ],
        out_specs=[pl.BlockSpec((BLOCK_ROWS, LANES), lambda i: (i, 0))] * 2 + [spec] * 2,
        out_shape=[half, half, power, power],
        compiler_params=PARAMS,
        name="spectra",
    )(flat, mask, table, asked)


def event_rows(event):
    start = event * ROWS + event // EVENT_BLOCK * (BLOCK_ROWS - EVENT_BLOCK * ROWS)
    return pl.ds(pl.multiple_of(start, 16), ROWS)


def tile_of(y, x, core):
    return (lax.rem(y + SIDE, SIDE) * SIDE + lax.rem(x + SIDE, SIDE)) * 2 + core


def pack_kernel(plan, asks, place_ref, *refs):
    asked = dict(zip(asks, refs))
    refs = refs[len(asks) :]
    pieces, outs = refs[:10], refs[10 : 10 + len(plan)]
    held_ref, sems = refs[10 + len(plan) :]
    y, x, core = place_ref[0], place_ref[1], place_ref[2]
    whole = held_ref.shape[2]
    copies = []
    for half in range(2):
        own, after, before, low, high = pieces[5 * half : 5 * half + 5]
        for number, (piece, step, start, size) in enumerate(
            (
                (own, 0, 0, whole),
                (after, 1, 0, whole),
                (before, 3, 0, whole),
                (low, 2, 0, whole // 2),
                (high, 2, whole // 2, whole // 2),
            )
        ):
            copy = pltpu.make_async_copy(
                piece, held_ref.at[half, step, pl.ds(start, size), :], sems.at[5 * half + number]
            )
            copy.start()
            copies.append(copy)
    for half in range(2):
        for copy in copies[5 * half : 5 * half + 5]:
            copy.wait()
        for out_ref, blocks in zip(outs, plan):
            for place, (which, hops, other) in enumerate(blocks):
                if which != half:
                    continue
                asked_ref = asked[half, hops]
                for step in range(SIDE):
                    tile = tile_of(y, x - step, core) if half == 0 else tile_of(y - step, x, core)
                    base = other * 256 + tile * SLOTS
                    for slot in range(SLOTS):
                        row = (place * SIDE + step) * SLOTS + slot
                        event = asked_ref[base + slot]
                        out_ref[row] = held_ref[half, step, event_rows(event), :]


def pack(plan, place, asked, pieces):
    shape = lambda blocks: (len(blocks) * SIDE * SLOTS, ROWS, LANES)
    whole = pieces[0].shape[0]
    return pl.pallas_call(
        functools.partial(pack_kernel, plan, tuple(asked)),
        in_specs=[SMEM] * (1 + len(asked)) + [ANY] * 10,
        out_specs=[VMEM] * len(plan),
        out_shape=[jax.ShapeDtypeStruct(shape(blocks), jnp.bfloat16) for blocks in plan],
        scratch_shapes=[
            pltpu.VMEM((2, SIDE, whole, LANES), jnp.bfloat16),
            pltpu.SemaphoreType.DMA((10,)),
        ],
        compiler_params=PARAMS,
        name="pack",
    )(place, *asked.values(), *pieces)


def join_kernel(*refs):
    *parts, _, out_ref, sems = refs
    size = parts[0].shape[0] // 2
    copies = [
        pltpu.make_async_copy(
            part.at[pl.ds(size, size)], out_ref.at[pl.ds(i * size, size)], sems.at[i]
        )
        for i, part in enumerate(parts)
    ]
    for copy in copies:
        copy.start()
    for copy in copies:
        copy.wait()


def join(parts, after):
    count = len(parts)
    shape = (parts[0].shape[0] // 2 * count,) + parts[0].shape[1:]
    return pl.pallas_call(
        join_kernel,
        in_specs=[ANY] * (count + 1),
        out_specs=ANY,
        out_shape=jax.ShapeDtypeStruct(shape, parts[0].dtype),
        scratch_shapes=[pltpu.SemaphoreType.DMA((count,))],
        compiler_params=PARAMS,
        name="join",
    )(*parts, after)


def pair_kernel(blocks, arrays, first, last, place_ref, local_ref, count_ref, table_ref, *refs):
    own, power = refs[:2], refs[2:4]
    partner = refs[4 : 4 + arrays]
    refs = refs[4 + arrays :]
    if not first:
        before_ref, refs = refs[0], refs[1:]
    out_ref, refs = refs[0], refs[1:]
    if last:
        chunks, refs = refs[:last], refs[last:]
    cross_ref, energy_ref, factor_ref, turned_ref = refs
    y, x, core = place_ref[0], place_ref[1], place_ref[2]
    if not first:
        out_ref[...] = before_ref[...]
    for half, shift, other, array, offset in blocks:
        partner_ref = partner[array]
        from_core = lax.rem(core + other, 2)

        def tile_at(step):
            if half == 0:
                return tile_of(y - shift, x - step, from_core)
            return tile_of(y - step, x - shift, from_core)

        def one_tile(step, carry):
            tile = tile_at(step)
            live = count_ref[tile]
            for slot in range(SLOTS):
                event = local_ref[tile * SLOTS + slot]
                mine = own[half][event_rows(event), :].astype(jnp.float32)
                mine = mine.reshape(3, 2, 8, LANES)
                row = step * SLOTS + slot
                theirs = partner_ref[offset + row].astype(jnp.float32).reshape(3, 2, 8, LANES)
                real = jnp.sum(mine * theirs, axis=(0, 1))
                imag = jnp.sum(mine[:, 1] * theirs[:, 0] - mine[:, 0] * theirs[:, 1], axis=0)
                cross = jnp.concatenate([real, imag], -1)
                cross_ref[pl.ds(pl.multiple_of(row * 8, 8), 8), :] = cross
                energy_ref[row] = jnp.sum(theirs * theirs, axis=(0, 1))
                alive = jnp.where(slot < live, jnp.float32(2.0 / SCALE_WIDTH), jnp.float32(0))
                factor_ref[0, row] = power[half][event]
                factor_ref[1, row] = jnp.full((8, LANES), alive, jnp.float32)
            return carry

        lax.fori_loop(0, SIDE, one_tile, 0)
        rows = SIDE * SLOTS
        corr = jnp.dot(
            cross_ref[...].astype(jnp.bfloat16), table_ref[...], preferred_element_type=jnp.float32
        ).reshape(rows, 8, 2 * LANES)
        low = lax.broadcasted_iota(jnp.int32, (rows, 8, LANES), 1) < 4
        corr = jnp.where(low, corr[..., :LANES], corr[..., LANES:])
        corr = corr + pltpu.roll(corr, 4, 1)
        energy = jnp.broadcast_to(
            jnp.sum(energy_ref[...], axis=-1, keepdims=True), (rows, 8, LANES)
        )
        energy = (energy + pltpu.roll(energy, 4, 1)) * (2.0 / SCALE_WIDTH)
        corr = corr * (lax.rsqrt(factor_ref[0] * energy + 1e-06) * factor_ref[1])
        for step in range(SIDE):
            at = pl.ds(pl.multiple_of(tile_at(jnp.int32(step)) * SLOTS, SLOTS), SLOTS)
            out_ref[at, 4 * half : 4 * half + 4, :] = corr[
                step * SLOTS : (step + 1) * SLOTS, 4 * half : 4 * half + 4
            ]
    if last:
        group = place_ref[3]
        turned_ref[...] = jnp.sum(out_ref[...], axis=1).T
        size = turned_ref.shape[0] // len(chunks)
        for step, chunk_ref in enumerate(chunks):
            at = lax.rem(group + step, len(chunks)) * size
            chunk_ref[...] = turned_ref[pl.ds(pl.multiple_of(at, size), size), :]


def pairs(blocks, place, local, count, table, own, power, partner, total, last):
    rows, slots = SIDE * SLOTS, local.shape[0]
    first = total is None
    out_shape = [jax.ShapeDtypeStruct((slots, 8, LAGS), jnp.float32)]
    if last:
        out_shape += [jax.ShapeDtypeStruct((LAGS // last, slots), jnp.float32)] * last
    args = [place, local, count, table, *own, *power, *partner] + ([] if first else [total])
    return pl.pallas_call(
        functools.partial(pair_kernel, blocks, len(partner), first, last),
        in_specs=[SMEM] * 3 + [VMEM] * (len(args) - 3),
        out_specs=[VMEM] * len(out_shape),
        out_shape=out_shape,
        scratch_shapes=[
            pltpu.VMEM((rows * 8, 2 * LANES), jnp.float32),
            pltpu.VMEM((rows, 8, LANES), jnp.float32),
            pltpu.VMEM((2, rows, 8, LANES), jnp.float32),
            pltpu.VMEM((LAGS, slots), jnp.float32),
        ],
        compiler_params=PARAMS,
        name="pairs",
    )(*args)


def hop(value, dy, dx, dcore):
    moves = []
    for y in range(SIDE):
        for x in range(SIDE):
            for core in range(2):
                target = ((y + dy) % SIDE * SIDE + (x + dx) % SIDE) * 2 + (core + dcore) % 2
                moves.append(((y * SIDE + x) * 2 + core, target))
    return lax.ppermute(value, "tile", moves)


def on_device(waves, station_mask, pair_local, pair_remote, pair_count):
    width = waves.shape[-1]
    events, stations = station_mask.shape
    groups = lax.axis_size("sta")
    here = lax.axis_index("tile")
    place = jnp.stack([here // (2 * SIDE), here // 2 % SIDE, here % 2, lax.axis_index("sta")])
    place = place.astype(jnp.int32)
    local, count = pair_local.reshape(-1), pair_count.reshape(-1)

    wanted = pair_remote.reshape(-1)
    wanted = jnp.concatenate([wanted, hop(wanted, 0, 0, 1)])
    rows = wanted.shape[0] // LANES
    carried = jnp.pad(wanted.astype(jnp.bfloat16).reshape(rows, LANES), ((0, 16 - rows), (0, 0)))
    mask = jnp.broadcast_to(station_mask.astype(jnp.float32)[..., None], (events, stations, LANES))
    own = own_spectra(waves, mask, jnp.asarray(forward_table(width)), carried)
    own, power = own[:2], own[2:]
    middle = own[0].shape[0] // 2

    along = lambda half, value, hops: hop(value, *((0, hops) if half == 0 else (hops, 0)), 0)
    across = lambda half, value, hops, other: hop(value, *((hops, 0) if half == 0 else (0, hops)), other)
    after = [along(half, own[half], 1) for half in range(2)]
    before = [along(half, own[half], SIDE - 1) for half in range(2)]
    low = [along(half, after[half][:middle], 1) for half in range(2)]
    high = [along(half, before[half][middle:], SIDE - 1) for half in range(2)]
    pieces = []
    asked = {(0, 0): wanted, (1, 0): wanted}
    for half in range(2):
        pieces += [own[half], after[half], before[half], low[half], high[half]]
        first_row = EVENT_BLOCK * ROWS
        for hops, value in ((1, before[half]), (3, after[half]), (2, low[half])):
            took = value[first_row : first_row + rows].astype(jnp.int32).reshape(-1)
            asked[1 - half, hops] = took

    def packed(plan):
        needed = {key: asked[key] for key in sorted({block[:2] for blocks in plan for block in blocks})}
        return pack(plan, place, needed, pieces)

    next_plan = tuple(
        ((half, hops, 0), (half, hops, 1)) for half in range(2) for hops in (1, 3)
    )
    got = [
        across(blocks[0][0], value, blocks[0][1], 0)
        for blocks, value in zip(next_plan, packed(next_plan))
    ]
    rest = packed(
        tuple(((half, 2, other),) for half in range(2) for other in range(2))
        + (((0, 0, 0), (1, 0, 0)), ((0, 0, 1), (1, 0, 1)))
    )
    near = [rest[4], hop(rest[5], 0, 0, 1)]
    far = [across(number // 2, rest[number], 2, number % 2) for number in range(4)]
    size = SIDE * SLOTS
    swapped = hop(join(got, rest[0]), 0, 0, 1)

    table = jnp.asarray(lag_table(width))
    calc = functools.partial(pairs, place=place, local=local, count=count, table=table, own=own, power=power)
    blocks = tuple((half, 0, other, other, half * size) for half in range(2) for other in range(2))
    total = calc(blocks, partner=near, total=None, last=0)[0]
    blocks = tuple(
        (block[0], block[1], other, 4 if other else number, number * size if other else 0)
        for number, (block, _) in enumerate(next_plan)
        for other in range(2)
    )
    total = calc(blocks, partner=got + [swapped], total=total, last=0)[0]
    blocks = tuple((half, 2, other, half * 2 + other, 0) for half in range(2) for other in range(2))
    total, *chunks = calc(blocks, partner=far, total=total, last=groups)

    stack = chunks[0]
    for step in range(1, groups):
        moves = [(i, (i + step) % groups) for i in range(groups)]
        stack = stack + lax.ppermute(chunks[step], "sta", moves)
    tiles = pair_remote.shape[1]
    station_coef = total.astype(jnp.bfloat16).reshape(1, tiles, SLOTS, stations, LAGS)
    return (station_coef, stack.T.reshape(1, tiles, SLOTS, LAGS // groups))


def solution(mesh):
    placed = (
        P("tile", None, "sta", None),
        P("tile", "sta"),
        P("tile", None, None),
        P("tile", None, None),
        P("tile", None),
    )
    return jax.shard_map(
        on_device,
        mesh=mesh,
        in_specs=placed,
        out_specs=(P("tile", None, None, "sta", None), P("tile", None, None, "sta")),
        check_vma=False,
    )
```

```python
import functools
import math

import jax
import jax.numpy as jnp
import ml_dtypes
import numpy as np
from jax import lax
from jax.experimental import pallas as pl
from jax.experimental.pallas import tpu as pltpu
from jax.sharding import PartitionSpec as P

BAND = 256
LAGS = 128
SLOTS = 8
SIDE = 4
LANES = 128
ROWS = 48
EVENT_BLOCK = 16
BLOCK_ROWS = EVENT_BLOCK * ROWS + 32
SCALE_WIDTH = 1024.0
VMEM = pl.BlockSpec(memory_space=pltpu.VMEM)
SMEM = pl.BlockSpec(memory_space=pltpu.SMEM)
PARAMS = pltpu.CompilerParams(vmem_limit_bytes=20 * 1024 * 1024)


def forward_table(width):
    phase = np.arange(width)[:, None] * np.arange(1, BAND + 1)[None, :] % width * (2.0 * math.pi / width)
    return np.concatenate([np.cos(phase), -np.sin(phase)], 1).astype(ml_dtypes.bfloat16)


def lag_table(width):
    phase = np.arange(1, BAND + 1)[:, None] * (np.arange(LAGS)[None, :] - LAGS // 2) % width
    phase = phase * (2.0 * math.pi / width)
    table = np.concatenate([np.cos(phase), -np.sin(phase)], 0).astype(ml_dtypes.bfloat16)
    low_re, high_re, low_im, high_im = (table[i * LANES : (i + 1) * LANES] for i in range(4))
    return np.concatenate(
        [np.concatenate([low_re, high_re], 1), np.concatenate([low_im, high_im], 1)], 0
    )


def spectra_kernel(waves_ref, mask_ref, table_ref, mine_ref, other_ref, *outs):
    events = mask_ref.shape[0]
    same = lax.broadcasted_iota(jnp.int32, (1, 8, 8), 1) == lax.broadcasted_iota(jnp.int32, (1, 8, 8), 2)
    mask = jnp.where(same, mask_ref[...].astype(jnp.float32)[:, None, :], 0.0)
    mask = jnp.sum(mask, axis=-1, keepdims=True)[:, None]
    asked = jnp.concatenate([mine_ref[0], other_ref[0]], 1).astype(jnp.float32).astype(jnp.bfloat16)
    flat = jnp.dot(waves_ref[...], table_ref[...], preferred_element_type=jnp.float32)
    flat = flat.reshape(events, 3, 8, 4 * LANES) * mask
    part = [flat[..., i * LANES : (i + 1) * LANES].reshape(events * 3, 8, LANES) for i in range(4)]
    turned = [pltpu.roll(value, 4, 1) for value in part]
    low = lax.broadcasted_iota(jnp.int32, part[0].shape, 1) < 4
    halves = (
        (jnp.where(low, part[0], turned[1]), jnp.where(low, part[2], turned[3])),
        (jnp.where(low, turned[0], part[1]), jnp.where(low, turned[2], part[3])),
    )
    for (real, imag), out_ref, power_ref in zip(halves, outs[:2], outs[2:]):
        packed = jnp.concatenate([real, imag], 1).astype(jnp.bfloat16)
        out_ref[: events * ROWS, :] = packed.reshape(events * ROWS, LANES)
        out_ref[events * ROWS :, : 2 * SLOTS] = asked
        values = packed.astype(jnp.float32).reshape(events, 3, 2, 8, LANES)
        total = jnp.sum(values * values, axis=(1, 2))
        total = jnp.broadcast_to(jnp.sum(total, axis=-1, keepdims=True), (events, 8, LANES))
        power_ref[...] = (total + pltpu.roll(total, 4, 1)) * (2.0 / SCALE_WIDTH)


def own_spectra(waves, mask, table, mine, other):
    events = waves.shape[0]
    flat = waves.reshape(-1, waves.shape[-1])
    block = EVENT_BLOCK
    half = jax.ShapeDtypeStruct((events // block * BLOCK_ROWS, LANES), jnp.bfloat16)
    power = jax.ShapeDtypeStruct((events, 8, LANES), jnp.float32)
    spec = pl.BlockSpec((block, 8, LANES), lambda i: (i, 0, 0))
    return pl.pallas_call(
        spectra_kernel,
        grid=(events // block,),
        in_specs=[
            pl.BlockSpec((block * 24, flat.shape[-1]), lambda i: (i, 0)),
            pl.BlockSpec((block, mask.shape[1]), lambda i: (i, 0)),
            pl.BlockSpec(table.shape, lambda i: (0, 0)),
            pl.BlockSpec(mine.shape, lambda i: (0, 0, 0)),
            pl.BlockSpec(mine.shape, lambda i: (0, 0, 0)),
        ],
        out_specs=[pl.BlockSpec((BLOCK_ROWS, LANES), lambda i: (i, 0))] * 2 + [spec] * 2,
        out_shape=[half, half, power, power],
        compiler_params=PARAMS,
        name="spectra",
    )(flat, mask, table, mine, other)


def event_rows(event):
    start = event * ROWS + event // EVENT_BLOCK * (BLOCK_ROWS - EVENT_BLOCK * ROWS)
    return pl.ds(pl.multiple_of(start, 16), ROWS)


def tile_of(y, x, core):
    return (lax.rem(y + SIDE, SIDE) * SIDE + lax.rem(x + SIDE, SIDE)) * 2 + core


def pack_kernel(plan, asks, place_ref, *refs):
    asked = dict(zip(asks, refs))
    refs = refs[len(asks) :]
    pieces, outs = refs[:10], refs[10:]
    y, x, core = place_ref[0], place_ref[1], place_ref[2]
    for half in range(2):
        own, after, before, low, high = pieces[5 * half : 5 * half + 5]
        middle = EVENT_BLOCK * (low.shape[0] // BLOCK_ROWS)

        def rows_of(step, event):
            if step != 2:
                return (own, after, None, before)[step][event_rows(event), :]
            early = low[event_rows(jnp.minimum(event, middle - 1)), :]
            late = high[event_rows(jnp.maximum(event - middle, 0)), :]
            return jnp.where(event < middle, early, late)

        for out_ref, blocks in zip(outs, plan):
            for place, (which, hops, other) in enumerate(blocks):
                if which != half:
                    continue
                asked_ref = asked[half, hops]
                for step in range(SIDE):
                    tile = tile_of(y, x - step, core) if half == 0 else tile_of(y - step, x, core)
                    base = (tile * 2 + other) * SLOTS
                    for slot in range(SLOTS):
                        row = (place * SIDE + step) * SLOTS + slot
                        out_ref[row] = rows_of(step, asked_ref[base + slot])


def pack(plan, place, asked, pieces):
    shape = lambda blocks: (len(blocks) * SIDE * SLOTS, ROWS, LANES)
    return pl.pallas_call(
        functools.partial(pack_kernel, plan, tuple(asked)),
        in_specs=[SMEM] * (1 + len(asked)) + [VMEM] * 10,
        out_specs=[VMEM] * len(plan),
        out_shape=[jax.ShapeDtypeStruct(shape(blocks), jnp.bfloat16) for blocks in plan],
        compiler_params=PARAMS,
        name="pack",
    )(place, *asked.values(), *pieces)


def join_kernel(*refs):
    *parts, _, out_ref = refs
    size = parts[0].shape[0] // 2
    for i, part in enumerate(parts):
        out_ref[i * size : (i + 1) * size] = part[size:]


def join(parts, after):
    count = len(parts)
    shape = (parts[0].shape[0] // 2 * count,) + parts[0].shape[1:]
    return pl.pallas_call(
        join_kernel,
        in_specs=[VMEM] * count + [pl.BlockSpec(memory_space=pl.ANY)],
        out_specs=VMEM,
        out_shape=jax.ShapeDtypeStruct(shape, parts[0].dtype),
        compiler_params=PARAMS,
        name="join",
    )(*parts, after)


def pair_kernel(blocks, arrays, first, last, place_ref, local_ref, count_ref, table_ref, *refs):
    own, power = refs[:2], refs[2:4]
    partner = refs[4 : 4 + arrays]
    refs = refs[4 + arrays :]
    if not first:
        before_ref, refs = refs[0], refs[1:]
    out_ref, refs = refs[0], refs[1:]
    if last:
        turned_ref, refs = refs[0], refs[1:]
    cross_ref, energy_ref, factor_ref = refs
    y, x, core = place_ref[0], place_ref[1], place_ref[2]
    if not first:
        out_ref[...] = before_ref[...]
    for half, shift, other, array, offset in blocks:
        partner_ref = partner[array]
        from_core = lax.rem(core + other, 2)

        def tile_at(step):
            if half == 0:
                return tile_of(y - shift, x - step, from_core)
            return tile_of(y - step, x - shift, from_core)

        def one_tile(step, carry):
            tile = tile_at(step)
            live = count_ref[tile]
            for slot in range(SLOTS):
                event = local_ref[tile * SLOTS + slot]
                mine = own[half][event_rows(event), :].astype(jnp.float32)
                mine = mine.reshape(3, 2, 8, LANES)
                row = step * SLOTS + slot
                theirs = partner_ref[offset + row].astype(jnp.float32).reshape(3, 2, 8, LANES)
                real = jnp.sum(mine * theirs, axis=(0, 1))
                imag = jnp.sum(mine[:, 1] * theirs[:, 0] - mine[:, 0] * theirs[:, 1], axis=0)
                cross = jnp.concatenate([real, imag], -1)
                cross_ref[pl.ds(pl.multiple_of(row * 8, 8), 8), :] = cross
                energy_ref[row] = jnp.sum(theirs * theirs, axis=(0, 1))
                alive = jnp.where(slot < live, jnp.float32(2.0 / SCALE_WIDTH), jnp.float32(0))
                factor_ref[0, row] = power[half][event]
                factor_ref[1, row] = jnp.full((8, LANES), alive, jnp.float32)
            return carry

        lax.fori_loop(0, SIDE, one_tile, 0)
        rows = SIDE * SLOTS
        corr = jnp.dot(
            cross_ref[...].astype(jnp.bfloat16), table_ref[...], preferred_element_type=jnp.float32
        ).reshape(rows, 8, 2 * LANES)
        low = lax.broadcasted_iota(jnp.int32, (rows, 8, LANES), 1) < 4
        corr = jnp.where(low, corr[..., :LANES], corr[..., LANES:])
        corr = corr + pltpu.roll(corr, 4, 1)
        energy = jnp.broadcast_to(
            jnp.sum(energy_ref[...], axis=-1, keepdims=True), (rows, 8, LANES)
        )
        energy = (energy + pltpu.roll(energy, 4, 1)) * (2.0 / SCALE_WIDTH)
        corr = corr * (lax.rsqrt(factor_ref[0] * energy + 1e-06) * factor_ref[1])
        for step in range(SIDE):
            at = pl.ds(pl.multiple_of(tile_at(jnp.int32(step)) * SLOTS, SLOTS), SLOTS)
            out_ref[at, 4 * half : 4 * half + 4, :] = corr[
                step * SLOTS : (step + 1) * SLOTS, 4 * half : 4 * half + 4
            ]
    if last:
        turned_ref[...] = jnp.sum(out_ref[...], axis=1).T


def pairs(blocks, place, local, count, table, own, power, partner, total, last):
    rows, slots = SIDE * SLOTS, local.shape[0]
    first = total is None
    out_shape = [jax.ShapeDtypeStruct((slots, 8, LAGS), jnp.float32)]
    if last:
        out_shape += [jax.ShapeDtypeStruct((LAGS, slots), jnp.float32)]
    args = [place, local, count, table, *own, *power, *partner] + ([] if first else [total])
    return pl.pallas_call(
        functools.partial(pair_kernel, blocks, len(partner), first, last),
        in_specs=[SMEM] * 3 + [VMEM] * (len(args) - 3),
        out_specs=[VMEM] * len(out_shape),
        out_shape=out_shape,
        scratch_shapes=[
            pltpu.VMEM((rows * 8, 2 * LANES), jnp.float32),
            pltpu.VMEM((rows, 8, LANES), jnp.float32),
            pltpu.VMEM((2, rows, 8, LANES), jnp.float32),
        ],
        compiler_params=PARAMS,
        name="pairs",
    )(*args)


def hop(value, dy, dx, dcore):
    moves = []
    for y in range(SIDE):
        for x in range(SIDE):
            for core in range(2):
                target = ((y + dy) % SIDE * SIDE + (x + dx) % SIDE) * 2 + (core + dcore) % 2
                moves.append(((y * SIDE + x) * 2 + core, target))
    return lax.ppermute(value, "tile", moves)


def on_device(waves, station_mask, pair_local, pair_remote, pair_count):
    width, tiles = waves.shape[-1], pair_remote.shape[1]
    events, stations = station_mask.shape
    groups = lax.axis_size("sta")
    here = lax.axis_index("tile")
    place = jnp.stack([here // (2 * SIDE), here // 2 % SIDE, here % 2]).astype(jnp.int32)
    local, count = pair_local.reshape(-1), pair_count.reshape(-1)

    other = hop(pair_remote, 0, 0, 1)
    wanted = jnp.concatenate([pair_remote, other], -1).reshape(-1)
    own = own_spectra(waves, station_mask, jnp.asarray(forward_table(width)), pair_remote, other)
    own, power = own[:2], own[2:]
    middle = own[0].shape[0] // 2

    along = lambda half, value, hops: hop(value, *((0, hops) if half == 0 else (hops, 0)), 0)
    across = lambda half, value, hops, other: hop(value, *((hops, 0) if half == 0 else (0, hops)), other)
    after = [along(half, own[half], 1) for half in range(2)]
    before = [along(half, own[half], SIDE - 1) for half in range(2)]
    low = [along(half, after[half][:middle], 1) for half in range(2)]
    high = [along(half, before[half][middle:], SIDE - 1) for half in range(2)]
    pieces = []
    asked = {(0, 0): wanted, (1, 0): wanted}
    for half in range(2):
        pieces += [own[half], after[half], before[half], low[half], high[half]]
        first_row = EVENT_BLOCK * ROWS
        for hops, value in ((1, before[half]), (3, after[half]), (2, low[half])):
            took = value[first_row : first_row + tiles, : 2 * SLOTS].astype(jnp.int32).reshape(-1)
            asked[1 - half, hops] = took

    def packed(plan):
        needed = {key: asked[key] for key in sorted({block[:2] for blocks in plan for block in blocks})}
        return pack(plan, place, needed, pieces)

    next_plan = tuple(
        ((half, hops, 0), (half, hops, 1)) for half in range(2) for hops in (1, 3)
    )
    got = [
        across(blocks[0][0], value, blocks[0][1], 0)
        for blocks, value in zip(next_plan, packed(next_plan))
    ]
    rest = packed(
        tuple(((half, 2, other),) for half in range(2) for other in range(2))
        + (((0, 0, 0), (1, 0, 0)), ((0, 0, 1), (1, 0, 1)))
    )
    near = [rest[4], hop(rest[5], 0, 0, 1)]
    far = [across(number // 2, rest[number], 2, number % 2) for number in range(4)]
    size = SIDE * SLOTS
    swapped = hop(join(got, rest[0]), 0, 0, 1)

    table = jnp.asarray(lag_table(width))
    calc = functools.partial(pairs, place=place, local=local, count=count, table=table, own=own, power=power)
    blocks = tuple((half, 0, other, other, half * size) for half in range(2) for other in range(2))
    total = calc(blocks, partner=near, total=None, last=False)[0]
    blocks = tuple(
        (block[0], block[1], other, 4 if other else number, number * size if other else 0)
        for number, (block, _) in enumerate(next_plan)
        for other in range(2)
    )
    total = calc(blocks, partner=got + [swapped], total=total, last=False)[0]
    blocks = tuple((half, 2, other, half * 2 + other, 0) for half in range(2) for other in range(2))
    total, stack = calc(blocks, partner=far, total=total, last=True)

    stack = lax.all_to_all(stack, "sta", split_axis=0, concat_axis=0, tiled=True)
    stack = jnp.sum(stack.reshape(groups, LAGS // groups, -1), axis=0).T
    station_coef = total.astype(jnp.bfloat16).reshape(1, tiles, SLOTS, stations, LAGS)
    return (station_coef, stack.reshape(1, tiles, SLOTS, LAGS // groups))


def solution(mesh):
    placed = (
        P("tile", None, "sta", None),
        P("tile", "sta"),
        P("tile", None, None),
        P("tile", None, None),
        P("tile", None),
    )
    return jax.shard_map(
        on_device,
        mesh=mesh,
        in_specs=placed,
        out_specs=(P("tile", None, None, "sta", None), P("tile", None, None, "sta")),
        check_vma=False,
    )
```

```python
import functools
import math

import jax
import jax.numpy as jnp
import ml_dtypes
import numpy as np
from jax import lax
from jax.experimental import pallas as pl
from jax.experimental.pallas import tpu as pltpu
from jax.sharding import PartitionSpec as P

BAND = 256
LAGS = 128
SLOTS = 8
SIDE = 4
LANES = 128
ROWS = 48
EVENT_BLOCK = 16
BLOCK_ROWS = EVENT_BLOCK * ROWS + 32
SCALE_WIDTH = 1024.0
VMEM = pl.BlockSpec(memory_space=pltpu.VMEM)
SMEM = pl.BlockSpec(memory_space=pltpu.SMEM)
PARAMS = pltpu.CompilerParams(vmem_limit_bytes=20 * 1024 * 1024)


def forward_table(width):
    phase = np.arange(width)[:, None] * np.arange(1, BAND + 1)[None, :] % width * (2.0 * math.pi / width)
    return np.concatenate([np.cos(phase), -np.sin(phase)], 1).astype(ml_dtypes.bfloat16)


def lag_table(width):
    phase = np.arange(1, BAND + 1)[:, None] * (np.arange(LAGS)[None, :] - LAGS // 2) % width
    phase = phase * (2.0 * math.pi / width)
    table = np.concatenate([np.cos(phase), -np.sin(phase)], 0).astype(ml_dtypes.bfloat16)
    low_re, high_re, low_im, high_im = (table[i * LANES : (i + 1) * LANES] for i in range(4))
    return np.concatenate(
        [np.concatenate([low_re, high_re], 1), np.concatenate([low_im, high_im], 1)], 0
    )


def spectra_kernel(waves_ref, mask_ref, table_ref, mine_ref, other_ref, *outs):
    events = mask_ref.shape[0]
    same = lax.broadcasted_iota(jnp.int32, (1, 8, 8), 1) == lax.broadcasted_iota(jnp.int32, (1, 8, 8), 2)
    mask = jnp.where(same, mask_ref[...].astype(jnp.float32)[:, None, :], 0.0)
    mask = jnp.sum(mask, axis=-1, keepdims=True)[:, None]
    mine, other = mine_ref[0], other_ref[0]
    blank = jnp.zeros((mine.shape[0], LANES - 2 * SLOTS), mine.dtype)
    asked = jnp.concatenate([mine, other, blank], 1).astype(jnp.float32).astype(jnp.bfloat16)
    flat = jnp.dot(waves_ref[...], table_ref[...], preferred_element_type=jnp.float32)
    flat = flat.reshape(events, 3, 8, 4 * LANES) * mask
    part = [flat[..., i * LANES : (i + 1) * LANES].reshape(events * 3, 8, LANES) for i in range(4)]
    turned = [pltpu.roll(value, 4, 1) for value in part]
    low = lax.broadcasted_iota(jnp.int32, part[0].shape, 1) < 4
    halves = (
        (jnp.where(low, part[0], turned[1]), jnp.where(low, part[2], turned[3])),
        (jnp.where(low, turned[0], part[1]), jnp.where(low, turned[2], part[3])),
    )
    for (real, imag), out_ref, power_ref in zip(halves, outs[:2], outs[2:]):
        packed = jnp.concatenate([real, imag], 1).astype(jnp.bfloat16)
        out_ref[: events * ROWS, :] = packed.reshape(events * ROWS, LANES)
        out_ref[events * ROWS :, :] = asked
        values = packed.astype(jnp.float32).reshape(events, 3, 2, 8, LANES)
        total = jnp.sum(values * values, axis=(1, 2))
        total = jnp.broadcast_to(jnp.sum(total, axis=-1, keepdims=True), (events, 8, LANES))
        power_ref[...] = (total + pltpu.roll(total, 4, 1)) * (2.0 / SCALE_WIDTH)


def own_spectra(waves, mask, table, mine, other):
    events = waves.shape[0]
    flat = waves.reshape(-1, waves.shape[-1])
    block = EVENT_BLOCK
    half = jax.ShapeDtypeStruct((events // block * BLOCK_ROWS, LANES), jnp.bfloat16)
    power = jax.ShapeDtypeStruct((events, 8, LANES), jnp.float32)
    spec = pl.BlockSpec((block, 8, LANES), lambda i: (i, 0, 0))
    return pl.pallas_call(
        spectra_kernel,
        grid=(events // block,),
        in_specs=[
            pl.BlockSpec((block * 24, flat.shape[-1]), lambda i: (i, 0)),
            pl.BlockSpec((block, mask.shape[1]), lambda i: (i, 0)),
            pl.BlockSpec(table.shape, lambda i: (0, 0)),
            pl.BlockSpec(mine.shape, lambda i: (0, 0, 0)),
            pl.BlockSpec(mine.shape, lambda i: (0, 0, 0)),
        ],
        out_specs=[pl.BlockSpec((BLOCK_ROWS, LANES), lambda i: (i, 0))] * 2 + [spec] * 2,
        out_shape=[half, half, power, power],
        compiler_params=PARAMS,
        name="spectra",
    )(flat, mask, table, mine, other)


def event_rows(event):
    start = event * ROWS + event // EVENT_BLOCK * (BLOCK_ROWS - EVENT_BLOCK * ROWS)
    return pl.ds(pl.multiple_of(start, 16), ROWS)


def tile_of(y, x, core):
    return (lax.rem(y + SIDE, SIDE) * SIDE + lax.rem(x + SIDE, SIDE)) * 2 + core


def pack_kernel(plan, asks, halves, place_ref, *refs):
    sources, refs = refs[: len(asks)], refs[len(asks) :]
    held, outs = refs[: SIDE * len(halves)], refs[SIDE * len(halves) : -3]
    words_ref, asked_ref, sems = refs[-3:]
    y, x, core = place_ref[0], place_ref[1], place_ref[2]
    copies = []
    for i, source in enumerate(sources):
        words_ref[i] = source[...].astype(jnp.float32).astype(jnp.int32)
        copies.append(pltpu.make_async_copy(words_ref.at[i], asked_ref.at[i], sems.at[i]))
        copies[i].start()
    for copy in copies:
        copy.wait()
    for out_ref, blocks in zip(outs, plan):
        for place, (half, hops, other) in enumerate(blocks):
            which, first = asks.index((half, hops)), halves.index(half) * SIDE
            for step in range(SIDE):
                tile = tile_of(y, x - step, core) if half == 0 else tile_of(y - step, x, core)
                for slot in range(SLOTS):
                    row = (place * SIDE + step) * SLOTS + slot
                    event = asked_ref[which, tile, other * SLOTS + slot]
                    out_ref[row] = held[first + step][event_rows(event), :]


def pack(plan, place, held):
    asks = tuple(sorted({block[:2] for blocks in plan for block in blocks}))
    halves = tuple(sorted({half for half, _ in asks}))
    sources = [held[1 - half][-hops % SIDE] for half, hops in asks]
    pieces = [piece for half in halves for piece in held[half]]
    shape = lambda blocks: (len(blocks) * SIDE * SLOTS, ROWS, LANES)
    tiles = BLOCK_ROWS - EVENT_BLOCK * ROWS
    asked_rows = pl.BlockSpec((tiles, LANES), lambda i: (EVENT_BLOCK * ROWS // tiles, 0))
    whole = lambda size: pl.BlockSpec(size, lambda i: (0,) * len(size))
    return pl.pallas_call(
        functools.partial(pack_kernel, plan, asks, halves),
        grid=(1,),
        in_specs=[SMEM] + [asked_rows] * len(asks) + [whole(piece.shape) for piece in pieces],
        out_specs=[whole(shape(blocks)) for blocks in plan],
        out_shape=[jax.ShapeDtypeStruct(shape(blocks), jnp.bfloat16) for blocks in plan],
        scratch_shapes=[
            pltpu.VMEM((len(asks), tiles, LANES), jnp.int32),
            pltpu.SMEM((len(asks), tiles, LANES), jnp.int32),
            pltpu.SemaphoreType.DMA((len(asks),)),
        ],
        compiler_params=PARAMS,
        name="pack",
    )(place, *sources, *pieces)


def join_kernel(count, *refs):
    parts, out_ref = refs[:count], refs[-1]
    size = parts[0].shape[0] // 2
    for i, part in enumerate(parts):
        out_ref[i * size : (i + 1) * size] = part[size:]


def join(parts, after):
    count = len(parts)
    shape = (parts[0].shape[0] // 2 * count,) + parts[0].shape[1:]
    return pl.pallas_call(
        functools.partial(join_kernel, count),
        in_specs=[VMEM] * count + [pl.BlockSpec(memory_space=pl.ANY)] * len(after),
        out_specs=VMEM,
        out_shape=jax.ShapeDtypeStruct(shape, parts[0].dtype),
        compiler_params=PARAMS,
        name="join",
    )(*parts, *after)


def pair_kernel(blocks, arrays, first, last, place_ref, local_ref, count_ref, table_ref, *refs):
    own, power = refs[:2], refs[2:4]
    partner = refs[4 : 4 + arrays]
    refs = refs[4 + arrays :]
    if not first:
        before_ref, refs = refs[0], refs[1:]
    out_ref, refs = refs[0], refs[1:]
    if last:
        turned_ref, refs = refs[0], refs[1:]
    cross_ref, energy_ref, factor_ref = refs
    y, x, core = place_ref[0], place_ref[1], place_ref[2]
    if not first:
        out_ref[...] = before_ref[...]
    for half, shift, other, array, offset in blocks:
        partner_ref = partner[array]
        from_core = lax.rem(core + other, 2)

        def tile_at(step):
            if half == 0:
                return tile_of(y - shift, x - step, from_core)
            return tile_of(y - step, x - shift, from_core)

        def one_tile(step, carry):
            tile = tile_at(step)
            live = count_ref[tile]
            for slot in range(SLOTS):
                event = local_ref[tile * SLOTS + slot]
                mine = own[half][event_rows(event), :].astype(jnp.float32)
                mine = mine.reshape(3, 2, 8, LANES)
                row = step * SLOTS + slot
                theirs = partner_ref[offset + row].astype(jnp.float32).reshape(3, 2, 8, LANES)
                real = jnp.sum(mine * theirs, axis=(0, 1))
                imag = jnp.sum(mine[:, 1] * theirs[:, 0] - mine[:, 0] * theirs[:, 1], axis=0)
                cross = jnp.concatenate([real, imag], -1)
                cross_ref[pl.ds(pl.multiple_of(row * 8, 8), 8), :] = cross
                energy_ref[row] = jnp.sum(theirs * theirs, axis=(0, 1))
                alive = jnp.where(slot < live, jnp.float32(2.0 / SCALE_WIDTH), jnp.float32(0))
                factor_ref[0, row] = power[half][event]
                factor_ref[1, row] = jnp.full((8, LANES), alive, jnp.float32)
            return carry

        lax.fori_loop(0, SIDE, one_tile, 0)
        rows = SIDE * SLOTS
        corr = jnp.dot(
            cross_ref[...].astype(jnp.bfloat16), table_ref[...], preferred_element_type=jnp.float32
        ).reshape(rows, 8, 2 * LANES)
        low = lax.broadcasted_iota(jnp.int32, (rows, 8, LANES), 1) < 4
        corr = jnp.where(low, corr[..., :LANES], corr[..., LANES:])
        corr = corr + pltpu.roll(corr, 4, 1)
        energy = jnp.broadcast_to(
            jnp.sum(energy_ref[...], axis=-1, keepdims=True), (rows, 8, LANES)
        )
        energy = (energy + pltpu.roll(energy, 4, 1)) * (2.0 / SCALE_WIDTH)
        corr = corr * (lax.rsqrt(factor_ref[0] * energy + 1e-06) * factor_ref[1])
        for step in range(SIDE):
            at = pl.ds(pl.multiple_of(tile_at(jnp.int32(step)) * SLOTS, SLOTS), SLOTS)
            out_ref[at, 4 * half : 4 * half + 4, :] = corr[
                step * SLOTS : (step + 1) * SLOTS, 4 * half : 4 * half + 4
            ]
    if last:
        turned_ref[...] = jnp.sum(out_ref[...], axis=1).T


def pairs(blocks, place, local, count, table, own, power, partner, total, last):
    rows, slots = SIDE * SLOTS, local.shape[0]
    first = total is None
    out_shape = [jax.ShapeDtypeStruct((slots, 8, LAGS), jnp.float32)]
    if last:
        out_shape += [jax.ShapeDtypeStruct((LAGS, slots), jnp.float32)]
    needed = {}
    for *_, array, offset in blocks:
        needed[5 + array] = max(needed.get(5 + array, 0), offset + rows)

    def whole(value, length=None):
        size = (length or value.shape[0],) + value.shape[1:]
        return pl.BlockSpec(size, lambda i: (0,) * len(size))

    args = [place, local, count, table, *own, *power, *partner] + ([] if first else [total])
    return pl.pallas_call(
        functools.partial(pair_kernel, blocks, len(partner), first, last),
        grid=(1,),
        in_specs=[SMEM] * 3 + [whole(value, needed.get(i)) for i, value in enumerate(args[3:])],
        out_specs=[whole(value) for value in out_shape],
        out_shape=out_shape,
        scratch_shapes=[
            pltpu.VMEM((rows * 8, 2 * LANES), jnp.float32),
            pltpu.VMEM((rows, 8, LANES), jnp.float32),
            pltpu.VMEM((2, rows, 8, LANES), jnp.float32),
        ],
        compiler_params=PARAMS,
        name="pairs",
    )(*args)


def hop(value, dy, dx, dcore):
    moves = []
    for y in range(SIDE):
        for x in range(SIDE):
            for core in range(2):
                target = ((y + dy) % SIDE * SIDE + (x + dx) % SIDE) * 2 + (core + dcore) % 2
                moves.append(((y * SIDE + x) * 2 + core, target))
    return lax.ppermute(value, "tile", moves)


def on_device(waves, station_mask, pair_local, pair_remote, pair_count):
    width, tiles = waves.shape[-1], pair_remote.shape[1]
    events, stations = station_mask.shape
    groups = lax.axis_size("sta")
    here = lax.axis_index("tile")
    place = jnp.stack([here // (2 * SIDE), here // 2 % SIDE, here % 2]).astype(jnp.int32)
    local, count = pair_local.reshape(-1), pair_count.reshape(-1)

    other = hop(pair_remote, 0, 0, 1)
    own = own_spectra(waves, station_mask, jnp.asarray(forward_table(width)), pair_remote, other)
    own, power = own[:2], own[2:]

    along = lambda half, value, hops: hop(value, *((0, hops) if half == 0 else (hops, 0)), 0)
    across = lambda half, value, hops, other: hop(value, *((hops, 0) if half == 0 else (0, hops)), other)
    held = [[own[half], None, None, None] for half in range(2)]
    for hops in (1, 3, 2):
        for half in range(2):
            held[half][hops] = along(half, own[half], hops)

    got, beside = [], []
    for half in range(2):
        plan = tuple(((half, hops, 0), (half, hops, 1)) for hops in (1, 3))
        got += [
            across(half, value, hops, 0) for value, hops in zip(pack(plan, place, held), (1, 3))
        ]
        beside += [(half, 1), (half, 3)]
    far = pack(tuple(((half, 2, other),) for half in range(2) for other in range(2)), place, held)
    far = [across(number // 2, far[number], 2, number % 2) for number in range(4)]
    near = pack((((0, 0, 0), (1, 0, 0)), ((0, 0, 1), (1, 0, 1))), place, held)
    near = [near[0], hop(near[1], 0, 0, 1)]
    size = SIDE * SLOTS

    table = jnp.asarray(lag_table(width))
    calc = functools.partial(pairs, place=place, local=local, count=count, table=table, own=own, power=power)
    blocks = tuple((half, 0, other, other, half * size) for half in range(2) for other in range(2))
    total = calc(blocks, partner=near, total=None, last=False)[0]
    blocks = tuple((half, 2, other, half * 2 + other, 0) for half in range(2) for other in range(2))
    total = calc(blocks, partner=far, total=total, last=False)[0]
    swapped = hop(join(got, [total]), 0, 0, 1)
    blocks = tuple((*where, 0, number, 0) for number, where in enumerate(beside))
    total = calc(blocks, partner=got, total=total, last=False)[0]
    blocks = tuple((*where, 1, 0, number * size) for number, where in enumerate(beside))
    total, stack = calc(blocks, partner=[swapped], total=total, last=True)

    stack = lax.all_to_all(stack, "sta", split_axis=0, concat_axis=0, tiled=True)
    stack = jnp.sum(stack.reshape(groups, LAGS // groups, -1), axis=0).T
    station_coef = total.astype(jnp.bfloat16).reshape(1, tiles, SLOTS, stations, LAGS)
    return (station_coef, stack.reshape(1, tiles, SLOTS, LAGS // groups))


def solution(mesh):
    placed = (
        P("tile", None, "sta", None),
        P("tile", "sta"),
        P("tile", None, None),
        P("tile", None, None),
        P("tile", None),
    )
    return jax.shard_map(
        on_device,
        mesh=mesh,
        in_specs=placed,
        out_specs=(P("tile", None, None, "sta", None), P("tile", None, None, "sta")),
        check_vma=False,
    )
```

```python
import functools
import math

import jax
import jax.numpy as jnp
import ml_dtypes
import numpy as np
from jax import lax
from jax.experimental import pallas as pl
from jax.experimental.pallas import tpu as pltpu
from jax.sharding import PartitionSpec as P

BAND = 256
LAGS = 128
SLOTS = 8
SIDE = 4
LANES = 128
ROWS = 48
BLOCK_BITS = 4
EVENT_BLOCK = 1 << BLOCK_BITS
BLOCK_ROWS = EVENT_BLOCK * ROWS + 32
SCALE_WIDTH = 1024.0
VMEM = pl.BlockSpec(memory_space=pltpu.VMEM)
HBM = pl.BlockSpec(memory_space=pltpu.HBM)
SMEM = pl.BlockSpec(memory_space=pltpu.SMEM)
PARAMS = pltpu.CompilerParams(vmem_limit_bytes=24 * 1024 * 1024)


def forward_table(width):
    phase = np.arange(width)[:, None] * np.arange(1, BAND + 1)[None, :] % width * (2.0 * math.pi / width)
    return np.concatenate([np.cos(phase), -np.sin(phase)], 1).astype(ml_dtypes.bfloat16)


def lag_table(width):
    phase = np.arange(1, BAND + 1)[:, None] * (np.arange(LAGS)[None, :] - LAGS // 2) % width
    phase = phase * (2.0 * math.pi / width)
    table = np.concatenate([np.cos(phase), -np.sin(phase)], 0).astype(ml_dtypes.bfloat16)
    low_re, high_re, low_im, high_im = (table[i * LANES : (i + 1) * LANES] for i in range(4))
    return np.concatenate(
        [np.concatenate([low_re, high_re], 1), np.concatenate([low_im, high_im], 1)], 0
    )


def spectra_kernel(waves_ref, mask_ref, table_ref, mine_ref, other_ref, *outs):
    events = mask_ref.shape[0]
    same = lax.broadcasted_iota(jnp.int32, (1, 8, 8), 1) == lax.broadcasted_iota(jnp.int32, (1, 8, 8), 2)
    mask = jnp.where(same, mask_ref[...].astype(jnp.float32)[:, None, :], 0.0)
    mask = jnp.sum(mask, axis=-1, keepdims=True)[:, None]
    mine, other = mine_ref[0], other_ref[0]
    blank = jnp.zeros((mine.shape[0], LANES - 2 * SLOTS), mine.dtype)
    asked = jnp.concatenate([mine, other, blank], 1).astype(jnp.float32).astype(jnp.bfloat16)
    flat = jnp.dot(waves_ref[...], table_ref[...], preferred_element_type=jnp.float32)
    flat = flat.reshape(events, 3, 8, 4 * LANES) * mask
    part = [flat[..., i * LANES : (i + 1) * LANES].reshape(events * 3, 8, LANES) for i in range(4)]
    turned = [pltpu.roll(value, 4, 1) for value in part]
    low = lax.broadcasted_iota(jnp.int32, part[0].shape, 1) < 4
    halves = (
        (jnp.where(low, part[0], turned[1]), jnp.where(low, part[2], turned[3])),
        (jnp.where(low, turned[0], part[1]), jnp.where(low, turned[2], part[3])),
    )
    for (real, imag), out_ref, power_ref in zip(halves, outs[:2], outs[2:]):
        packed = jnp.concatenate([real, imag], 1).astype(jnp.bfloat16)
        out_ref[: events * ROWS, :] = packed.reshape(events * ROWS, LANES)
        out_ref[events * ROWS :, :] = asked
        values = packed.astype(jnp.float32).reshape(events, 3, 2, 8, LANES)
        total = jnp.sum(values * values, axis=(1, 2))
        total = jnp.broadcast_to(jnp.sum(total, axis=-1, keepdims=True), (events, 8, LANES))
        power_ref[...] = (total + pltpu.roll(total, 4, 1)) * (2.0 / SCALE_WIDTH)


def own_spectra(waves, mask, table, mine, other):
    events = waves.shape[0]
    flat = waves.reshape(-1, waves.shape[-1])
    block = EVENT_BLOCK
    half = jax.ShapeDtypeStruct((events // block * BLOCK_ROWS, LANES), jnp.bfloat16)
    power = jax.ShapeDtypeStruct((events, 8, LANES), jnp.float32)
    spec = pl.BlockSpec((block, 8, LANES), lambda i: (i, 0, 0))
    return pl.pallas_call(
        spectra_kernel,
        grid=(events // block,),
        in_specs=[
            pl.BlockSpec((block * 24, flat.shape[-1]), lambda i: (i, 0)),
            pl.BlockSpec((block, mask.shape[1]), lambda i: (i, 0)),
            pl.BlockSpec(table.shape, lambda i: (0, 0)),
            pl.BlockSpec(mine.shape, lambda i: (0, 0, 0)),
            pl.BlockSpec(mine.shape, lambda i: (0, 0, 0)),
        ],
        out_specs=[pl.BlockSpec((BLOCK_ROWS, LANES), lambda i: (i, 0))] * 2 + [spec] * 2,
        out_shape=[half, half, power, power],
        compiler_params=PARAMS,
        name="spectra",
    )(flat, mask, table, mine, other)


def event_rows(event):
    start = event * ROWS + (event >> BLOCK_BITS) * (BLOCK_ROWS - EVENT_BLOCK * ROWS)
    return pl.ds(pl.multiple_of(start, 16), ROWS)


def tile_of(y, x, core):
    return (lax.rem(y + SIDE, SIDE) * SIDE + lax.rem(x + SIDE, SIDE)) * 2 + core


def pack_kernel(plan, asks, halves, place_ref, *refs):
    sources, refs = refs[: len(asks)], refs[len(asks) :]
    held, outs = refs[: SIDE * len(halves)], refs[SIDE * len(halves) : -8]
    near_ref, full_ref, words_ref, chosen_ref, asked_ref, in_sems, out_sems, sem = refs[-8:]
    y, x, core = place_ref[0], place_ref[1], place_ref[2]
    tiles = near_ref.shape[1]
    asking = [
        pltpu.make_async_copy(
            source.at[pl.ds(EVENT_BLOCK * ROWS, tiles), :], near_ref.at[i], in_sems.at[i]
        )
        for i, source in enumerate(sources)
    ]
    coming = [
        pltpu.make_async_copy(piece, full_ref.at[i], in_sems.at[len(asks) + i])
        for i, piece in enumerate(held)
    ]
    for copy in asking + coming:
        copy.start()
    for i, ((half, _), copy) in enumerate(zip(asks, asking)):
        copy.wait()
        event = near_ref[i].astype(jnp.float32).astype(jnp.int32)
        words_ref[i] = event * ROWS + (event >> BLOCK_BITS) * (BLOCK_ROWS - EVENT_BLOCK * ROWS)
        for step in range(SIDE):
            tile = tile_of(y, x - step, core) if half == 0 else tile_of(y - step, x, core)
            at = i * SIDE + step
            chosen_ref[at : at + 1, :] = words_ref[i, pl.ds(tile, 1), :]
    copy = pltpu.make_async_copy(chosen_ref, asked_ref, sem)
    copy.start()
    copy.wait()
    for copy in coming:
        copy.wait()
    going = []
    for i, (out_ref, blocks) in enumerate(zip(outs[: len(plan)], plan)):
        packed_ref = outs[len(plan) + i]
        for place, (half, hops, other) in enumerate(blocks):
            which, first = asks.index((half, hops)), halves.index(half) * SIDE
            for step in range(SIDE):
                for slot in range(SLOTS):
                    row = (place * SIDE + step) * SLOTS + slot
                    start = asked_ref[which * SIDE + step, other * SLOTS + slot]
                    packed_ref[row] = full_ref[first + step, pl.ds(pl.multiple_of(start, 16), ROWS), :]
        going.append(pltpu.make_async_copy(packed_ref, out_ref, out_sems.at[i]))
        going[i].start()
    for copy in going:
        copy.wait()


def pack(plan, place, held):
    asks = tuple(sorted({block[:2] for blocks in plan for block in blocks}))
    halves = tuple(sorted({half for half, _ in asks}))
    sources = [held[1 - half][-hops % SIDE] for half, hops in asks]
    pieces = [piece for half in halves for piece in held[half]]
    shape = lambda blocks: (len(blocks) * SIDE * SLOTS, ROWS, LANES)
    tiles = BLOCK_ROWS - EVENT_BLOCK * ROWS
    chosen = ((len(asks) * SIDE + 7) // 8 * 8, LANES)
    return pl.pallas_call(
        functools.partial(pack_kernel, plan, asks, halves),
        in_specs=[SMEM] + [HBM] * (len(asks) + len(pieces)),
        out_specs=[HBM] * len(plan),
        out_shape=[pltpu.HBM(shape(blocks), jnp.bfloat16) for blocks in plan],
        scratch_shapes=[pltpu.VMEM(shape(blocks), jnp.bfloat16) for blocks in plan]
        + [
            pltpu.VMEM((len(asks), tiles, LANES), jnp.bfloat16),
            pltpu.VMEM((len(pieces),) + pieces[0].shape, jnp.bfloat16),
            pltpu.VMEM((len(asks), tiles, LANES), jnp.int32),
            pltpu.VMEM(chosen, jnp.int32),
            pltpu.SMEM(chosen, jnp.int32),
            pltpu.SemaphoreType.DMA((len(asks) + len(pieces),)),
            pltpu.SemaphoreType.DMA((len(plan),)),
            pltpu.SemaphoreType.DMA,
        ],
        compiler_params=PARAMS,
        name="pack",
    )(place, *sources, *pieces)


def pair_kernel(blocks, arrays, first, last, place_ref, local_ref, count_ref, table_ref, *refs):
    own, power = refs[:2], refs[2:4]
    partner = refs[4 : 4 + arrays]
    refs = refs[4 + arrays :]
    if not first:
        before_ref, refs = refs[0], refs[1:]
    out_ref, refs = refs[0], refs[1:]
    if last:
        turned_ref, refs = refs[0], refs[1:]
    cross_ref, energy_ref, factor_ref, came_ref, sems = refs
    y, x, core = place_ref[0], place_ref[1], place_ref[2]
    rows = SIDE * SLOTS
    copies = [
        pltpu.make_async_copy(partner[array].at[pl.ds(offset, rows)], came_ref.at[i], sems.at[i])
        for i, (*_, array, offset) in enumerate(blocks)
    ]
    for copy in copies:
        copy.start()
    if not first:
        out_ref[...] = before_ref[...]
    for number, (half, shift, other, *_) in enumerate(blocks):
        copies[number].wait()
        from_core = lax.rem(core + other, 2)

        def tile_at(step):
            if half == 0:
                return tile_of(y - shift, x - step, from_core)
            return tile_of(y - step, x - shift, from_core)

        def one_tile(step, carry):
            tile = tile_at(step)
            live = count_ref[tile]
            for slot in range(SLOTS):
                event = local_ref[tile * SLOTS + slot]
                mine = own[half][event_rows(event), :].astype(jnp.float32)
                mine = mine.reshape(3, 2, 8, LANES)
                row = step * SLOTS + slot
                theirs = came_ref[number, row].astype(jnp.float32).reshape(3, 2, 8, LANES)
                real = jnp.sum(mine * theirs, axis=(0, 1))
                imag = jnp.sum(mine[:, 1] * theirs[:, 0] - mine[:, 0] * theirs[:, 1], axis=0)
                cross = jnp.concatenate([real, imag], -1)
                cross_ref[pl.ds(pl.multiple_of(row * 8, 8), 8), :] = cross
                energy_ref[row] = jnp.sum(theirs * theirs, axis=(0, 1))
                alive = jnp.where(slot < live, jnp.float32(2.0 / SCALE_WIDTH), jnp.float32(0))
                factor_ref[0, row] = power[half][event]
                factor_ref[1, row] = jnp.full((8, LANES), alive, jnp.float32)
            return carry

        lax.fori_loop(0, SIDE, one_tile, 0)
        corr = jnp.dot(
            cross_ref[...].astype(jnp.bfloat16), table_ref[...], preferred_element_type=jnp.float32
        ).reshape(rows, 8, 2 * LANES)
        low = lax.broadcasted_iota(jnp.int32, (rows, 8, LANES), 1) < 4
        corr = jnp.where(low, corr[..., :LANES], corr[..., LANES:])
        corr = corr + pltpu.roll(corr, 4, 1)
        energy = jnp.broadcast_to(
            jnp.sum(energy_ref[...], axis=-1, keepdims=True), (rows, 8, LANES)
        )
        energy = (energy + pltpu.roll(energy, 4, 1)) * (2.0 / SCALE_WIDTH)
        corr = corr * (lax.rsqrt(factor_ref[0] * energy + 1e-06) * factor_ref[1])
        for step in range(SIDE):
            at = pl.ds(pl.multiple_of(tile_at(jnp.int32(step)) * SLOTS, SLOTS), SLOTS)
            out_ref[at, 4 * half : 4 * half + 4, :] = corr[
                step * SLOTS : (step + 1) * SLOTS, 4 * half : 4 * half + 4
            ]
    if last:
        turned_ref[...] = jnp.sum(out_ref[...], axis=1).T


def pairs(blocks, place, local, count, table, own, power, partner, total, last):
    rows, slots = SIDE * SLOTS, local.shape[0]
    first = total is None
    out_shape = [jax.ShapeDtypeStruct((slots, 8, LAGS), jnp.float32)]
    if last:
        out_shape += [jax.ShapeDtypeStruct((LAGS, slots), jnp.float32)]
    args = [place, local, count, table, *own, *power, *partner] + ([] if first else [total])
    return pl.pallas_call(
        functools.partial(pair_kernel, blocks, len(partner), first, last),
        in_specs=[SMEM] * 3 + [VMEM] * 5 + [HBM] * len(partner) + [VMEM] * (not first),
        out_specs=[VMEM] * len(out_shape),
        out_shape=out_shape,
        scratch_shapes=[
            pltpu.VMEM((rows * 8, 2 * LANES), jnp.float32),
            pltpu.VMEM((rows, 8, LANES), jnp.float32),
            pltpu.VMEM((2, rows, 8, LANES), jnp.float32),
            pltpu.VMEM((len(blocks), rows, ROWS, LANES), jnp.bfloat16),
            pltpu.SemaphoreType.DMA((len(blocks),)),
        ],
        compiler_params=PARAMS,
        name="pairs",
    )(*args)


def hop(value, dy, dx, dcore):
    moves = []
    for y in range(SIDE):
        for x in range(SIDE):
            for core in range(2):
                target = ((y + dy) % SIDE * SIDE + (x + dx) % SIDE) * 2 + (core + dcore) % 2
                moves.append(((y * SIDE + x) * 2 + core, target))
    return lax.ppermute(value, "tile", moves)


def on_device(waves, station_mask, pair_local, pair_remote, pair_count):
    width, tiles = waves.shape[-1], pair_remote.shape[1]
    events, stations = station_mask.shape
    groups = lax.axis_size("sta")
    here = lax.axis_index("tile")
    place = jnp.stack([here // (2 * SIDE), here // 2 % SIDE, here % 2]).astype(jnp.int32)
    local, count = pair_local.reshape(-1), pair_count.reshape(-1)

    other = hop(pair_remote, 0, 0, 1)
    own = own_spectra(waves, station_mask, jnp.asarray(forward_table(width)), pair_remote, other)
    own, power = own[:2], own[2:]

    along = lambda half, value, hops: hop(value, *((0, hops) if half == 0 else (hops, 0)), 0)
    across = lambda half, value, hops, other: hop(value, *((hops, 0) if half == 0 else (0, hops)), other)
    held = [[own[half], None, None, None] for half in range(2)]
    for hops in (1, 3, 2):
        for half in range(2):
            held[half][hops] = along(half, own[half], hops)

    partner = {}
    for half in range(2):
        plan = tuple(((half, hops, other),) for hops in (1, 3, 2) for other in range(2))
        for blocks, value in zip(plan, pack(plan, place, held)):
            partner[blocks[0]] = across(*blocks[0][:1], value, *blocks[0][1:])
    near = pack((((0, 0, 0), (1, 0, 0)), ((0, 0, 1), (1, 0, 1))), place, held)
    near = [near[0], hop(near[1], 0, 0, 1)]
    size = SIDE * SLOTS

    table = jnp.asarray(lag_table(width))
    calc = functools.partial(pairs, place=place, local=local, count=count, table=table, own=own, power=power)
    blocks = tuple((half, 0, other, other, half * size) for half in range(2) for other in range(2))
    total = calc(blocks, partner=near, total=None, last=False)[0]
    for hops in (1, 3, 2):
        keys = [(half, hops, other) for half in range(2) for other in range(2)]
        blocks = tuple((*key, number, 0) for number, key in enumerate(keys))
        total, *stack = calc(blocks, partner=[partner[key] for key in keys], total=total, last=hops == 2)
    stack = stack[0]

    stack = lax.all_to_all(stack, "sta", split_axis=0, concat_axis=0, tiled=True)
    stack = jnp.sum(stack.reshape(groups, LAGS // groups, -1), axis=0).T
    station_coef = total.astype(jnp.bfloat16).reshape(1, tiles, SLOTS, stations, LAGS)
    return (station_coef, stack.reshape(1, tiles, SLOTS, LAGS // groups))


def solution(mesh):
    placed = (
        P("tile", None, "sta", None),
        P("tile", "sta"),
        P("tile", None, None),
        P("tile", None, None),
        P("tile", None),
    )
    return jax.shard_map(
        on_device,
        mesh=mesh,
        in_specs=placed,
        out_specs=(P("tile", None, None, "sta", None), P("tile", None, None, "sta")),
        check_vma=False,
    )
```

```python
import functools
import math

import jax
import jax.numpy as jnp
import ml_dtypes
import numpy as np
from jax import lax
from jax.experimental import pallas as pl
from jax.experimental.pallas import tpu as pltpu
from jax.sharding import PartitionSpec as P

BAND = 256
LAGS = 128
SLOTS = 8
SIDE = 4
LANES = 128
ROWS = 48
BLOCK_BITS = 4
EVENT_BLOCK = 1 << BLOCK_BITS
BLOCK_ROWS = EVENT_BLOCK * ROWS + 32
SCALE_WIDTH = 1024.0
VMEM = pl.BlockSpec(memory_space=pltpu.VMEM)
ANY = pl.BlockSpec(memory_space=pl.ANY)
SMEM = pl.BlockSpec(memory_space=pltpu.SMEM)
PARAMS = pltpu.CompilerParams(vmem_limit_bytes=24 * 1024 * 1024)


def forward_table(width):
    phase = np.arange(width)[:, None] * np.arange(1, BAND + 1)[None, :] % width * (2.0 * math.pi / width)
    return np.concatenate([np.cos(phase), -np.sin(phase)], 1).astype(ml_dtypes.bfloat16)


def lag_table(width):
    phase = np.arange(1, BAND + 1)[:, None] * (np.arange(LAGS)[None, :] - LAGS // 2) % width
    phase = phase * (2.0 * math.pi / width)
    table = np.concatenate([np.cos(phase), -np.sin(phase)], 0).astype(ml_dtypes.bfloat16)
    low_re, high_re, low_im, high_im = (table[i * LANES : (i + 1) * LANES] for i in range(4))
    return np.concatenate(
        [np.concatenate([low_re, high_re], 1), np.concatenate([low_im, high_im], 1)], 0
    )


def spectra_kernel(waves_ref, mask_ref, table_ref, mine_ref, other_ref, *outs):
    events = mask_ref.shape[0]
    same = lax.broadcasted_iota(jnp.int32, (1, 8, 8), 1) == lax.broadcasted_iota(jnp.int32, (1, 8, 8), 2)
    mask = jnp.where(same, mask_ref[...].astype(jnp.float32)[:, None, :], 0.0)
    mask = jnp.sum(mask, axis=-1, keepdims=True)[:, None]
    mine, other = mine_ref[0], other_ref[0]
    blank = jnp.zeros((mine.shape[0], LANES - 2 * SLOTS), mine.dtype)
    asked = jnp.concatenate([mine, other, blank], 1).astype(jnp.float32).astype(jnp.bfloat16)
    flat = jnp.dot(waves_ref[...], table_ref[...], preferred_element_type=jnp.float32)
    flat = flat.reshape(events, 3, 8, 4 * LANES) * mask
    part = [flat[..., i * LANES : (i + 1) * LANES].reshape(events * 3, 8, LANES) for i in range(4)]
    turned = [pltpu.roll(value, 4, 1) for value in part]
    low = lax.broadcasted_iota(jnp.int32, part[0].shape, 1) < 4
    halves = (
        (jnp.where(low, part[0], turned[1]), jnp.where(low, part[2], turned[3])),
        (jnp.where(low, turned[0], part[1]), jnp.where(low, turned[2], part[3])),
    )
    for (real, imag), out_ref, power_ref in zip(halves, outs[:2], outs[2:]):
        packed = jnp.concatenate([real, imag], 1).astype(jnp.bfloat16)
        out_ref[: events * ROWS, :] = packed.reshape(events * ROWS, LANES)
        out_ref[events * ROWS :, :] = asked
        values = packed.astype(jnp.float32).reshape(events, 3, 2, 8, LANES)
        total = jnp.sum(values * values, axis=(1, 2))
        total = jnp.broadcast_to(jnp.sum(total, axis=-1, keepdims=True), (events, 8, LANES))
        power_ref[...] = (total + pltpu.roll(total, 4, 1)) * (2.0 / SCALE_WIDTH)


def own_spectra(waves, mask, table, mine, other):
    events = waves.shape[0]
    flat = waves.reshape(-1, waves.shape[-1])
    block = EVENT_BLOCK
    half = jax.ShapeDtypeStruct((events // block * BLOCK_ROWS, LANES), jnp.bfloat16)
    power = jax.ShapeDtypeStruct((events, 8, LANES), jnp.float32)
    spec = pl.BlockSpec((block, 8, LANES), lambda i: (i, 0, 0))
    return pl.pallas_call(
        spectra_kernel,
        grid=(events // block,),
        in_specs=[
            pl.BlockSpec((block * 24, flat.shape[-1]), lambda i: (i, 0)),
            pl.BlockSpec((block, mask.shape[1]), lambda i: (i, 0)),
            pl.BlockSpec(table.shape, lambda i: (0, 0)),
            pl.BlockSpec(mine.shape, lambda i: (0, 0, 0)),
            pl.BlockSpec(mine.shape, lambda i: (0, 0, 0)),
        ],
        out_specs=[pl.BlockSpec((BLOCK_ROWS, LANES), lambda i: (i, 0))] * 2 + [spec] * 2,
        out_shape=[half, half, power, power],
        compiler_params=PARAMS,
        name="spectra",
    )(flat, mask, table, mine, other)


def event_rows(event):
    start = event * ROWS + (event >> BLOCK_BITS) * (BLOCK_ROWS - EVENT_BLOCK * ROWS)
    return pl.ds(pl.multiple_of(start, 16), ROWS)


def tile_of(y, x, core):
    return (lax.rem(y + SIDE, SIDE) * SIDE + lax.rem(x + SIDE, SIDE)) * 2 + core


def pack_kernel(plan, asks, halves, place_ref, *refs):
    held, outs = refs[:2], refs[2:-8]
    near_ref, full_ref, words_ref, chosen_ref, asked_ref, in_sems, out_sems, sem = refs[-8:]
    y, x, core = place_ref[0], place_ref[1], place_ref[2]
    tiles, size = near_ref.shape[1], held[0].shape[0] // SIDE
    asking = []
    for i, (half, hops) in enumerate(asks):
        asker = lax.rem((y if half == 0 else x) + hops, SIDE)
        start = pl.multiple_of(asker * size + EVENT_BLOCK * ROWS, 16)
        source = held[1 - half].at[pl.ds(start, tiles), :]
        asking.append(pltpu.make_async_copy(source, near_ref.at[i], in_sems.at[i]))
    coming = [
        pltpu.make_async_copy(held[half], full_ref.at[i], in_sems.at[len(asks) + i])
        for i, half in enumerate(halves)
    ]
    for copy in asking + coming:
        copy.start()
    for i, ((half, _), copy) in enumerate(zip(asks, asking)):
        copy.wait()
        event = near_ref[i].astype(jnp.float32).astype(jnp.int32)
        words_ref[i] = event * ROWS + (event >> BLOCK_BITS) * (BLOCK_ROWS - EVENT_BLOCK * ROWS)
        for step in range(SIDE):
            tile = tile_of(y, x - step, core) if half == 0 else tile_of(y - step, x, core)
            at = i * SIDE + step
            start = lax.rem((x if half == 0 else y) - step + SIDE, SIDE) * size
            chosen_ref[at : at + 1, :] = words_ref[i, pl.ds(tile, 1), :] + start
    copy = pltpu.make_async_copy(chosen_ref, asked_ref, sem)
    copy.start()
    copy.wait()
    for copy in coming:
        copy.wait()
    going = []
    for i, (out_ref, blocks) in enumerate(zip(outs[: len(plan)], plan)):
        packed_ref = outs[len(plan) + i]
        for place, (half, hops, other) in enumerate(blocks):
            which, first = asks.index((half, hops)), halves.index(half)
            for step in range(SIDE):
                for slot in range(SLOTS):
                    row = (place * SIDE + step) * SLOTS + slot
                    start = asked_ref[which * SIDE + step, other * SLOTS + slot]
                    packed_ref[row] = full_ref[first, pl.ds(pl.multiple_of(start, 16), ROWS), :]
        going.append(pltpu.make_async_copy(packed_ref, out_ref, out_sems.at[i]))
        going[i].start()
    for copy in going:
        copy.wait()


def pack(plan, place, held):
    asks = tuple(sorted({block[:2] for blocks in plan for block in blocks}))
    halves = tuple(sorted({half for half, _ in asks}))
    shape = lambda blocks: (len(blocks) * SIDE * SLOTS, ROWS, LANES)
    tiles = BLOCK_ROWS - EVENT_BLOCK * ROWS
    chosen = ((len(asks) * SIDE + 7) // 8 * 8, LANES)
    return pl.pallas_call(
        functools.partial(pack_kernel, plan, asks, halves),
        in_specs=[SMEM] + [ANY] * 2,
        out_specs=[ANY] * len(plan),
        out_shape=[jax.ShapeDtypeStruct(shape(blocks), jnp.bfloat16) for blocks in plan],
        scratch_shapes=[pltpu.VMEM(shape(blocks), jnp.bfloat16) for blocks in plan]
        + [
            pltpu.VMEM((len(asks), tiles, LANES), jnp.bfloat16),
            pltpu.VMEM((len(halves),) + held[0].shape, jnp.bfloat16),
            pltpu.VMEM((len(asks), tiles, LANES), jnp.int32),
            pltpu.VMEM(chosen, jnp.int32),
            pltpu.SMEM(chosen, jnp.int32),
            pltpu.SemaphoreType.DMA((len(asks) + len(halves),)),
            pltpu.SemaphoreType.DMA((len(plan),)),
            pltpu.SemaphoreType.DMA,
        ],
        compiler_params=PARAMS,
        name="pack",
    )(place, *held)


def join_kernel(count, *refs):
    parts, out_ref = refs[:count], refs[-1]
    size = parts[0].shape[0] // 2
    for i, part in enumerate(parts):
        out_ref[i * size : (i + 1) * size] = part[size:]


def join(parts, after):
    count = len(parts)
    shape = (parts[0].shape[0] // 2 * count,) + parts[0].shape[1:]
    return pl.pallas_call(
        functools.partial(join_kernel, count),
        in_specs=[VMEM] * count + [ANY] * len(after),
        out_specs=VMEM,
        out_shape=jax.ShapeDtypeStruct(shape, parts[0].dtype),
        compiler_params=PARAMS,
        name="join",
    )(*parts, *after)


def pair_kernel(blocks, arrays, first, last, place_ref, local_ref, count_ref, table_ref, *refs):
    own, power = refs[:2], refs[2:4]
    partner = refs[4 : 4 + arrays]
    refs = refs[4 + arrays :]
    if not first:
        before_ref, refs = refs[0], refs[1:]
    out_ref, refs = refs[0], refs[1:]
    if last:
        turned_ref, refs = refs[0], refs[1:]
    cross_ref, energy_ref, factor_ref, came_ref, sems = refs
    y, x, core = place_ref[0], place_ref[1], place_ref[2]
    rows = SIDE * SLOTS
    copies = [
        pltpu.make_async_copy(partner[array].at[pl.ds(offset, rows)], came_ref.at[i], sems.at[i])
        for i, (*_, array, offset) in enumerate(blocks)
    ]
    for copy in copies:
        copy.start()
    if not first:
        out_ref[...] = before_ref[...]
    for number, (half, shift, other, *_) in enumerate(blocks):
        copies[number].wait()
        from_core = lax.rem(core + other, 2)

        def tile_at(step):
            if half == 0:
                return tile_of(y - shift, x - step, from_core)
            return tile_of(y - step, x - shift, from_core)

        def one_tile(step, carry):
            tile = tile_at(step)
            live = count_ref[tile]
            for slot in range(SLOTS):
                event = local_ref[tile * SLOTS + slot]
                mine = own[half][event_rows(event), :].astype(jnp.float32)
                mine = mine.reshape(3, 2, 8, LANES)
                row = step * SLOTS + slot
                theirs = came_ref[number, row].astype(jnp.float32).reshape(3, 2, 8, LANES)
                real = jnp.sum(mine * theirs, axis=(0, 1))
                imag = jnp.sum(mine[:, 1] * theirs[:, 0] - mine[:, 0] * theirs[:, 1], axis=0)
                cross = jnp.concatenate([real, imag], -1)
                cross_ref[pl.ds(pl.multiple_of(row * 8, 8), 8), :] = cross
                energy_ref[row] = jnp.sum(theirs * theirs, axis=(0, 1))
                alive = jnp.where(slot < live, jnp.float32(2.0 / SCALE_WIDTH), jnp.float32(0))
                factor_ref[0, row] = power[half][event]
                factor_ref[1, row] = jnp.full((8, LANES), alive, jnp.float32)
            return carry

        lax.fori_loop(0, SIDE, one_tile, 0)
        corr = jnp.dot(
            cross_ref[...].astype(jnp.bfloat16), table_ref[...], preferred_element_type=jnp.float32
        ).reshape(rows, 8, 2 * LANES)
        low = lax.broadcasted_iota(jnp.int32, (rows, 8, LANES), 1) < 4
        corr = jnp.where(low, corr[..., :LANES], corr[..., LANES:])
        corr = corr + pltpu.roll(corr, 4, 1)
        energy = jnp.broadcast_to(
            jnp.sum(energy_ref[...], axis=-1, keepdims=True), (rows, 8, LANES)
        )
        energy = (energy + pltpu.roll(energy, 4, 1)) * (2.0 / SCALE_WIDTH)
        corr = corr * (lax.rsqrt(factor_ref[0] * energy + 1e-06) * factor_ref[1])
        for step in range(SIDE):
            at = pl.ds(pl.multiple_of(tile_at(jnp.int32(step)) * SLOTS, SLOTS), SLOTS)
            out_ref[at, 4 * half : 4 * half + 4, :] = corr[
                step * SLOTS : (step + 1) * SLOTS, 4 * half : 4 * half + 4
            ]
    if last:
        turned_ref[...] = jnp.sum(out_ref[...], axis=1).T


def pairs(blocks, place, local, count, table, own, power, partner, total, last):
    rows, slots = SIDE * SLOTS, local.shape[0]
    first = total is None
    out_shape = [jax.ShapeDtypeStruct((slots, 8, LAGS), jnp.float32)]
    if last:
        out_shape += [jax.ShapeDtypeStruct((LAGS, slots), jnp.float32)]
    args = [place, local, count, table, *own, *power, *partner] + ([] if first else [total])
    return pl.pallas_call(
        functools.partial(pair_kernel, blocks, len(partner), first, last),
        in_specs=[SMEM] * 3 + [VMEM] * 5 + [ANY] * len(partner) + [VMEM] * (not first),
        out_specs=[VMEM] * len(out_shape),
        out_shape=out_shape,
        scratch_shapes=[
            pltpu.VMEM((rows * 8, 2 * LANES), jnp.float32),
            pltpu.VMEM((rows, 8, LANES), jnp.float32),
            pltpu.VMEM((2, rows, 8, LANES), jnp.float32),
            pltpu.VMEM((len(blocks), rows, ROWS, LANES), jnp.bfloat16),
            pltpu.SemaphoreType.DMA((len(blocks),)),
        ],
        compiler_params=PARAMS,
        name="pairs",
    )(*args)


def hop(value, dy, dx, dcore):
    moves = []
    for y in range(SIDE):
        for x in range(SIDE):
            for core in range(2):
                target = ((y + dy) % SIDE * SIDE + (x + dx) % SIDE) * 2 + (core + dcore) % 2
                moves.append(((y * SIDE + x) * 2 + core, target))
    return lax.ppermute(value, "tile", moves)


def on_device(waves, station_mask, pair_local, pair_remote, pair_count):
    width, tiles = waves.shape[-1], pair_remote.shape[1]
    events, stations = station_mask.shape
    groups = lax.axis_size("sta")
    here = lax.axis_index("tile")
    place = jnp.stack([here // (2 * SIDE), here // 2 % SIDE, here % 2]).astype(jnp.int32)
    local, count = pair_local.reshape(-1), pair_count.reshape(-1)

    other = hop(pair_remote, 0, 0, 1)
    own = own_spectra(waves, station_mask, jnp.asarray(forward_table(width)), pair_remote, other)
    own, power = own[:2], own[2:]

    row = [[(y * SIDE + x) * 2 + c for x in range(SIDE)] for y in range(SIDE) for c in range(2)]
    column = [[(y * SIDE + x) * 2 + c for y in range(SIDE)] for x in range(SIDE) for c in range(2)]
    held = [
        lax.all_gather(value, "tile", axis=0, tiled=True, axis_index_groups=who)
        for value, who in zip(own, (row, column))
    ]
    across = lambda half, value, hops, other: hop(value, *((hops, 0) if half == 0 else (0, hops)), other)

    beside = [(half, hops) for half in range(2) for hops in (1, 3)]
    got = pack(tuple(((*where, 0), (*where, 1)) for where in beside), place, held)
    got = [across(where[0], value, where[1], 0) for value, where in zip(got, beside)]
    rest = pack(
        tuple(((half, 2, other),) for half in range(2) for other in range(2))
        + (((0, 0, 0), (1, 0, 0)), ((0, 0, 1), (1, 0, 1))),
        place,
        held,
    )
    far = [across(number // 2, rest[number], 2, number % 2) for number in range(4)]
    near = [rest[4], hop(rest[5], 0, 0, 1)]
    size = SIDE * SLOTS
    swapped = hop(join(got, [rest[0]]), 0, 0, 1)

    table = jnp.asarray(lag_table(width))
    calc = functools.partial(pairs, place=place, local=local, count=count, table=table, own=own, power=power)
    blocks = tuple((half, 0, other, other, half * size) for half in range(2) for other in range(2))
    total = calc(blocks, partner=near, total=None, last=False)[0]
    blocks = tuple((*where, 0, number, 0) for number, where in enumerate(beside))
    total = calc(blocks, partner=got, total=total, last=False)[0]
    blocks = tuple((*where, 1, 0, number * size) for number, where in enumerate(beside))
    total = calc(blocks, partner=[swapped], total=total, last=False)[0]
    blocks = tuple((half, 2, other, half * 2 + other, 0) for half in range(2) for other in range(2))
    total, stack = calc(blocks, partner=far, total=total, last=True)

    stack = lax.all_to_all(stack, "sta", split_axis=0, concat_axis=0, tiled=True)
    stack = jnp.sum(stack.reshape(groups, LAGS // groups, -1), axis=0).T
    station_coef = total.astype(jnp.bfloat16).reshape(1, tiles, SLOTS, stations, LAGS)
    return (station_coef, stack.reshape(1, tiles, SLOTS, LAGS // groups))


def solution(mesh):
    placed = (
        P("tile", None, "sta", None),
        P("tile", "sta"),
        P("tile", None, None),
        P("tile", None, None),
        P("tile", None),
    )
    return jax.shard_map(
        on_device,
        mesh=mesh,
        in_specs=placed,
        out_specs=(P("tile", None, None, "sta", None), P("tile", None, None, "sta")),
        check_vma=False,
    )
```

```python
import functools
import math

import jax
import jax.numpy as jnp
import ml_dtypes
import numpy as np
from jax import lax
from jax.experimental import pallas as pl
from jax.experimental.pallas import tpu as pltpu
from jax.sharding import PartitionSpec as P

BAND = 256
LAGS = 128
SLOTS = 8
SIDE = 4
LANES = 128
ROWS = 48
BLOCK_BITS = 4
EVENT_BLOCK = 1 << BLOCK_BITS
BLOCK_ROWS = EVENT_BLOCK * ROWS + 32
SCALE_WIDTH = 1024.0
VMEM = pl.BlockSpec(memory_space=pltpu.VMEM)
ANY = pl.BlockSpec(memory_space=pl.ANY)
SMEM = pl.BlockSpec(memory_space=pltpu.SMEM)
PARAMS = pltpu.CompilerParams(vmem_limit_bytes=24 * 1024 * 1024)


def forward_table(width):
    phase = np.arange(width)[:, None] * np.arange(1, BAND + 1)[None, :] % width * (2.0 * math.pi / width)
    return np.concatenate([np.cos(phase), -np.sin(phase)], 1).astype(ml_dtypes.bfloat16)


def lag_table(width):
    phase = np.arange(1, BAND + 1)[:, None] * (np.arange(LAGS)[None, :] - LAGS // 2) % width
    phase = phase * (2.0 * math.pi / width)
    table = np.concatenate([np.cos(phase), -np.sin(phase)], 0).astype(ml_dtypes.bfloat16)
    low_re, high_re, low_im, high_im = (table[i * LANES : (i + 1) * LANES] for i in range(4))
    return np.concatenate(
        [np.concatenate([low_re, high_re], 1), np.concatenate([low_im, high_im], 1)], 0
    )


def spectra_kernel(waves_ref, mask_ref, table_ref, mine_ref, other_ref, *refs):
    outs, (came_ref, factors_ref, sems) = refs[:2], refs[2:]
    rows = EVENT_BLOCK * 24
    blocks = waves_ref.shape[0] // rows
    copies = [pltpu.make_async_copy(table_ref, factors_ref, sems.at[blocks])]
    copies += [
        pltpu.make_async_copy(waves_ref.at[pl.ds(i * rows, rows), :], came_ref.at[i], sems.at[i])
        for i in range(blocks)
    ]
    for copy in copies:
        copy.start()
    same = lax.broadcasted_iota(jnp.int32, (1, 8, 8), 1) == lax.broadcasted_iota(jnp.int32, (1, 8, 8), 2)
    mine, other = mine_ref[0], other_ref[0]
    blank = jnp.zeros((mine.shape[0], LANES - 2 * SLOTS), mine.dtype)
    asked = jnp.concatenate([mine, other, blank], 1).astype(jnp.float32).astype(jnp.bfloat16)
    copies[0].wait()
    low = lax.broadcasted_iota(jnp.int32, (EVENT_BLOCK * 3, 8, LANES), 1) < 4
    for block in range(blocks):
        mask = mask_ref[block * EVENT_BLOCK : (block + 1) * EVENT_BLOCK, :].astype(jnp.float32)
        mask = jnp.sum(jnp.where(same, mask[:, None, :], 0.0), axis=-1, keepdims=True)[:, None]
        copies[block + 1].wait()
        flat = jnp.dot(came_ref[block], factors_ref[...], preferred_element_type=jnp.float32)
        flat = flat.reshape(EVENT_BLOCK, 3, 8, 4 * LANES) * mask
        part = [
            flat[..., i * LANES : (i + 1) * LANES].reshape(EVENT_BLOCK * 3, 8, LANES)
            for i in range(4)
        ]
        turned = [pltpu.roll(value, 4, 1) for value in part]
        halves = (
            (jnp.where(low, part[0], turned[1]), jnp.where(low, part[2], turned[3])),
            (jnp.where(low, turned[0], part[1]), jnp.where(low, turned[2], part[3])),
        )
        first, last = block * BLOCK_ROWS, block * BLOCK_ROWS + EVENT_BLOCK * ROWS
        for (real, imag), out_ref in zip(halves, outs):
            packed = jnp.concatenate([real, imag], 1).astype(jnp.bfloat16)
            out_ref[first:last, :] = packed.reshape(EVENT_BLOCK * ROWS, LANES)
            out_ref[last : first + BLOCK_ROWS, :] = asked


def own_spectra(waves, mask, table, mine, other):
    flat = waves.reshape(-1, waves.shape[-1])
    blocks = mask.shape[0] // EVENT_BLOCK
    half = jax.ShapeDtypeStruct((blocks * BLOCK_ROWS, LANES), jnp.bfloat16)
    return pl.pallas_call(
        spectra_kernel,
        in_specs=[ANY, VMEM, ANY, VMEM, VMEM],
        out_specs=[VMEM] * 2,
        out_shape=[half, half],
        scratch_shapes=[
            pltpu.VMEM((blocks, flat.shape[0] // blocks, flat.shape[1]), flat.dtype),
            pltpu.VMEM(table.shape, table.dtype),
            pltpu.SemaphoreType.DMA((blocks + 1,)),
        ],
        compiler_params=PARAMS,
        name="spectra",
    )(flat, mask, table, mine, other)


def power_kernel(first_ref, second_ref, *outs):
    for spectra_ref, out_ref in zip((first_ref, second_ref), outs):
        for block in range(out_ref.shape[0] // EVENT_BLOCK):
            start = block * BLOCK_ROWS
            values = spectra_ref[start : start + EVENT_BLOCK * ROWS, :].astype(jnp.float32)
            values = values.reshape(EVENT_BLOCK, 3, 2, 8, LANES)
            total = jnp.sum(jnp.sum(values * values, axis=(1, 2)), axis=-1, keepdims=True)
            total = jnp.broadcast_to(total, (EVENT_BLOCK, 8, LANES))
            total = (total + pltpu.roll(total, 4, 1)) * (2.0 / SCALE_WIDTH)
            out_ref[block * EVENT_BLOCK : (block + 1) * EVENT_BLOCK] = total


def own_power(own):
    events = own[0].shape[0] // BLOCK_ROWS * EVENT_BLOCK
    return pl.pallas_call(
        power_kernel,
        in_specs=[VMEM] * 2,
        out_specs=[VMEM] * 2,
        out_shape=[jax.ShapeDtypeStruct((events, 8, LANES), jnp.float32)] * 2,
        compiler_params=PARAMS,
        name="power",
    )(*own)


def split(values):
    rows = values[0].shape[0]
    part = lambda i: pl.BlockSpec((rows // 2, LANES), lambda _: (i % 2, 0))
    whole = pl.BlockSpec((rows // 2, LANES), lambda _: (0, 0))

    def kernel(*refs):
        for in_ref, out_ref in zip(refs[: len(values)], refs[len(values) :]):
            out_ref[...] = in_ref[...]

    return pl.pallas_call(
        kernel,
        grid=(1,),
        in_specs=[part(i) for i in range(len(values))],
        out_specs=[whole] * len(values),
        out_shape=[jax.ShapeDtypeStruct((rows // 2, LANES), values[0].dtype)] * len(values),
        compiler_params=PARAMS,
        name="split",
    )(*values)


def event_rows(event):
    start = event * ROWS + (event >> BLOCK_BITS) * (BLOCK_ROWS - EVENT_BLOCK * ROWS)
    return pl.ds(pl.multiple_of(start, 16), ROWS)


def tile_of(y, x, core):
    return (lax.rem(y + SIDE, SIDE) * SIDE + lax.rem(x + SIDE, SIDE)) * 2 + core


def pack_kernel(plan, asks, halves, later, place_ref, *refs):
    sources, refs = refs[: len(asks)], refs[len(asks) :]
    held, outs = refs[: 5 * len(halves)], refs[5 * len(halves) + later : -8]
    near_ref, full_ref, words_ref, chosen_ref, asked_ref, in_sems, out_sems, sem = refs[-8:]
    y, x, core = place_ref[0], place_ref[1], place_ref[2]
    tiles, size = near_ref.shape[1], full_ref.shape[2]
    asking = [
        pltpu.make_async_copy(
            source.at[pl.ds(EVENT_BLOCK * ROWS, tiles), :], near_ref.at[i], in_sems.at[i]
        )
        for i, source in enumerate(sources)
    ]
    coming = []
    for i in range(len(halves)):
        steps = ((0, 0, size), (1, 0, size), (3, 0, size), (2, 0, size // 2), (2, size // 2, size // 2))
        for number, (step, start, length) in enumerate(steps):
            target = full_ref.at[i, step, pl.ds(start, length), :]
            which = 5 * i + number
            coming.append(pltpu.make_async_copy(held[which], target, in_sems.at[len(asks) + which]))
    for copy in asking + coming:
        copy.start()
    for i, ((half, _), copy) in enumerate(zip(asks, asking)):
        copy.wait()
        event = near_ref[i].astype(jnp.float32).astype(jnp.int32)
        words_ref[i] = event * ROWS + (event >> BLOCK_BITS) * (BLOCK_ROWS - EVENT_BLOCK * ROWS)
        for step in range(SIDE):
            tile = tile_of(y, x - step, core) if half == 0 else tile_of(y - step, x, core)
            at = i * SIDE + step
            chosen_ref[at : at + 1, :] = words_ref[i, pl.ds(tile, 1), :]
    copy = pltpu.make_async_copy(chosen_ref, asked_ref, sem)
    copy.start()
    copy.wait()
    going = []
    for i, (out_ref, blocks) in enumerate(zip(outs[: len(plan)], plan)):
        packed_ref = outs[len(plan) + i]
        for place, (half, hops, other) in enumerate(blocks):
            which, first = asks.index((half, hops)), halves.index(half)
            while len(coming) > 5 * (len(halves) - 1 - first):
                coming.pop(0).wait()
            for step in range(SIDE):
                for slot in range(SLOTS):
                    row = (place * SIDE + step) * SLOTS + slot
                    start = asked_ref[which * SIDE + step, other * SLOTS + slot]
                    packed_ref[row] = full_ref[first, step, pl.ds(pl.multiple_of(start, 16), ROWS), :]
        going.append(pltpu.make_async_copy(packed_ref, out_ref, out_sems.at[i]))
        going[i].start()
    for copy in going:
        copy.wait()


def pack(plan, place, held, after=()):
    asks = tuple(sorted({block[:2] for blocks in plan for block in blocks}))
    halves = tuple(sorted({half for half, _ in asks}))
    sources = [held[1 - half][{0: 0, 1: 2, 2: 3, 3: 1}[hops]] for half, hops in asks]
    pieces = [piece for half in halves for piece in held[half]]
    shape = lambda blocks: (len(blocks) * SIDE * SLOTS, ROWS, LANES)
    tiles = BLOCK_ROWS - EVENT_BLOCK * ROWS
    chosen = ((len(asks) * SIDE + 7) // 8 * 8, LANES)
    return pl.pallas_call(
        functools.partial(pack_kernel, plan, asks, halves, len(after)),
        in_specs=[SMEM] + [ANY] * (len(asks) + len(pieces) + len(after)),
        out_specs=[ANY] * len(plan),
        out_shape=[jax.ShapeDtypeStruct(shape(blocks), jnp.bfloat16) for blocks in plan],
        scratch_shapes=[pltpu.VMEM(shape(blocks), jnp.bfloat16) for blocks in plan]
        + [
            pltpu.VMEM((len(asks), tiles, LANES), jnp.bfloat16),
            pltpu.VMEM((len(halves), SIDE) + pieces[0].shape, jnp.bfloat16),
            pltpu.VMEM((len(asks), tiles, LANES), jnp.int32),
            pltpu.VMEM(chosen, jnp.int32),
            pltpu.SMEM(chosen, jnp.int32),
            pltpu.SemaphoreType.DMA((len(asks) + len(pieces),)),
            pltpu.SemaphoreType.DMA((len(plan),)),
            pltpu.SemaphoreType.DMA,
        ],
        compiler_params=PARAMS,
        name="pack",
    )(place, *sources, *pieces, *after)


def join_kernel(count, *refs):
    parts, out_ref = refs[:count], refs[-1]
    size = parts[0].shape[0] // 2
    for i, part in enumerate(parts):
        out_ref[i * size : (i + 1) * size] = part[size:]


def join(parts, after):
    count = len(parts)
    shape = (parts[0].shape[0] // 2 * count,) + parts[0].shape[1:]
    return pl.pallas_call(
        functools.partial(join_kernel, count),
        in_specs=[VMEM] * count + [ANY] * len(after),
        out_specs=VMEM,
        out_shape=jax.ShapeDtypeStruct(shape, parts[0].dtype),
        compiler_params=PARAMS,
        name="join",
    )(*parts, *after)


def pair_kernel(blocks, arrays, first, last, place_ref, local_ref, count_ref, table_ref, *refs):
    own, power = refs[:2], refs[2:4]
    partner = refs[4 : 4 + arrays]
    refs = refs[4 + arrays :]
    if not first:
        before_ref, refs = refs[0], refs[1:]
    out_ref, refs = refs[0], refs[1:]
    if last:
        turned_ref, refs = refs[0], refs[1:]
    cross_ref, energy_ref, factor_ref, came_ref, sems = refs
    y, x, core = place_ref[0], place_ref[1], place_ref[2]
    rows = SIDE * SLOTS
    copies = [
        pltpu.make_async_copy(partner[array].at[pl.ds(offset, rows)], came_ref.at[i], sems.at[i])
        for i, (*_, array, offset) in enumerate(blocks)
    ]
    for copy in copies:
        copy.start()
    if not first:
        out_ref[...] = before_ref[...]
    for number, (half, shift, other, *_) in enumerate(blocks):
        copies[number].wait()
        from_core = lax.rem(core + other, 2)

        def tile_at(step):
            if half == 0:
                return tile_of(y - shift, x - step, from_core)
            return tile_of(y - step, x - shift, from_core)

        def one_tile(step, carry):
            tile = tile_at(step)
            live = count_ref[tile]
            for slot in range(SLOTS):
                event = local_ref[tile * SLOTS + slot]
                mine = own[half][event_rows(event), :].astype(jnp.float32)
                mine = mine.reshape(3, 2, 8, LANES)
                row = step * SLOTS + slot
                theirs = came_ref[number, row].astype(jnp.float32).reshape(3, 2, 8, LANES)
                real = jnp.sum(mine * theirs, axis=(0, 1))
                imag = jnp.sum(mine[:, 1] * theirs[:, 0] - mine[:, 0] * theirs[:, 1], axis=0)
                cross = jnp.concatenate([real, imag], -1)
                cross_ref[pl.ds(pl.multiple_of(row * 8, 8), 8), :] = cross
                energy_ref[row] = jnp.sum(theirs * theirs, axis=(0, 1))
                alive = jnp.where(slot < live, jnp.float32(2.0 / SCALE_WIDTH), jnp.float32(0))
                factor_ref[0, row] = power[half][event]
                factor_ref[1, row] = jnp.full((8, LANES), alive, jnp.float32)
            return carry

        lax.fori_loop(0, SIDE, one_tile, 0)
        corr = jnp.dot(
            cross_ref[...].astype(jnp.bfloat16), table_ref[...], preferred_element_type=jnp.float32
        ).reshape(rows, 8, 2 * LANES)
        low = lax.broadcasted_iota(jnp.int32, (rows, 8, LANES), 1) < 4
        corr = jnp.where(low, corr[..., :LANES], corr[..., LANES:])
        corr = corr + pltpu.roll(corr, 4, 1)
        energy = jnp.broadcast_to(
            jnp.sum(energy_ref[...], axis=-1, keepdims=True), (rows, 8, LANES)
        )
        energy = (energy + pltpu.roll(energy, 4, 1)) * (2.0 / SCALE_WIDTH)
        corr = corr * (lax.rsqrt(factor_ref[0] * energy + 1e-06) * factor_ref[1])
        for step in range(SIDE):
            at = pl.ds(pl.multiple_of(tile_at(jnp.int32(step)) * SLOTS, SLOTS), SLOTS)
            out_ref[at, 4 * half : 4 * half + 4, :] = corr[
                step * SLOTS : (step + 1) * SLOTS, 4 * half : 4 * half + 4
            ]
    if last:
        turned_ref[...] = jnp.sum(out_ref[...], axis=1).T


def pairs(blocks, place, local, count, table, own, power, partner, total, last):
    rows, slots = SIDE * SLOTS, local.shape[0]
    first = total is None
    out_shape = [jax.ShapeDtypeStruct((slots, 8, LAGS), jnp.float32)]
    if last:
        out_shape += [jax.ShapeDtypeStruct((LAGS, slots), jnp.float32)]
    args = [place, local, count, table, *own, *power, *partner] + ([] if first else [total])
    return pl.pallas_call(
        functools.partial(pair_kernel, blocks, len(partner), first, last),
        in_specs=[SMEM] * 3 + [VMEM] * 5 + [ANY] * len(partner) + [VMEM] * (not first),
        out_specs=[VMEM] * len(out_shape),
        out_shape=out_shape,
        scratch_shapes=[
            pltpu.VMEM((rows * 8, 2 * LANES), jnp.float32),
            pltpu.VMEM((rows, 8, LANES), jnp.float32),
            pltpu.VMEM((2, rows, 8, LANES), jnp.float32),
            pltpu.VMEM((len(blocks), rows, ROWS, LANES), jnp.bfloat16),
            pltpu.SemaphoreType.DMA((len(blocks),)),
        ],
        compiler_params=PARAMS,
        name="pairs",
    )(*args)


def hop(value, dy, dx, dcore):
    moves = []
    for y in range(SIDE):
        for x in range(SIDE):
            for core in range(2):
                target = ((y + dy) % SIDE * SIDE + (x + dx) % SIDE) * 2 + (core + dcore) % 2
                moves.append(((y * SIDE + x) * 2 + core, target))
    return lax.ppermute(value, "tile", moves)


def on_device(waves, station_mask, pair_local, pair_remote, pair_count):
    width, tiles = waves.shape[-1], pair_remote.shape[1]
    events, stations = station_mask.shape
    groups = lax.axis_size("sta")
    here = lax.axis_index("tile")
    place = jnp.stack([here // (2 * SIDE), here // 2 % SIDE, here % 2]).astype(jnp.int32)
    local, count = pair_local.reshape(-1), pair_count.reshape(-1)

    other = hop(pair_remote, 0, 0, 1)
    own = own_spectra(waves, station_mask, jnp.asarray(forward_table(width)), pair_remote, other)
    power = own_power(own)

    along = lambda half, value, hops: hop(value, *((0, hops) if half == 0 else (hops, 0)), 0)
    came = [along(half, own[half], hops) for half in range(2) for hops in (1, SIDE - 1)]
    passed = split(came)
    far = [along(i // 2, value, (1, SIDE - 1)[i % 2]) for i, value in enumerate(passed)]
    held = [[own[half], *came[2 * half : 2 * half + 2], *far[2 * half : 2 * half + 2]] for half in range(2)]
    across = lambda half, value, hops, other: hop(value, *((hops, 0) if half == 0 else (0, hops)), other)

    beside = [(half, hops) for half in range(2) for hops in (1, 3)]
    packed = pack(tuple(((*where, 0), (*where, 1)) for where in beside), place, held)
    got = [across(where[0], value, where[1], 0) for value, where in zip(packed, beside)]
    rest = pack(
        tuple(((half, 2, other),) for half in range(2) for other in range(2))
        + (((0, 0, 0), (1, 0, 0)), ((0, 0, 1), (1, 0, 1))),
        place,
        held,
        packed[:1],
    )
    far = [across(number // 2, rest[number], 2, number % 2) for number in range(4)]
    near = [rest[4], hop(rest[5], 0, 0, 1)]
    size = SIDE * SLOTS
    swapped = hop(join(got, [rest[0], near[1]]), 0, 0, 1)

    table = jnp.asarray(lag_table(width))
    calc = functools.partial(pairs, place=place, local=local, count=count, table=table, own=own, power=power)
    blocks = tuple((half, 0, other, other, half * size) for half in range(2) for other in range(2))
    total = calc(blocks, partner=near, total=None, last=False)[0]
    blocks = tuple((*where, 0, number, 0) for number, where in enumerate(beside))
    total = calc(blocks, partner=got, total=total, last=False)[0]
    blocks = tuple((*where, 1, 0, number * size) for number, where in enumerate(beside))
    total = calc(blocks, partner=[swapped], total=total, last=False)[0]
    blocks = tuple((half, 2, other, half * 2 + other, 0) for half in range(2) for other in range(2))
    total, stack = calc(blocks, partner=far, total=total, last=True)

    stack = lax.all_to_all(stack, "sta", split_axis=0, concat_axis=0, tiled=True)
    stack = jnp.sum(stack.reshape(groups, LAGS // groups, -1), axis=0).T
    station_coef = total.astype(jnp.bfloat16).reshape(1, tiles, SLOTS, stations, LAGS)
    return (station_coef, stack.reshape(1, tiles, SLOTS, LAGS // groups))


def solution(mesh):
    placed = (
        P("tile", None, "sta", None),
        P("tile", "sta"),
        P("tile", None, None),
        P("tile", None, None),
        P("tile", None),
    )
    return jax.shard_map(
        on_device,
        mesh=mesh,
        in_specs=placed,
        out_specs=(P("tile", None, None, "sta", None), P("tile", None, None, "sta")),
        check_vma=False,
    )
```

```python
import functools
import math

import jax
import jax.numpy as jnp
import ml_dtypes
import numpy as np
from jax import lax
from jax.experimental import pallas as pl
from jax.experimental.pallas import tpu as pltpu
from jax.sharding import PartitionSpec as P

BAND = 256
LAGS = 128
SLOTS = 8
SIDE = 4
LANES = 128
ROWS = 48
BLOCK_BITS = 4
EVENT_BLOCK = 1 << BLOCK_BITS
BLOCK_ROWS = EVENT_BLOCK * ROWS + 32
SCALE_WIDTH = 1024.0
VMEM = pl.BlockSpec(memory_space=pltpu.VMEM)
ANY = pl.BlockSpec(memory_space=pl.ANY)
SMEM = pl.BlockSpec(memory_space=pltpu.SMEM)
PARAMS = pltpu.CompilerParams(vmem_limit_bytes=24 * 1024 * 1024)


def forward_table(width):
    phase = np.arange(width)[:, None] * np.arange(1, BAND + 1)[None, :] % width * (2.0 * math.pi / width)
    return np.concatenate([np.cos(phase), -np.sin(phase)], 1).astype(ml_dtypes.bfloat16)


def lag_table(width):
    phase = np.arange(1, BAND + 1)[:, None] * (np.arange(LAGS)[None, :] - LAGS // 2) % width
    phase = phase * (2.0 * math.pi / width)
    table = np.concatenate([np.cos(phase), -np.sin(phase)], 0).astype(ml_dtypes.bfloat16)
    low_re, high_re, low_im, high_im = (table[i * LANES : (i + 1) * LANES] for i in range(4))
    return np.concatenate(
        [np.concatenate([low_re, high_re], 1), np.concatenate([low_im, high_im], 1)], 0
    )


def spectra_kernel(waves_ref, mask_ref, table_ref, mine_ref, other_ref, *refs):
    outs, (came_ref, factors_ref, sems) = refs[:2], refs[2:]
    rows = EVENT_BLOCK * 24
    blocks = waves_ref.shape[0] // rows
    copies = [pltpu.make_async_copy(table_ref, factors_ref, sems.at[blocks])]
    copies += [
        pltpu.make_async_copy(waves_ref.at[pl.ds(i * rows, rows), :], came_ref.at[i], sems.at[i])
        for i in range(blocks)
    ]
    for copy in copies:
        copy.start()
    same = lax.broadcasted_iota(jnp.int32, (1, 8, 8), 1) == lax.broadcasted_iota(jnp.int32, (1, 8, 8), 2)
    mine, other = mine_ref[0], other_ref[0]
    blank = jnp.zeros((mine.shape[0], LANES - 2 * SLOTS), mine.dtype)
    asked = jnp.concatenate([mine, other, blank], 1).astype(jnp.float32).astype(jnp.bfloat16)
    copies[0].wait()
    low = lax.broadcasted_iota(jnp.int32, (EVENT_BLOCK * 3, 8, LANES), 1) < 4
    for block in range(blocks):
        mask = mask_ref[block * EVENT_BLOCK : (block + 1) * EVENT_BLOCK, :].astype(jnp.float32)
        mask = jnp.sum(jnp.where(same, mask[:, None, :], 0.0), axis=-1, keepdims=True)[:, None]
        copies[block + 1].wait()
        flat = jnp.dot(came_ref[block], factors_ref[...], preferred_element_type=jnp.float32)
        flat = flat.reshape(EVENT_BLOCK, 3, 8, 4 * LANES) * mask
        part = [
            flat[..., i * LANES : (i + 1) * LANES].reshape(EVENT_BLOCK * 3, 8, LANES)
            for i in range(4)
        ]
        turned = [pltpu.roll(value, 4, 1) for value in part]
        halves = (
            (jnp.where(low, part[0], turned[1]), jnp.where(low, part[2], turned[3])),
            (jnp.where(low, turned[0], part[1]), jnp.where(low, turned[2], part[3])),
        )
        first, last = block * BLOCK_ROWS, block * BLOCK_ROWS + EVENT_BLOCK * ROWS
        for (real, imag), out_ref in zip(halves, outs):
            packed = jnp.concatenate([real, imag], 1).astype(jnp.bfloat16)
            out_ref[first:last, :] = packed.reshape(EVENT_BLOCK * ROWS, LANES)
            out_ref[last : first + BLOCK_ROWS, :] = asked


def own_spectra(waves, mask, table, mine, other):
    flat = waves.reshape(-1, waves.shape[-1])
    blocks = mask.shape[0] // EVENT_BLOCK
    half = jax.ShapeDtypeStruct((blocks * BLOCK_ROWS, LANES), jnp.bfloat16)
    return pl.pallas_call(
        spectra_kernel,
        in_specs=[ANY, VMEM, ANY, VMEM, VMEM],
        out_specs=[VMEM] * 2,
        out_shape=[half, half],
        scratch_shapes=[
            pltpu.VMEM((blocks, flat.shape[0] // blocks, flat.shape[1]), flat.dtype),
            pltpu.VMEM(table.shape, table.dtype),
            pltpu.SemaphoreType.DMA((blocks + 1,)),
        ],
        compiler_params=PARAMS,
        name="spectra",
    )(flat, mask, table, mine, other)


def power_kernel(first_ref, second_ref, *outs):
    for spectra_ref, out_ref in zip((first_ref, second_ref), outs):
        for block in range(out_ref.shape[0] // EVENT_BLOCK):
            start = block * BLOCK_ROWS
            values = spectra_ref[start : start + EVENT_BLOCK * ROWS, :].astype(jnp.float32)
            values = values.reshape(EVENT_BLOCK, 3, 2, 8, LANES)
            total = jnp.sum(jnp.sum(values * values, axis=(1, 2)), axis=-1, keepdims=True)
            total = jnp.broadcast_to(total, (EVENT_BLOCK, 8, LANES))
            total = (total + pltpu.roll(total, 4, 1)) * (2.0 / SCALE_WIDTH)
            out_ref[block * EVENT_BLOCK : (block + 1) * EVENT_BLOCK] = total


def own_power(own):
    events = own[0].shape[0] // BLOCK_ROWS * EVENT_BLOCK
    return pl.pallas_call(
        power_kernel,
        in_specs=[VMEM] * 2,
        out_specs=[VMEM] * 2,
        out_shape=[jax.ShapeDtypeStruct((events, 8, LANES), jnp.float32)] * 2,
        compiler_params=PARAMS,
        name="power",
    )(*own)


def split(values):
    rows = values[0].shape[0]
    part = lambda i: pl.BlockSpec((rows // 2, LANES), lambda _: (2 * i // len(values), 0))
    whole = pl.BlockSpec((rows // 2, LANES), lambda _: (0, 0))

    def kernel(*refs):
        for in_ref, out_ref in zip(refs[: len(values)], refs[len(values) :]):
            out_ref[...] = in_ref[...]

    return pl.pallas_call(
        kernel,
        grid=(1,),
        in_specs=[part(i) for i in range(len(values))],
        out_specs=[whole] * len(values),
        out_shape=[jax.ShapeDtypeStruct((rows // 2, LANES), values[0].dtype)] * len(values),
        compiler_params=PARAMS,
        name="split",
    )(*values)


def event_rows(event):
    start = event * ROWS + (event >> BLOCK_BITS) * (BLOCK_ROWS - EVENT_BLOCK * ROWS)
    return pl.ds(pl.multiple_of(start, 16), ROWS)


def tile_of(y, x, core):
    return (lax.rem(y + SIDE, SIDE) * SIDE + lax.rem(x + SIDE, SIDE)) * 2 + core


def pack_kernel(plan, asks, halves, later, place_ref, *refs):
    sources, refs = refs[: len(asks)], refs[len(asks) :]
    held, outs = refs[: 5 * len(halves)], refs[5 * len(halves) + later : -8]
    near_ref, full_ref, words_ref, chosen_ref, asked_ref, in_sems, out_sems, sem = refs[-8:]
    y, x, core = place_ref[0], place_ref[1], place_ref[2]
    tiles, size = near_ref.shape[1], full_ref.shape[2]
    asking = [
        pltpu.make_async_copy(
            source.at[pl.ds(EVENT_BLOCK * ROWS, tiles), :], near_ref.at[i], in_sems.at[i]
        )
        for i, source in enumerate(sources)
    ]
    coming = []
    for i in range(len(halves)):
        steps = ((0, 0, size), (1, 0, size), (3, 0, size), (2, 0, size // 2), (2, size // 2, size // 2))
        for number, (step, start, length) in enumerate(steps):
            target = full_ref.at[i, step, pl.ds(start, length), :]
            which = 5 * i + number
            coming.append(pltpu.make_async_copy(held[which], target, in_sems.at[len(asks) + which]))
    for copy in asking + coming:
        copy.start()
    for i, ((half, _), copy) in enumerate(zip(asks, asking)):
        copy.wait()
        event = near_ref[i].astype(jnp.float32).astype(jnp.int32)
        words_ref[i] = event * ROWS + (event >> BLOCK_BITS) * (BLOCK_ROWS - EVENT_BLOCK * ROWS)
        for step in range(SIDE):
            back = step * (1 - 2 * core)
            tile = tile_of(y, x - back, core) if half == 0 else tile_of(y - back, x, core)
            at = i * SIDE + step
            chosen_ref[at : at + 1, :] = words_ref[i, pl.ds(tile, 1), :]
    copy = pltpu.make_async_copy(chosen_ref, asked_ref, sem)
    copy.start()
    copy.wait()
    going = []
    for i, (out_ref, blocks) in enumerate(zip(outs[: len(plan)], plan)):
        packed_ref = outs[len(plan) + i]
        for place, (half, hops, other) in enumerate(blocks):
            which, first = asks.index((half, hops)), halves.index(half)
            while len(coming) > 5 * (len(halves) - 1 - first):
                coming.pop(0).wait()
            for step in range(SIDE):
                for slot in range(SLOTS):
                    row = (place * SIDE + step) * SLOTS + slot
                    start = asked_ref[which * SIDE + step, other * SLOTS + slot]
                    packed_ref[row] = full_ref[first, step, pl.ds(pl.multiple_of(start, 16), ROWS), :]
        going.append(pltpu.make_async_copy(packed_ref, out_ref, out_sems.at[i]))
        going[i].start()
    for copy in going:
        copy.wait()


def pack(plan, place, held, after=()):
    asks = tuple(sorted({block[:2] for blocks in plan for block in blocks}))
    halves = tuple(sorted({half for half, _ in asks}))
    sources = [held[1 - half][{0: 0, 1: 2, 2: 3, 3: 1}[hops]] for half, hops in asks]
    pieces = [piece for half in halves for piece in held[half]]
    shape = lambda blocks: (len(blocks) * SIDE * SLOTS, ROWS, LANES)
    tiles = BLOCK_ROWS - EVENT_BLOCK * ROWS
    chosen = ((len(asks) * SIDE + 7) // 8 * 8, LANES)
    return pl.pallas_call(
        functools.partial(pack_kernel, plan, asks, halves, len(after)),
        in_specs=[SMEM] + [ANY] * (len(asks) + len(pieces) + len(after)),
        out_specs=[ANY] * len(plan),
        out_shape=[jax.ShapeDtypeStruct(shape(blocks), jnp.bfloat16) for blocks in plan],
        scratch_shapes=[pltpu.VMEM(shape(blocks), jnp.bfloat16) for blocks in plan]
        + [
            pltpu.VMEM((len(asks), tiles, LANES), jnp.bfloat16),
            pltpu.VMEM((len(halves), SIDE) + pieces[0].shape, jnp.bfloat16),
            pltpu.VMEM((len(asks), tiles, LANES), jnp.int32),
            pltpu.VMEM(chosen, jnp.int32),
            pltpu.SMEM(chosen, jnp.int32),
            pltpu.SemaphoreType.DMA((len(asks) + len(pieces),)),
            pltpu.SemaphoreType.DMA((len(plan),)),
            pltpu.SemaphoreType.DMA,
        ],
        compiler_params=PARAMS,
        name="pack",
    )(place, *sources, *pieces, *after)


def join_kernel(*refs):
    *parts, more_ref, out_ref = refs
    size = parts[0].shape[0] // 2
    for i, part in enumerate(parts):
        out_ref[i * size : (i + 1) * size] = part[size:]
    out_ref[len(parts) * size :] = more_ref[...]


def join(parts, more):
    length = parts[0].shape[0] // 2 * len(parts) + more.shape[0]
    return pl.pallas_call(
        join_kernel,
        in_specs=[VMEM] * (len(parts) + 1),
        out_specs=VMEM,
        out_shape=jax.ShapeDtypeStruct((length,) + more.shape[1:], more.dtype),
        compiler_params=PARAMS,
        name="join",
    )(*parts, more)


def pair_kernel(blocks, arrays, first, last, place_ref, local_ref, count_ref, table_ref, *refs):
    own, power = refs[:2], refs[2:4]
    partner = refs[4 : 4 + arrays]
    refs = refs[4 + arrays :]
    if not first:
        before_ref, refs = refs[0], refs[1:]
    out_ref, refs = refs[0], refs[1:]
    if last:
        turned_ref, refs = refs[0], refs[1:]
    cross_ref, energy_ref, factor_ref, came_ref, sems = refs
    y, x, core = place_ref[0], place_ref[1], place_ref[2]
    rows = SIDE * SLOTS
    copies = [
        pltpu.make_async_copy(partner[array].at[pl.ds(offset, rows)], came_ref.at[i], sems.at[i])
        for i, (*_, array, offset) in enumerate(blocks)
    ]
    for copy in copies:
        copy.start()
    if not first:
        out_ref[...] = before_ref[...]
    for number, (half, shift, other, *_) in enumerate(blocks):
        copies[number].wait()
        from_core = lax.rem(core + other, 2)

        def tile_at(step):
            way = 1 - 2 * from_core
            if half == 0:
                return tile_of(y - way * shift, x - way * step, from_core)
            return tile_of(y - way * step, x - way * shift, from_core)

        def one_tile(step, carry):
            tile = tile_at(step)
            live = count_ref[tile]
            for slot in range(SLOTS):
                event = local_ref[tile * SLOTS + slot]
                mine = own[half][event_rows(event), :].astype(jnp.float32)
                mine = mine.reshape(3, 2, 8, LANES)
                row = step * SLOTS + slot
                theirs = came_ref[number, row].astype(jnp.float32).reshape(3, 2, 8, LANES)
                real = jnp.sum(mine * theirs, axis=(0, 1))
                imag = jnp.sum(mine[:, 1] * theirs[:, 0] - mine[:, 0] * theirs[:, 1], axis=0)
                cross = jnp.concatenate([real, imag], -1)
                cross_ref[pl.ds(pl.multiple_of(row * 8, 8), 8), :] = cross
                energy_ref[row] = jnp.sum(theirs * theirs, axis=(0, 1))
                alive = jnp.where(slot < live, jnp.float32(2.0 / SCALE_WIDTH), jnp.float32(0))
                factor_ref[0, row] = power[half][event]
                factor_ref[1, row] = jnp.full((8, LANES), alive, jnp.float32)
            return carry

        lax.fori_loop(0, SIDE, one_tile, 0)
        corr = jnp.dot(
            cross_ref[...].astype(jnp.bfloat16), table_ref[...], preferred_element_type=jnp.float32
        ).reshape(rows, 8, 2 * LANES)
        low = lax.broadcasted_iota(jnp.int32, (rows, 8, LANES), 1) < 4
        corr = jnp.where(low, corr[..., :LANES], corr[..., LANES:])
        corr = corr + pltpu.roll(corr, 4, 1)
        energy = jnp.broadcast_to(
            jnp.sum(energy_ref[...], axis=-1, keepdims=True), (rows, 8, LANES)
        )
        energy = (energy + pltpu.roll(energy, 4, 1)) * (2.0 / SCALE_WIDTH)
        corr = corr * (lax.rsqrt(factor_ref[0] * energy + 1e-06) * factor_ref[1])
        for step in range(SIDE):
            at = pl.ds(pl.multiple_of(tile_at(jnp.int32(step)) * SLOTS, SLOTS), SLOTS)
            out_ref[at, 4 * half : 4 * half + 4, :] = corr[
                step * SLOTS : (step + 1) * SLOTS, 4 * half : 4 * half + 4
            ]
    if last:
        turned_ref[...] = jnp.sum(out_ref[...], axis=1).T


def pairs(blocks, place, local, count, table, own, power, partner, total, last):
    rows, slots = SIDE * SLOTS, local.shape[0]
    first = total is None
    out_shape = [jax.ShapeDtypeStruct((slots, 8, LAGS), jnp.float32)]
    if last:
        out_shape += [jax.ShapeDtypeStruct((LAGS, slots), jnp.float32)]
    args = [place, local, count, table, *own, *power, *partner] + ([] if first else [total])
    return pl.pallas_call(
        functools.partial(pair_kernel, blocks, len(partner), first, last),
        in_specs=[SMEM] * 3 + [VMEM] * 5 + [ANY] * len(partner) + [VMEM] * (not first),
        out_specs=[VMEM] * len(out_shape),
        out_shape=out_shape,
        scratch_shapes=[
            pltpu.VMEM((rows * 8, 2 * LANES), jnp.float32),
            pltpu.VMEM((rows, 8, LANES), jnp.float32),
            pltpu.VMEM((2, rows, 8, LANES), jnp.float32),
            pltpu.VMEM((len(blocks), rows, ROWS, LANES), jnp.bfloat16),
            pltpu.SemaphoreType.DMA((len(blocks),)),
        ],
        compiler_params=PARAMS,
        name="pairs",
    )(*args)


def hop(value, dy, dx, dcore):
    moves = []
    for y in range(SIDE):
        for x in range(SIDE):
            for core in range(2):
                way = 1 - 2 * core
                target = ((y + way * dy) % SIDE * SIDE + (x + way * dx) % SIDE) * 2 + (core + dcore) % 2
                moves.append(((y * SIDE + x) * 2 + core, target))
    return lax.ppermute(value, "tile", moves)


def on_device(waves, station_mask, pair_local, pair_remote, pair_count):
    width, tiles = waves.shape[-1], pair_remote.shape[1]
    events, stations = station_mask.shape
    groups = lax.axis_size("sta")
    here = lax.axis_index("tile")
    place = jnp.stack([here // (2 * SIDE), here // 2 % SIDE, here % 2]).astype(jnp.int32)
    local, count = pair_local.reshape(-1), pair_count.reshape(-1)

    other = hop(pair_remote, 0, 0, 1)
    own = own_spectra(waves, station_mask, jnp.asarray(forward_table(width)), pair_remote, other)
    power = own_power(own)

    along = lambda half, value, hops: hop(value, *((0, hops) if half == 0 else (hops, 0)), 0)
    rings = [(half, hops) for hops in (1, SIDE - 1) for half in range(2)]
    came = [along(half, own[half], hops) for half, hops in rings]
    passed = [along(half, value, hops) for (half, hops), value in zip(rings, split(came))]
    held = [[own[half], *came[half::2], *passed[half::2]] for half in range(2)]
    across = lambda half, value, hops, other: hop(value, *((hops, 0) if half == 0 else (0, hops)), other)

    packed = pack(tuple(((*where, 0), (*where, 1)) for where in rings), place, held)
    got = [across(where[0], value, where[1], 0) for value, where in zip(packed, rings)]
    distant = [(half, 2, other) for other in range(2) for half in range(2)]
    rest = pack(
        tuple((where,) for where in distant)
        + (((0, 0, 0), (1, 0, 0)), ((0, 0, 1), (1, 0, 1))),
        place,
        held,
        packed[:1],
    )
    far = [across(where[0], value, *where[1:]) for value, where in zip(rest, distant)]
    size = SIDE * SLOTS
    swapped = hop(join(got, rest[5]), 0, 0, 1)

    table = jnp.asarray(lag_table(width))
    calc = functools.partial(pairs, place=place, local=local, count=count, table=table, own=own, power=power)
    near = [(half, 0) for half in range(2)]
    blocks = tuple((half, 0, 0, 4, half * size) for half in range(2))
    blocks += tuple((*where, 0, number, 0) for number, where in enumerate(rings))
    total = calc(blocks, partner=got + [rest[4]], total=None, last=False)[0]
    blocks = tuple((*where, 1, 0, number * size) for number, where in enumerate(rings + near))
    total = calc(blocks, partner=[swapped], total=total, last=False)[0]
    blocks = tuple((*where, number, 0) for number, where in enumerate(distant))
    total, stack = calc(blocks, partner=far, total=total, last=True)

    stack = lax.all_to_all(stack, "sta", split_axis=0, concat_axis=0, tiled=True)
    stack = jnp.sum(stack.reshape(groups, LAGS // groups, -1), axis=0).T
    station_coef = total.astype(jnp.bfloat16).reshape(1, tiles, SLOTS, stations, LAGS)
    return (station_coef, stack.reshape(1, tiles, SLOTS, LAGS // groups))


def solution(mesh):
    placed = (
        P("tile", None, "sta", None),
        P("tile", "sta"),
        P("tile", None, None),
        P("tile", None, None),
        P("tile", None),
    )
    return jax.shard_map(
        on_device,
        mesh=mesh,
        in_specs=placed,
        out_specs=(P("tile", None, None, "sta", None), P("tile", None, None, "sta")),
        check_vma=False,
    )
```

```python
import functools
import math

import jax
import jax.numpy as jnp
import ml_dtypes
import numpy as np
from jax import lax
from jax.experimental import pallas as pl
from jax.experimental.pallas import tpu as pltpu
from jax.sharding import PartitionSpec as P

BAND = 256
LAGS = 128
SLOTS = 8
SIDE = 4
LANES = 128
ROWS = 48
BLOCK_BITS = 4
EVENT_BLOCK = 1 << BLOCK_BITS
BLOCK_ROWS = EVENT_BLOCK * ROWS + 32
SCALE_WIDTH = 1024.0
VMEM = pl.BlockSpec(memory_space=pltpu.VMEM)
ANY = pl.BlockSpec(memory_space=pl.ANY)
SMEM = pl.BlockSpec(memory_space=pltpu.SMEM)
PARAMS = pltpu.CompilerParams(vmem_limit_bytes=16 * 1024 * 1024)
WHOLE = pltpu.CompilerParams(vmem_limit_bytes=60 * 1024 * 1024)


def forward_table(width):
    phase = np.arange(width)[:, None] * np.arange(1, BAND + 1)[None, :] % width * (2.0 * math.pi / width)
    return np.concatenate([np.cos(phase), -np.sin(phase)], 1).astype(ml_dtypes.bfloat16)


def lag_table(width):
    phase = np.arange(1, BAND + 1)[:, None] * (np.arange(LAGS)[None, :] - LAGS // 2) % width
    phase = phase * (2.0 * math.pi / width)
    table = np.concatenate([np.cos(phase), -np.sin(phase)], 0).astype(ml_dtypes.bfloat16)
    low_re, high_re, low_im, high_im = (table[i * LANES : (i + 1) * LANES] for i in range(4))
    return np.concatenate(
        [np.concatenate([low_re, high_re], 1), np.concatenate([low_im, high_im], 1)], 0
    )


def spectra_kernel(waves_ref, mask_ref, table_ref, mine_ref, other_ref, *refs):
    outs, (came_ref, factors_ref, sems) = refs[:2], refs[2:]
    rows = EVENT_BLOCK * 24
    blocks = waves_ref.shape[0] // rows
    copies = [pltpu.make_async_copy(table_ref, factors_ref, sems.at[blocks])]
    copies += [
        pltpu.make_async_copy(waves_ref.at[pl.ds(i * rows, rows), :], came_ref.at[i], sems.at[i])
        for i in range(blocks)
    ]
    for copy in copies:
        copy.start()
    same = lax.broadcasted_iota(jnp.int32, (1, 8, 8), 1) == lax.broadcasted_iota(jnp.int32, (1, 8, 8), 2)
    mine, other = mine_ref[0], other_ref[0]
    blank = jnp.zeros((mine.shape[0], LANES - 2 * SLOTS), mine.dtype)
    asked = jnp.concatenate([mine, other, blank], 1).astype(jnp.float32).astype(jnp.bfloat16)
    copies[0].wait()
    low = lax.broadcasted_iota(jnp.int32, (EVENT_BLOCK * 3, 8, LANES), 1) < 4
    for block in range(blocks):
        mask = mask_ref[block * EVENT_BLOCK : (block + 1) * EVENT_BLOCK, :].astype(jnp.float32)
        mask = jnp.sum(jnp.where(same, mask[:, None, :], 0.0), axis=-1, keepdims=True)[:, None]
        copies[block + 1].wait()
        flat = jnp.dot(came_ref[block], factors_ref[...], preferred_element_type=jnp.float32)
        flat = flat.reshape(EVENT_BLOCK, 3, 8, 4 * LANES) * mask
        part = [
            flat[..., i * LANES : (i + 1) * LANES].reshape(EVENT_BLOCK * 3, 8, LANES)
            for i in range(4)
        ]
        turned = [pltpu.roll(value, 4, 1) for value in part]
        halves = (
            (jnp.where(low, part[0], turned[1]), jnp.where(low, part[2], turned[3])),
            (jnp.where(low, turned[0], part[1]), jnp.where(low, turned[2], part[3])),
        )
        first, last = block * BLOCK_ROWS, block * BLOCK_ROWS + EVENT_BLOCK * ROWS
        for (real, imag), out_ref in zip(halves, outs):
            packed = jnp.concatenate([real, imag], 1).astype(jnp.bfloat16)
            out_ref[first:last, :] = packed.reshape(EVENT_BLOCK * ROWS, LANES)
            out_ref[last : first + BLOCK_ROWS, :] = asked


def own_spectra(waves, mask, table, mine, other):
    flat = waves.reshape(-1, waves.shape[-1])
    blocks = mask.shape[0] // EVENT_BLOCK
    half = jax.ShapeDtypeStruct((blocks * BLOCK_ROWS, LANES), jnp.bfloat16)
    return pl.pallas_call(
        spectra_kernel,
        in_specs=[ANY, VMEM, ANY, VMEM, VMEM],
        out_specs=[VMEM] * 2,
        out_shape=[half, half],
        scratch_shapes=[
            pltpu.VMEM((blocks, flat.shape[0] // blocks, flat.shape[1]), flat.dtype),
            pltpu.VMEM(table.shape, table.dtype),
            pltpu.SemaphoreType.DMA((blocks + 1,)),
        ],
        compiler_params=WHOLE,
        name="spectra",
    )(flat, mask, table, mine, other)


def power_kernel(first_ref, second_ref, *outs):
    for spectra_ref, out_ref in zip((first_ref, second_ref), outs):
        for block in range(out_ref.shape[0] // EVENT_BLOCK):
            start = block * BLOCK_ROWS
            values = spectra_ref[start : start + EVENT_BLOCK * ROWS, :].astype(jnp.float32)
            values = values.reshape(EVENT_BLOCK, 3, 2, 8, LANES)
            total = jnp.sum(jnp.sum(values * values, axis=(1, 2)), axis=-1, keepdims=True)
            total = jnp.broadcast_to(total, (EVENT_BLOCK, 8, LANES))
            total = (total + pltpu.roll(total, 4, 1)) * (2.0 / SCALE_WIDTH)
            out_ref[block * EVENT_BLOCK : (block + 1) * EVENT_BLOCK] = total


def own_power(own):
    events = own[0].shape[0] // BLOCK_ROWS * EVENT_BLOCK
    return pl.pallas_call(
        power_kernel,
        in_specs=[VMEM] * 2,
        out_specs=[VMEM] * 2,
        out_shape=[jax.ShapeDtypeStruct((events, 8, LANES), jnp.float32)] * 2,
        compiler_params=PARAMS,
        name="power",
    )(*own)


def split(values):
    rows = values[0].shape[0]
    part = lambda i: pl.BlockSpec((rows // 2, LANES), lambda _: (2 * i // len(values), 0))
    whole = pl.BlockSpec((rows // 2, LANES), lambda _: (0, 0))

    def kernel(*refs):
        for in_ref, out_ref in zip(refs[: len(values)], refs[len(values) :]):
            out_ref[...] = in_ref[...]

    return pl.pallas_call(
        kernel,
        grid=(1,),
        in_specs=[part(i) for i in range(len(values))],
        out_specs=[whole] * len(values),
        out_shape=[jax.ShapeDtypeStruct((rows // 2, LANES), values[0].dtype)] * len(values),
        compiler_params=PARAMS,
        name="split",
    )(*values)


def event_rows(event):
    start = event * ROWS + (event >> BLOCK_BITS) * (BLOCK_ROWS - EVENT_BLOCK * ROWS)
    return pl.ds(pl.multiple_of(start, 16), ROWS)


def tile_of(y, x, core):
    return (lax.rem(y + SIDE, SIDE) * SIDE + lax.rem(x + SIDE, SIDE)) * 2 + core


def pack_kernel(plan, asks, halves, later, place_ref, *refs):
    sources, refs = refs[: len(asks)], refs[len(asks) :]
    held, outs = refs[: 5 * len(halves)], refs[5 * len(halves) + later : -8]
    near_ref, full_ref, words_ref, chosen_ref, asked_ref, in_sems, out_sems, sem = refs[-8:]
    y, x, core = place_ref[0], place_ref[1], place_ref[2]
    tiles, size = near_ref.shape[1], full_ref.shape[2]
    asking = [
        pltpu.make_async_copy(
            source.at[pl.ds(EVENT_BLOCK * ROWS, tiles), :], near_ref.at[i], in_sems.at[i]
        )
        for i, source in enumerate(sources)
    ]
    coming = []
    for i in range(len(halves)):
        steps = ((0, 0, size), (1, 0, size), (3, 0, size), (2, 0, size // 2), (2, size // 2, size // 2))
        for number, (step, start, length) in enumerate(steps):
            target = full_ref.at[i, step, pl.ds(start, length), :]
            which = 5 * i + number
            coming.append(pltpu.make_async_copy(held[which], target, in_sems.at[len(asks) + which]))
    for copy in asking + coming:
        copy.start()
    for i, ((half, _), copy) in enumerate(zip(asks, asking)):
        copy.wait()
        event = near_ref[i].astype(jnp.float32).astype(jnp.int32)
        words_ref[i] = event * ROWS + (event >> BLOCK_BITS) * (BLOCK_ROWS - EVENT_BLOCK * ROWS)
        for step in range(SIDE):
            back = step * (1 - 2 * core)
            tile = tile_of(y, x - back, core) if half == 0 else tile_of(y - back, x, core)
            at = i * SIDE + step
            chosen_ref[at : at + 1, :] = words_ref[i, pl.ds(tile, 1), :]
    copy = pltpu.make_async_copy(chosen_ref, asked_ref, sem)
    copy.start()
    copy.wait()
    going = []
    for i, (out_ref, blocks) in enumerate(zip(outs[: len(plan)], plan)):
        packed_ref = outs[len(plan) + i]
        for place, (half, hops, other) in enumerate(blocks):
            which, first = asks.index((half, hops)), halves.index(half)
            while len(coming) > 5 * (len(halves) - 1 - first):
                coming.pop(0).wait()
            for step in range(SIDE):
                for slot in range(SLOTS):
                    row = (place * SIDE + step) * SLOTS + slot
                    start = asked_ref[which * SIDE + step, other * SLOTS + slot]
                    packed_ref[row] = full_ref[first, step, pl.ds(pl.multiple_of(start, 16), ROWS), :]
        going.append(pltpu.make_async_copy(packed_ref, out_ref, out_sems.at[i]))
        going[i].start()
    for copy in going:
        copy.wait()


def pack(plan, place, held, after=()):
    asks = tuple(sorted({block[:2] for blocks in plan for block in blocks}))
    halves = tuple(sorted({half for half, _ in asks}))
    sources = [held[1 - half][{0: 0, 1: 2, 2: 3, 3: 1}[hops]] for half, hops in asks]
    pieces = [piece for half in halves for piece in held[half]]
    shape = lambda blocks: (len(blocks) * SIDE * SLOTS, ROWS, LANES)
    tiles = BLOCK_ROWS - EVENT_BLOCK * ROWS
    chosen = ((len(asks) * SIDE + 7) // 8 * 8, LANES)
    return pl.pallas_call(
        functools.partial(pack_kernel, plan, asks, halves, len(after)),
        in_specs=[SMEM] + [ANY] * (len(asks) + len(pieces) + len(after)),
        out_specs=[ANY] * len(plan),
        out_shape=[jax.ShapeDtypeStruct(shape(blocks), jnp.bfloat16) for blocks in plan],
        scratch_shapes=[pltpu.VMEM(shape(blocks), jnp.bfloat16) for blocks in plan]
        + [
            pltpu.VMEM((len(asks), tiles, LANES), jnp.bfloat16),
            pltpu.VMEM((len(halves), SIDE) + pieces[0].shape, jnp.bfloat16),
            pltpu.VMEM((len(asks), tiles, LANES), jnp.int32),
            pltpu.VMEM(chosen, jnp.int32),
            pltpu.SMEM(chosen, jnp.int32),
            pltpu.SemaphoreType.DMA((len(asks) + len(pieces),)),
            pltpu.SemaphoreType.DMA((len(plan),)),
            pltpu.SemaphoreType.DMA,
        ],
        compiler_params=WHOLE,
        name="pack",
    )(place, *sources, *pieces, *after)


def join_kernel(*refs):
    *parts, more_ref, out_ref = refs
    size = parts[0].shape[0] // 2
    for i, part in enumerate(parts):
        out_ref[i * size : (i + 1) * size] = part[size:]
    out_ref[len(parts) * size :] = more_ref[...]


def join(parts, more):
    length = parts[0].shape[0] // 2 * len(parts) + more.shape[0]
    return pl.pallas_call(
        join_kernel,
        in_specs=[VMEM] * (len(parts) + 1),
        out_specs=VMEM,
        out_shape=jax.ShapeDtypeStruct((length,) + more.shape[1:], more.dtype),
        compiler_params=PARAMS,
        name="join",
    )(*parts, more)


def pair_kernel(blocks, arrays, first, last, place_ref, local_ref, count_ref, table_ref, *refs):
    own, power = refs[:2], refs[2:4]
    partner = refs[4 : 4 + arrays]
    refs = refs[4 + arrays :]
    if not first:
        before_ref, refs = refs[0], refs[1:]
    out_ref, refs = refs[0], refs[1:]
    if last:
        turned_ref, refs = refs[0], refs[1:]
    cross_ref, energy_ref, factor_ref, came_ref, sems = refs
    y, x, core = place_ref[0], place_ref[1], place_ref[2]
    rows = SIDE * SLOTS
    copies = [
        pltpu.make_async_copy(partner[array].at[pl.ds(offset, rows)], came_ref.at[i], sems.at[i])
        for i, (*_, array, offset) in enumerate(blocks)
    ]
    for copy in copies:
        copy.start()
    if not first:
        out_ref[...] = before_ref[...]
    for number, (half, shift, other, *_) in enumerate(blocks):
        copies[number].wait()
        from_core = lax.rem(core + other, 2)

        def tile_at(step):
            way = 1 - 2 * from_core
            if half == 0:
                return tile_of(y - way * shift, x - way * step, from_core)
            return tile_of(y - way * step, x - way * shift, from_core)

        def one_tile(step, carry):
            tile = tile_at(step)
            live = count_ref[tile]
            for slot in range(SLOTS):
                event = local_ref[tile * SLOTS + slot]
                mine = own[half][event_rows(event), :].astype(jnp.float32)
                mine = mine.reshape(3, 2, 8, LANES)
                row = step * SLOTS + slot
                theirs = came_ref[number, row].astype(jnp.float32).reshape(3, 2, 8, LANES)
                real = jnp.sum(mine * theirs, axis=(0, 1))
                imag = jnp.sum(mine[:, 1] * theirs[:, 0] - mine[:, 0] * theirs[:, 1], axis=0)
                cross = jnp.concatenate([real, imag], -1)
                cross_ref[pl.ds(pl.multiple_of(row * 8, 8), 8), :] = cross
                energy_ref[row] = jnp.sum(theirs * theirs, axis=(0, 1))
                alive = jnp.where(slot < live, jnp.float32(2.0 / SCALE_WIDTH), jnp.float32(0))
                factor_ref[0, row] = power[half][event]
                factor_ref[1, row] = jnp.full((8, LANES), alive, jnp.float32)
            return carry

        lax.fori_loop(0, SIDE, one_tile, 0)
        corr = jnp.dot(
            cross_ref[...].astype(jnp.bfloat16), table_ref[...], preferred_element_type=jnp.float32
        ).reshape(rows, 8, 2 * LANES)
        low = lax.broadcasted_iota(jnp.int32, (rows, 8, LANES), 1) < 4
        corr = jnp.where(low, corr[..., :LANES], corr[..., LANES:])
        corr = corr + pltpu.roll(corr, 4, 1)
        energy = jnp.broadcast_to(
            jnp.sum(energy_ref[...], axis=-1, keepdims=True), (rows, 8, LANES)
        )
        energy = (energy + pltpu.roll(energy, 4, 1)) * (2.0 / SCALE_WIDTH)
        corr = corr * (lax.rsqrt(factor_ref[0] * energy + 1e-06) * factor_ref[1])
        for step in range(SIDE):
            at = pl.ds(pl.multiple_of(tile_at(jnp.int32(step)) * SLOTS, SLOTS), SLOTS)
            out_ref[at, 4 * half : 4 * half + 4, :] = corr[
                step * SLOTS : (step + 1) * SLOTS, 4 * half : 4 * half + 4
            ]
    if last:
        turned_ref[...] = jnp.sum(out_ref[...], axis=1).T


def pairs(blocks, place, local, count, table, own, power, partner, total, last):
    rows, slots = SIDE * SLOTS, local.shape[0]
    first = total is None
    out_shape = [jax.ShapeDtypeStruct((slots, 8, LAGS), jnp.float32)]
    if last:
        out_shape += [jax.ShapeDtypeStruct((LAGS, slots), jnp.float32)]
    args = [place, local, count, table, *own, *power, *partner] + ([] if first else [total])
    return pl.pallas_call(
        functools.partial(pair_kernel, blocks, len(partner), first, last),
        in_specs=[SMEM] * 3 + [VMEM] * 5 + [ANY] * len(partner) + [VMEM] * (not first),
        out_specs=[VMEM] * len(out_shape),
        out_shape=out_shape,
        scratch_shapes=[
            pltpu.VMEM((rows * 8, 2 * LANES), jnp.float32),
            pltpu.VMEM((rows, 8, LANES), jnp.float32),
            pltpu.VMEM((2, rows, 8, LANES), jnp.float32),
            pltpu.VMEM((len(blocks), rows, ROWS, LANES), jnp.bfloat16),
            pltpu.SemaphoreType.DMA((len(blocks),)),
        ],
        compiler_params=WHOLE,
        name="pairs",
    )(*args)


def hop(value, dy, dx, dcore):
    moves = []
    for y in range(SIDE):
        for x in range(SIDE):
            for core in range(2):
                way = 1 - 2 * core
                target = ((y + way * dy) % SIDE * SIDE + (x + way * dx) % SIDE) * 2 + (core + dcore) % 2
                moves.append(((y * SIDE + x) * 2 + core, target))
    return lax.ppermute(value, "tile", moves)


def on_device(waves, station_mask, pair_local, pair_remote, pair_count):
    width, tiles = waves.shape[-1], pair_remote.shape[1]
    events, stations = station_mask.shape
    groups = lax.axis_size("sta")
    here = lax.axis_index("tile")
    place = jnp.stack([here // (2 * SIDE), here // 2 % SIDE, here % 2]).astype(jnp.int32)
    local, count = pair_local.reshape(-1), pair_count.reshape(-1)

    other = hop(pair_remote, 0, 0, 1)
    own = own_spectra(waves, station_mask, jnp.asarray(forward_table(width)), pair_remote, other)
    power = own_power(own)

    along = lambda half, value, hops: hop(value, *((0, hops) if half == 0 else (hops, 0)), 0)
    rings = [(half, hops) for hops in (1, SIDE - 1) for half in range(2)]
    came = [along(half, own[half], hops) for half, hops in rings]
    passed = [along(half, value, hops) for (half, hops), value in zip(rings, split(came))]
    held = [[own[half], *came[half::2], *passed[half::2]] for half in range(2)]
    across = lambda half, value, hops, other: hop(value, *((hops, 0) if half == 0 else (0, hops)), other)

    packed = pack(tuple(((*where, 0), (*where, 1)) for where in rings), place, held)
    got = [across(where[0], value, where[1], 0) for value, where in zip(packed, rings)]
    distant = [(half, 2, other) for other in range(2) for half in range(2)]
    rest = pack(
        tuple((where,) for where in distant)
        + (((0, 0, 0), (1, 0, 0)), ((0, 0, 1), (1, 0, 1))),
        place,
        held,
        packed[:1],
    )
    far = [across(where[0], value, *where[1:]) for value, where in zip(rest, distant)]
    size = SIDE * SLOTS
    swapped = hop(join(got, rest[5]), 0, 0, 1)

    table = jnp.asarray(lag_table(width))
    calc = functools.partial(pairs, place=place, local=local, count=count, table=table, own=own, power=power)
    near = [(half, 0) for half in range(2)]
    blocks = tuple((half, 0, 0, 4, half * size) for half in range(2))
    blocks += tuple((*where, 0, number, 0) for number, where in enumerate(rings))
    blocks += tuple((*where, 1, 5, number * size) for number, where in enumerate(rings + near))
    total = calc(blocks, partner=got + [rest[4], swapped], total=None, last=False)[0]
    blocks = tuple((*where, number, 0) for number, where in enumerate(distant))
    total, stack = calc(blocks, partner=far, total=total, last=True)

    stack = lax.all_to_all(stack, "sta", split_axis=0, concat_axis=0, tiled=True)
    stack = jnp.sum(stack.reshape(groups, LAGS // groups, -1), axis=0).T
    station_coef = total.astype(jnp.bfloat16).reshape(1, tiles, SLOTS, stations, LAGS)
    return (station_coef, stack.reshape(1, tiles, SLOTS, LAGS // groups))


def solution(mesh):
    placed = (
        P("tile", None, "sta", None),
        P("tile", "sta"),
        P("tile", None, None),
        P("tile", None, None),
        P("tile", None),
    )
    return jax.shard_map(
        on_device,
        mesh=mesh,
        in_specs=placed,
        out_specs=(P("tile", None, None, "sta", None), P("tile", None, None, "sta")),
        check_vma=False,
    )
```

```python
import functools
import math

import jax
import jax.numpy as jnp
import ml_dtypes
import numpy as np
from jax import lax
from jax.experimental import pallas as pl
from jax.experimental.pallas import tpu as pltpu
from jax.sharding import PartitionSpec as P

BAND = 256
LAGS = 128
SLOTS = 8
SIDE = 4
LANES = 128
ROWS = 48
BLOCK_BITS = 4
EVENT_BLOCK = 1 << BLOCK_BITS
BLOCK_ROWS = EVENT_BLOCK * ROWS + 32
SCALE_WIDTH = 1024.0
VMEM = pl.BlockSpec(memory_space=pltpu.VMEM)
ANY = pl.BlockSpec(memory_space=pl.ANY)
SMEM = pl.BlockSpec(memory_space=pltpu.SMEM)
PARAMS = pltpu.CompilerParams(vmem_limit_bytes=24 * 1024 * 1024)
WHOLE = pltpu.CompilerParams(vmem_limit_bytes=60 * 1024 * 1024)


def forward_table(width):
    phase = np.arange(width)[:, None] * np.arange(1, BAND + 1)[None, :] % width * (2.0 * math.pi / width)
    return np.concatenate([np.cos(phase), -np.sin(phase)], 1).astype(ml_dtypes.bfloat16)


def lag_table(width):
    phase = np.arange(1, BAND + 1)[:, None] * (np.arange(LAGS)[None, :] - LAGS // 2) % width
    phase = phase * (2.0 * math.pi / width)
    table = np.concatenate([np.cos(phase), -np.sin(phase)], 0).astype(ml_dtypes.bfloat16)
    low_re, high_re, low_im, high_im = (table[i * LANES : (i + 1) * LANES] for i in range(4))
    return np.concatenate(
        [np.concatenate([low_re, high_re], 1), np.concatenate([low_im, high_im], 1)], 0
    )


def spectra_kernel(waves_ref, mask_ref, table_ref, mine_ref, other_ref, *refs):
    outs, (came_ref, factors_ref, sems) = refs[:2], refs[2:]
    rows = EVENT_BLOCK * 24
    blocks = waves_ref.shape[0] // rows
    copies = [pltpu.make_async_copy(table_ref, factors_ref, sems.at[blocks])]
    copies += [
        pltpu.make_async_copy(waves_ref.at[pl.ds(i * rows, rows), :], came_ref.at[i], sems.at[i])
        for i in range(blocks)
    ]
    for copy in copies:
        copy.start()
    same = lax.broadcasted_iota(jnp.int32, (1, 8, 8), 1) == lax.broadcasted_iota(jnp.int32, (1, 8, 8), 2)
    mine, other = mine_ref[0], other_ref[0]
    blank = jnp.zeros((mine.shape[0], LANES - 2 * SLOTS), mine.dtype)
    asked = jnp.concatenate([mine, other, blank], 1).astype(jnp.float32).astype(jnp.bfloat16)
    copies[0].wait()
    low = lax.broadcasted_iota(jnp.int32, (EVENT_BLOCK * 3, 8, LANES), 1) < 4
    for block in range(blocks):
        mask = mask_ref[block * EVENT_BLOCK : (block + 1) * EVENT_BLOCK, :].astype(jnp.float32)
        mask = jnp.sum(jnp.where(same, mask[:, None, :], 0.0), axis=-1, keepdims=True)[:, None]
        copies[block + 1].wait()
        flat = jnp.dot(came_ref[block], factors_ref[...], preferred_element_type=jnp.float32)
        flat = flat.reshape(EVENT_BLOCK, 3, 8, 4 * LANES) * mask
        part = [
            flat[..., i * LANES : (i + 1) * LANES].reshape(EVENT_BLOCK * 3, 8, LANES)
            for i in range(4)
        ]
        turned = [pltpu.roll(value, 4, 1) for value in part]
        halves = (
            (jnp.where(low, part[0], turned[1]), jnp.where(low, part[2], turned[3])),
            (jnp.where(low, turned[0], part[1]), jnp.where(low, turned[2], part[3])),
        )
        first, last = block * BLOCK_ROWS, block * BLOCK_ROWS + EVENT_BLOCK * ROWS
        for (real, imag), out_ref in zip(halves, outs):
            packed = jnp.concatenate([real, imag], 1).astype(jnp.bfloat16)
            out_ref[first:last, :] = packed.reshape(EVENT_BLOCK * ROWS, LANES)
            out_ref[last : first + BLOCK_ROWS, :] = asked


def own_spectra(waves, mask, table, mine, other):
    flat = waves.reshape(-1, waves.shape[-1])
    blocks = mask.shape[0] // EVENT_BLOCK
    half = jax.ShapeDtypeStruct((blocks * BLOCK_ROWS, LANES), jnp.bfloat16)
    return pl.pallas_call(
        spectra_kernel,
        in_specs=[ANY, VMEM, ANY, VMEM, VMEM],
        out_specs=[VMEM] * 2,
        out_shape=[half, half],
        scratch_shapes=[
            pltpu.VMEM((blocks, flat.shape[0] // blocks, flat.shape[1]), flat.dtype),
            pltpu.VMEM(table.shape, table.dtype),
            pltpu.SemaphoreType.DMA((blocks + 1,)),
        ],
        compiler_params=PARAMS,
        name="spectra",
    )(flat, mask, table, mine, other)


def power_kernel(first_ref, second_ref, *outs):
    for spectra_ref, out_ref in zip((first_ref, second_ref), outs):
        for block in range(out_ref.shape[0] // EVENT_BLOCK):
            start = block * BLOCK_ROWS
            values = spectra_ref[start : start + EVENT_BLOCK * ROWS, :].astype(jnp.float32)
            values = values.reshape(EVENT_BLOCK, 3, 2, 8, LANES)
            total = jnp.sum(jnp.sum(values * values, axis=(1, 2)), axis=-1, keepdims=True)
            total = jnp.broadcast_to(total, (EVENT_BLOCK, 8, LANES))
            total = (total + pltpu.roll(total, 4, 1)) * (2.0 / SCALE_WIDTH)
            out_ref[block * EVENT_BLOCK : (block + 1) * EVENT_BLOCK] = total


def own_power(own):
    events = own[0].shape[0] // BLOCK_ROWS * EVENT_BLOCK
    return pl.pallas_call(
        power_kernel,
        in_specs=[VMEM] * 2,
        out_specs=[VMEM] * 2,
        out_shape=[jax.ShapeDtypeStruct((events, 8, LANES), jnp.float32)] * 2,
        compiler_params=PARAMS,
        name="power",
    )(*own)


def split(values):
    rows = values[0].shape[0]
    part = lambda i: pl.BlockSpec((rows // 2, LANES), lambda _: (2 * i // len(values), 0))
    whole = pl.BlockSpec((rows // 2, LANES), lambda _: (0, 0))

    def kernel(*refs):
        for in_ref, out_ref in zip(refs[: len(values)], refs[len(values) :]):
            out_ref[...] = in_ref[...]

    return pl.pallas_call(
        kernel,
        grid=(1,),
        in_specs=[part(i) for i in range(len(values))],
        out_specs=[whole] * len(values),
        out_shape=[jax.ShapeDtypeStruct((rows // 2, LANES), values[0].dtype)] * len(values),
        compiler_params=PARAMS,
        name="split",
    )(*values)


def event_rows(event):
    start = event * ROWS + (event >> BLOCK_BITS) * (BLOCK_ROWS - EVENT_BLOCK * ROWS)
    return pl.ds(pl.multiple_of(start, 16), ROWS)


def tile_of(y, x, core):
    return (lax.rem(y + SIDE, SIDE) * SIDE + lax.rem(x + SIDE, SIDE)) * 2 + core


def pack_kernel(plan, asks, halves, later, place_ref, *refs):
    sources, refs = refs[: len(asks)], refs[len(asks) :]
    held, outs = refs[: 5 * len(halves)], refs[5 * len(halves) + later : -8]
    near_ref, full_ref, words_ref, chosen_ref, asked_ref, in_sems, out_sems, sem = refs[-8:]
    y, x, core = place_ref[0], place_ref[1], place_ref[2]
    tiles, size = near_ref.shape[1], full_ref.shape[2]
    asking = [
        pltpu.make_async_copy(
            source.at[pl.ds(EVENT_BLOCK * ROWS, tiles), :], near_ref.at[i], in_sems.at[i]
        )
        for i, source in enumerate(sources)
    ]
    coming = []
    for i in range(len(halves)):
        steps = ((0, 0, size), (1, 0, size), (3, 0, size), (2, 0, size // 2), (2, size // 2, size // 2))
        for number, (step, start, length) in enumerate(steps):
            target = full_ref.at[i, step, pl.ds(start, length), :]
            which = 5 * i + number
            coming.append(pltpu.make_async_copy(held[which], target, in_sems.at[len(asks) + which]))
    for copy in asking + coming:
        copy.start()
    for i, ((half, _), copy) in enumerate(zip(asks, asking)):
        copy.wait()
        event = near_ref[i].astype(jnp.float32).astype(jnp.int32)
        words_ref[i] = event * ROWS + (event >> BLOCK_BITS) * (BLOCK_ROWS - EVENT_BLOCK * ROWS)
        for step in range(SIDE):
            back = step * (1 - 2 * core)
            tile = tile_of(y, x - back, core) if half == 0 else tile_of(y - back, x, core)
            at = i * SIDE + step
            chosen_ref[at : at + 1, :] = words_ref[i, pl.ds(tile, 1), :]
    copy = pltpu.make_async_copy(chosen_ref, asked_ref, sem)
    copy.start()
    copy.wait()
    going = []
    for i, (out_ref, blocks) in enumerate(zip(outs[: len(plan)], plan)):
        packed_ref = outs[len(plan) + i]
        for place, (half, hops, other) in enumerate(blocks):
            if half < 2:
                which, first = asks.index((half, hops)), halves.index(half)
            else:
                first = core if half == 2 else 1 - core
                which = asks.index((0, hops)) + first * (asks.index((1, hops)) - asks.index((0, hops)))
            while len(coming) > (5 * (len(halves) - 1 - first) if half < 2 else 0):
                coming.pop(0).wait()
            for step in range(SIDE):
                for slot in range(SLOTS):
                    row = (place * SIDE + step) * SLOTS + slot
                    start = asked_ref[which * SIDE + step, other * SLOTS + slot]
                    packed_ref[row] = full_ref[first, step, pl.ds(pl.multiple_of(start, 16), ROWS), :]
        going.append(pltpu.make_async_copy(packed_ref, out_ref, out_sems.at[i]))
        going[i].start()
    for copy in going:
        copy.wait()


def pack(plan, place, held, after=()):
    asks = {block[:2] for blocks in plan for block in blocks}
    asks |= {(half, hops) for which, hops in asks if which > 1 for half in range(2)}
    asks = tuple(sorted(ask for ask in asks if ask[0] < 2))
    halves = tuple(sorted({half for half, _ in asks}))
    sources = [held[1 - half][{0: 0, 1: 2, 2: 3, 3: 1}[hops]] for half, hops in asks]
    pieces = [piece for half in halves for piece in held[half]]
    shape = lambda blocks: (len(blocks) * SIDE * SLOTS, ROWS, LANES)
    tiles = BLOCK_ROWS - EVENT_BLOCK * ROWS
    chosen = ((len(asks) * SIDE + 7) // 8 * 8, LANES)
    return pl.pallas_call(
        functools.partial(pack_kernel, plan, asks, halves, len(after)),
        in_specs=[SMEM] + [ANY] * (len(asks) + len(pieces) + len(after)),
        out_specs=[ANY] * len(plan),
        out_shape=[jax.ShapeDtypeStruct(shape(blocks), jnp.bfloat16) for blocks in plan],
        scratch_shapes=[pltpu.VMEM(shape(blocks), jnp.bfloat16) for blocks in plan]
        + [
            pltpu.VMEM((len(asks), tiles, LANES), jnp.bfloat16),
            pltpu.VMEM((len(halves), SIDE) + pieces[0].shape, jnp.bfloat16),
            pltpu.VMEM((len(asks), tiles, LANES), jnp.int32),
            pltpu.VMEM(chosen, jnp.int32),
            pltpu.SMEM(chosen, jnp.int32),
            pltpu.SemaphoreType.DMA((len(asks) + len(pieces),)),
            pltpu.SemaphoreType.DMA((len(plan),)),
            pltpu.SemaphoreType.DMA,
        ],
        compiler_params=PARAMS,
        name="pack",
    )(place, *sources, *pieces, *after)


def join_kernel(*refs):
    *parts, more_ref, out_ref = refs
    size = parts[0].shape[0] // 2
    for i, part in enumerate(parts):
        out_ref[i * size : (i + 1) * size] = part[size:]
    out_ref[len(parts) * size :] = more_ref[...]


def join(parts, more):
    length = parts[0].shape[0] // 2 * len(parts) + more.shape[0]
    return pl.pallas_call(
        join_kernel,
        in_specs=[VMEM] * (len(parts) + 1),
        out_specs=VMEM,
        out_shape=jax.ShapeDtypeStruct((length,) + more.shape[1:], more.dtype),
        compiler_params=PARAMS,
        name="join",
    )(*parts, more)


def pair_kernel(blocks, arrays, first, last, place_ref, local_ref, count_ref, table_ref, *refs):
    own, power = refs[:2], refs[2:4]
    partner = refs[4 : 4 + arrays]
    refs = refs[4 + arrays :]
    if not first:
        before_ref, refs = refs[0], refs[1:]
    out_ref, refs = refs[0], refs[1:]
    if last:
        turned_ref, refs = refs[0], refs[1:]
    cross_ref, energy_ref, factor_ref, came_ref, sems = refs
    y, x, core = place_ref[0], place_ref[1], place_ref[2]
    rows = SIDE * SLOTS
    copies = [
        pltpu.make_async_copy(partner[array].at[pl.ds(offset, rows)], came_ref.at[i], sems.at[i])
        for i, (*_, array, offset) in enumerate(blocks)
    ]
    for copy in copies:
        copy.start()
    if not first:
        out_ref[...] = before_ref[...]
    def one_block(number, half, shift, from_core):

        def tile_at(step):
            way = 1 - 2 * from_core
            if half == 0:
                return tile_of(y - way * shift, x - way * step, from_core)
            return tile_of(y - way * step, x - way * shift, from_core)

        def one_tile(step, carry):
            tile = tile_at(step)
            live = count_ref[tile]
            for slot in range(SLOTS):
                event = local_ref[tile * SLOTS + slot]
                mine = own[half][event_rows(event), :].astype(jnp.float32)
                mine = mine.reshape(3, 2, 8, LANES)
                row = step * SLOTS + slot
                theirs = came_ref[number, row].astype(jnp.float32).reshape(3, 2, 8, LANES)
                real = jnp.sum(mine * theirs, axis=(0, 1))
                imag = jnp.sum(mine[:, 1] * theirs[:, 0] - mine[:, 0] * theirs[:, 1], axis=0)
                cross = jnp.concatenate([real, imag], -1)
                cross_ref[pl.ds(pl.multiple_of(row * 8, 8), 8), :] = cross
                energy_ref[row] = jnp.sum(theirs * theirs, axis=(0, 1))
                alive = jnp.where(slot < live, jnp.float32(2.0 / SCALE_WIDTH), jnp.float32(0))
                factor_ref[0, row] = power[half][event]
                factor_ref[1, row] = jnp.full((8, LANES), alive, jnp.float32)
            return carry

        lax.fori_loop(0, SIDE, one_tile, 0)
        corr = jnp.dot(
            cross_ref[...].astype(jnp.bfloat16), table_ref[...], preferred_element_type=jnp.float32
        ).reshape(rows, 8, 2 * LANES)
        low = lax.broadcasted_iota(jnp.int32, (rows, 8, LANES), 1) < 4
        corr = jnp.where(low, corr[..., :LANES], corr[..., LANES:])
        corr = corr + pltpu.roll(corr, 4, 1)
        energy = jnp.broadcast_to(
            jnp.sum(energy_ref[...], axis=-1, keepdims=True), (rows, 8, LANES)
        )
        energy = (energy + pltpu.roll(energy, 4, 1)) * (2.0 / SCALE_WIDTH)
        corr = corr * (lax.rsqrt(factor_ref[0] * energy + 1e-06) * factor_ref[1])
        for step in range(SIDE):
            at = pl.ds(pl.multiple_of(tile_at(jnp.int32(step)) * SLOTS, SLOTS), SLOTS)
            out_ref[at, 4 * half : 4 * half + 4, :] = corr[
                step * SLOTS : (step + 1) * SLOTS, 4 * half : 4 * half + 4
            ]

    for number, (half, shift, other, *_) in enumerate(blocks):
        copies[number].wait()
        from_core = lax.rem(core + other, 2)
        if half < 2:
            one_block(number, half, shift, from_core)
            continue
        for fixed in range(2):
            sender = fixed if half == 2 else 1 - fixed
            pl.when(from_core == sender)(functools.partial(one_block, number, fixed, shift, from_core))
    if last:
        turned_ref[...] = jnp.sum(out_ref[...], axis=1).T


def pairs(blocks, place, local, count, table, own, power, partner, total, last):
    rows, slots = SIDE * SLOTS, local.shape[0]
    first = total is None
    out_shape = [jax.ShapeDtypeStruct((slots, 8, LAGS), jnp.float32)]
    if last:
        out_shape += [jax.ShapeDtypeStruct((LAGS, slots), jnp.float32)]
    args = [place, local, count, table, *own, *power, *partner] + ([] if first else [total])
    return pl.pallas_call(
        functools.partial(pair_kernel, blocks, len(partner), first, last),
        in_specs=[SMEM] * 3 + [VMEM] * 5 + [ANY] * len(partner) + [VMEM] * (not first),
        out_specs=[VMEM] * len(out_shape),
        out_shape=out_shape,
        scratch_shapes=[
            pltpu.VMEM((rows * 8, 2 * LANES), jnp.float32),
            pltpu.VMEM((rows, 8, LANES), jnp.float32),
            pltpu.VMEM((2, rows, 8, LANES), jnp.float32),
            pltpu.VMEM((len(blocks), rows, ROWS, LANES), jnp.bfloat16),
            pltpu.SemaphoreType.DMA((len(blocks),)),
        ],
        compiler_params=WHOLE,
        name="pairs",
    )(*args)


def permute(value, rule):
    moves = []
    for y in range(SIDE):
        for x in range(SIDE):
            for core in range(2):
                dy, dx, dcore = rule(core)
                target = ((y + dy) % SIDE * SIDE + (x + dx) % SIDE) * 2 + (core + dcore) % 2
                moves.append(((y * SIDE + x) * 2 + core, target))
    return lax.ppermute(value, "tile", moves)


def hop(value, dy, dx, dcore):
    return permute(value, lambda core: ((1 - 2 * core) * dy, (1 - 2 * core) * dx, dcore))


def far_hop(value, which, dcore):
    return permute(value, lambda core: (2, 0, dcore) if core == which else (0, 2, dcore))


def on_device(waves, station_mask, pair_local, pair_remote, pair_count):
    width, tiles = waves.shape[-1], pair_remote.shape[1]
    events, stations = station_mask.shape
    groups = lax.axis_size("sta")
    here = lax.axis_index("tile")
    place = jnp.stack([here // (2 * SIDE), here // 2 % SIDE, here % 2]).astype(jnp.int32)
    local, count = pair_local.reshape(-1), pair_count.reshape(-1)

    other = hop(pair_remote, 0, 0, 1)
    own = own_spectra(waves, station_mask, jnp.asarray(forward_table(width)), pair_remote, other)
    power = own_power(own)

    along = lambda half, value, hops: hop(value, *((0, hops) if half == 0 else (hops, 0)), 0)
    rings = [(half, hops) for hops in (1, SIDE - 1) for half in range(2)]
    came = [along(half, own[half], hops) for half, hops in rings]
    passed = [along(half, value, hops) for (half, hops), value in zip(rings, split(came))]
    held = [[own[half], *came[half::2], *passed[half::2]] for half in range(2)]
    across = lambda half, value, hops, other: hop(value, *((hops, 0) if half == 0 else (0, hops)), other)

    plan = tuple(((*where, 0), (*where, 1)) for where in rings + [(2, 2)])
    packed = pack(plan, place, held, power[:1])
    got = [across(where[0], value, where[1], 0) for value, where in zip(packed, rings)]
    got.append(far_hop(packed[4], 0, 0))
    rest = pack(
        (((0, 0, 0), (1, 0, 0)), ((0, 0, 1), (1, 0, 1)), ((3, 2, 0),), ((3, 2, 1),)),
        place,
        held,
        packed[:1],
    )
    far = [far_hop(rest[2 + other], 1, other) for other in range(2)]
    size = SIDE * SLOTS
    swapped = hop(join(got, rest[1]), 0, 0, 1)

    table = jnp.asarray(lag_table(width))
    calc = functools.partial(pairs, place=place, local=local, count=count, table=table, own=own, power=power)
    near, early = [(0, 0), (1, 0)], rings + [(2, 2)]
    blocks = tuple((*where, 0, 5, number * size) for number, where in enumerate(near))
    blocks += tuple((*where, 0, number, 0) for number, where in enumerate(early))
    total = calc(blocks, partner=got + [rest[0]], total=None, last=False)[0]
    blocks = tuple((*where, 1, 0, number * size) for number, where in enumerate(early + near))
    total = calc(blocks, partner=[swapped], total=total, last=False)[0]
    blocks = tuple((3, 2, other, other, 0) for other in range(2))
    total, stack = calc(blocks, partner=far, total=total, last=True)

    stack = lax.all_to_all(stack, "sta", split_axis=0, concat_axis=0, tiled=True)
    stack = jnp.sum(stack.reshape(groups, LAGS // groups, -1), axis=0).T
    station_coef = total.astype(jnp.bfloat16).reshape(1, tiles, SLOTS, stations, LAGS)
    return (station_coef, stack.reshape(1, tiles, SLOTS, LAGS // groups))


def solution(mesh):
    placed = (
        P("tile", None, "sta", None),
        P("tile", "sta"),
        P("tile", None, None),
        P("tile", None, None),
        P("tile", None),
    )
    return jax.shard_map(
        on_device,
        mesh=mesh,
        in_specs=placed,
        out_specs=(P("tile", None, None, "sta", None), P("tile", None, None, "sta")),
        check_vma=False,
    )
```

```python
import functools
import math

import jax
import jax.numpy as jnp
import ml_dtypes
import numpy as np
from jax import lax
from jax.experimental import pallas as pl
from jax.experimental.pallas import tpu as pltpu
from jax.sharding import PartitionSpec as P

BAND = 256
LAGS = 128
SLOTS = 8
SIDE = 4
LANES = 128
ROWS = 48
BLOCK_BITS = 4
EVENT_BLOCK = 1 << BLOCK_BITS
BLOCK_ROWS = EVENT_BLOCK * ROWS + 32
SCALE_WIDTH = 1024.0
VMEM = pl.BlockSpec(memory_space=pltpu.VMEM)
ANY = pl.BlockSpec(memory_space=pl.ANY)
SMEM = pl.BlockSpec(memory_space=pltpu.SMEM)
PARAMS = pltpu.CompilerParams(vmem_limit_bytes=24 * 1024 * 1024)
WHOLE = pltpu.CompilerParams(vmem_limit_bytes=60 * 1024 * 1024)


def forward_table(width):
    phase = np.arange(width)[:, None] * np.arange(1, BAND + 1)[None, :] % width * (2.0 * math.pi / width)
    return np.concatenate([np.cos(phase), -np.sin(phase)], 1).astype(ml_dtypes.bfloat16)


def lag_table(width):
    phase = np.arange(1, BAND + 1)[:, None] * (np.arange(LAGS)[None, :] - LAGS // 2) % width
    phase = phase * (2.0 * math.pi / width)
    table = np.concatenate([np.cos(phase), -np.sin(phase)], 0).astype(ml_dtypes.bfloat16)
    low_re, high_re, low_im, high_im = (table[i * LANES : (i + 1) * LANES] for i in range(4))
    return np.concatenate(
        [np.concatenate([low_re, high_re], 1), np.concatenate([low_im, high_im], 1)], 0
    )


def spectra_kernel(waves_ref, mask_ref, table_ref, mine_ref, other_ref, *refs):
    outs, (came_ref, factors_ref, sems) = refs[:2], refs[2:]
    rows = EVENT_BLOCK * 24
    blocks = waves_ref.shape[0] // rows
    copies = [pltpu.make_async_copy(table_ref, factors_ref, sems.at[blocks])]
    copies += [
        pltpu.make_async_copy(waves_ref.at[pl.ds(i * rows, rows), :], came_ref.at[i], sems.at[i])
        for i in range(blocks)
    ]
    for copy in copies:
        copy.start()
    same = lax.broadcasted_iota(jnp.int32, (1, 8, 8), 1) == lax.broadcasted_iota(jnp.int32, (1, 8, 8), 2)
    mine, other = mine_ref[0], other_ref[0]
    blank = jnp.zeros((mine.shape[0], LANES - 2 * SLOTS), mine.dtype)
    asked = jnp.concatenate([mine, other, blank], 1).astype(jnp.float32).astype(jnp.bfloat16)
    copies[0].wait()
    low = lax.broadcasted_iota(jnp.int32, (EVENT_BLOCK * 3, 8, LANES), 1) < 4
    for block in range(blocks):
        mask = mask_ref[block * EVENT_BLOCK : (block + 1) * EVENT_BLOCK, :].astype(jnp.float32)
        mask = jnp.sum(jnp.where(same, mask[:, None, :], 0.0), axis=-1, keepdims=True)[:, None]
        copies[block + 1].wait()
        flat = jnp.dot(came_ref[block], factors_ref[...], preferred_element_type=jnp.float32)
        flat = flat.reshape(EVENT_BLOCK, 3, 8, 4 * LANES) * mask
        part = [
            flat[..., i * LANES : (i + 1) * LANES].reshape(EVENT_BLOCK * 3, 8, LANES)
            for i in range(4)
        ]
        turned = [pltpu.roll(value, 4, 1) for value in part]
        halves = (
            (jnp.where(low, part[0], turned[1]), jnp.where(low, part[2], turned[3])),
            (jnp.where(low, turned[0], part[1]), jnp.where(low, turned[2], part[3])),
        )
        first, last = block * BLOCK_ROWS, block * BLOCK_ROWS + EVENT_BLOCK * ROWS
        for (real, imag), out_ref in zip(halves, outs):
            packed = jnp.concatenate([real, imag], 1).astype(jnp.bfloat16)
            out_ref[first:last, :] = packed.reshape(EVENT_BLOCK * ROWS, LANES)
            out_ref[last : first + BLOCK_ROWS, :] = asked


def own_spectra(waves, mask, table, mine, other):
    flat = waves.reshape(-1, waves.shape[-1])
    blocks = mask.shape[0] // EVENT_BLOCK
    half = jax.ShapeDtypeStruct((blocks * BLOCK_ROWS, LANES), jnp.bfloat16)
    return pl.pallas_call(
        spectra_kernel,
        in_specs=[ANY, VMEM, ANY, VMEM, VMEM],
        out_specs=[VMEM] * 2,
        out_shape=[half, half],
        scratch_shapes=[
            pltpu.VMEM((blocks, flat.shape[0] // blocks, flat.shape[1]), flat.dtype),
            pltpu.VMEM(table.shape, table.dtype),
            pltpu.SemaphoreType.DMA((blocks + 1,)),
        ],
        compiler_params=PARAMS,
        name="spectra",
    )(flat, mask, table, mine, other)


def power_kernel(first_ref, second_ref, *outs):
    for spectra_ref, out_ref in zip((first_ref, second_ref), outs):
        for block in range(out_ref.shape[0] // EVENT_BLOCK):
            start = block * BLOCK_ROWS
            values = spectra_ref[start : start + EVENT_BLOCK * ROWS, :].astype(jnp.float32)
            values = values.reshape(EVENT_BLOCK, 3, 2, 8, LANES)
            total = jnp.sum(jnp.sum(values * values, axis=(1, 2)), axis=-1, keepdims=True)
            total = jnp.broadcast_to(total, (EVENT_BLOCK, 8, LANES))
            total = (total + pltpu.roll(total, 4, 1)) * (2.0 / SCALE_WIDTH)
            out_ref[block * EVENT_BLOCK : (block + 1) * EVENT_BLOCK] = total


def own_power(own):
    events = own[0].shape[0] // BLOCK_ROWS * EVENT_BLOCK
    return pl.pallas_call(
        power_kernel,
        in_specs=[VMEM] * 2,
        out_specs=[VMEM] * 2,
        out_shape=[jax.ShapeDtypeStruct((events, 8, LANES), jnp.float32)] * 2,
        compiler_params=PARAMS,
        name="power",
    )(*own)


def split(values):
    rows = values[0].shape[0]
    part = lambda i: pl.BlockSpec((rows // 2, LANES), lambda _: (2 * i // len(values), 0))
    whole = pl.BlockSpec((rows // 2, LANES), lambda _: (0, 0))

    def kernel(*refs):
        for in_ref, out_ref in zip(refs[: len(values)], refs[len(values) :]):
            out_ref[...] = in_ref[...]

    return pl.pallas_call(
        kernel,
        grid=(1,),
        in_specs=[part(i) for i in range(len(values))],
        out_specs=[whole] * len(values),
        out_shape=[jax.ShapeDtypeStruct((rows // 2, LANES), values[0].dtype)] * len(values),
        compiler_params=PARAMS,
        name="split",
    )(*values)


def event_rows(event):
    start = event * ROWS + (event >> BLOCK_BITS) * (BLOCK_ROWS - EVENT_BLOCK * ROWS)
    return pl.ds(pl.multiple_of(start, 16), ROWS)


def tile_of(y, x, core):
    return (lax.rem(y + SIDE, SIDE) * SIDE + lax.rem(x + SIDE, SIDE)) * 2 + core


def pack_kernel(plan, asks, halves, later, place_ref, *refs):
    sources, refs = refs[: len(asks)], refs[len(asks) :]
    held, outs = refs[: 5 * len(halves)], refs[5 * len(halves) + later : -8]
    near_ref, full_ref, words_ref, chosen_ref, asked_ref, in_sems, out_sems, sem = refs[-8:]
    y, x, core = place_ref[0], place_ref[1], place_ref[2]
    tiles, size = near_ref.shape[1], full_ref.shape[2]
    asking = [
        pltpu.make_async_copy(
            source.at[pl.ds(EVENT_BLOCK * ROWS, tiles), :], near_ref.at[i], in_sems.at[i]
        )
        for i, source in enumerate(sources)
    ]
    coming = []
    for i in range(len(halves)):
        steps = ((0, 0, size), (1, 0, size), (3, 0, size), (2, 0, size // 2), (2, size // 2, size // 2))
        for number, (step, start, length) in enumerate(steps):
            target = full_ref.at[i, step, pl.ds(start, length), :]
            which = 5 * i + number
            coming.append(pltpu.make_async_copy(held[which], target, in_sems.at[len(asks) + which]))
    for copy in asking + coming:
        copy.start()
    for i, ((half, _), copy) in enumerate(zip(asks, asking)):
        copy.wait()
        event = near_ref[i].astype(jnp.float32).astype(jnp.int32)
        words_ref[i] = event * ROWS + (event >> BLOCK_BITS) * (BLOCK_ROWS - EVENT_BLOCK * ROWS)
        for step in range(SIDE):
            back = step * (1 - 2 * core)
            tile = tile_of(y, x - back, core) if half == 0 else tile_of(y - back, x, core)
            at = i * SIDE + step
            chosen_ref[at : at + 1, :] = words_ref[i, pl.ds(tile, 1), :]
    copy = pltpu.make_async_copy(chosen_ref, asked_ref, sem)
    copy.start()
    copy.wait()
    going = []
    for i, (out_ref, blocks) in enumerate(zip(outs[: len(plan)], plan)):
        packed_ref = outs[len(plan) + i]
        for place, (half, hops, other) in enumerate(blocks):
            if half < 2:
                which, first = asks.index((half, hops)), halves.index(half)
            else:
                first = core if half == 2 else 1 - core
                which = asks.index((0, hops)) + first * (asks.index((1, hops)) - asks.index((0, hops)))
            while len(coming) > (5 * (len(halves) - 1 - first) if half < 2 else 0):
                coming.pop(0).wait()
            for step in range(SIDE):
                for slot in range(SLOTS):
                    row = (place * SIDE + step) * SLOTS + slot
                    start = asked_ref[which * SIDE + step, other * SLOTS + slot]
                    packed_ref[row] = full_ref[first, step, pl.ds(pl.multiple_of(start, 16), ROWS), :]
        going.append(pltpu.make_async_copy(packed_ref, out_ref, out_sems.at[i]))
        going[i].start()
    for copy in going:
        copy.wait()


def pack(plan, place, held, after=()):
    asks = {block[:2] for blocks in plan for block in blocks}
    asks |= {(half, hops) for which, hops in asks if which > 1 for half in range(2)}
    asks = tuple(sorted(ask for ask in asks if ask[0] < 2))
    halves = tuple(sorted({half for half, _ in asks}))
    sources = [held[1 - half][{0: 0, 1: 2, 2: 3, 3: 1}[hops]] for half, hops in asks]
    pieces = [piece for half in halves for piece in held[half]]
    shape = lambda blocks: (len(blocks) * SIDE * SLOTS, ROWS, LANES)
    tiles = BLOCK_ROWS - EVENT_BLOCK * ROWS
    chosen = ((len(asks) * SIDE + 7) // 8 * 8, LANES)
    return pl.pallas_call(
        functools.partial(pack_kernel, plan, asks, halves, len(after)),
        in_specs=[SMEM] + [ANY] * (len(asks) + len(pieces) + len(after)),
        out_specs=[ANY] * len(plan),
        out_shape=[jax.ShapeDtypeStruct(shape(blocks), jnp.bfloat16) for blocks in plan],
        scratch_shapes=[pltpu.VMEM(shape(blocks), jnp.bfloat16) for blocks in plan]
        + [
            pltpu.VMEM((len(asks), tiles, LANES), jnp.bfloat16),
            pltpu.VMEM((len(halves), SIDE) + pieces[0].shape, jnp.bfloat16),
            pltpu.VMEM((len(asks), tiles, LANES), jnp.int32),
            pltpu.VMEM(chosen, jnp.int32),
            pltpu.SMEM(chosen, jnp.int32),
            pltpu.SemaphoreType.DMA((len(asks) + len(pieces),)),
            pltpu.SemaphoreType.DMA((len(plan),)),
            pltpu.SemaphoreType.DMA,
        ],
        compiler_params=PARAMS,
        name="pack",
    )(place, *sources, *pieces, *after)


def join_kernel(*refs):
    *parts, more_ref, out_ref = refs
    size = parts[0].shape[0] // 2
    for i, part in enumerate(parts):
        out_ref[i * size : (i + 1) * size] = part[size:]
    out_ref[len(parts) * size :] = more_ref[...]


def join(parts, more):
    length = parts[0].shape[0] // 2 * len(parts) + more.shape[0]
    return pl.pallas_call(
        join_kernel,
        in_specs=[VMEM] * (len(parts) + 1),
        out_specs=VMEM,
        out_shape=jax.ShapeDtypeStruct((length,) + more.shape[1:], more.dtype),
        compiler_params=PARAMS,
        name="join",
    )(*parts, more)


def pair_kernel(blocks, arrays, last, place_ref, local_ref, count_ref, table_ref, *refs):
    own, power = refs[:2], refs[2:4]
    partner, refs = refs[4 : 4 + arrays], refs[4 + arrays :]
    if last:
        _, before_ref, out_ref, turned_ref, *refs = refs
        stack_ref, send_ref, send_sems, *refs = refs
        stack_ref[...] = before_ref[...]
    else:
        out_ref, stack_ref, *refs = refs
        stack_ref[...] = jnp.zeros_like(stack_ref)
    cross_ref, energy_ref, factor_ref, came_ref, sems = refs
    y, x, core = place_ref[0], place_ref[1], place_ref[2]
    rows = SIDE * SLOTS
    copies = [
        pltpu.make_async_copy(partner[array].at[pl.ds(offset, rows)], came_ref.at[i], sems.at[i])
        for i, (*_, array, offset) in enumerate(blocks)
    ]
    for copy in copies:
        copy.start()
    ones = jnp.ones((LANES, LANES), jnp.bfloat16)

    def one_block(number, half, shift, from_core):
        def tile_at(step):
            way = 1 - 2 * from_core
            if half == 0:
                return tile_of(y - way * shift, x - way * step, from_core)
            return tile_of(y - way * step, x - way * shift, from_core)

        def one_tile(step, carry):
            tile = tile_at(step)
            live = count_ref[tile]
            for slot in range(SLOTS):
                event = local_ref[tile * SLOTS + slot]
                mine = own[half][event_rows(event), :].astype(jnp.float32)
                mine = mine.reshape(3, 2, 8, LANES)
                row = step * SLOTS + slot
                theirs = came_ref[number, row].astype(jnp.float32).reshape(3, 2, 8, LANES)
                real = jnp.sum(mine * theirs, axis=(0, 1))
                imag = jnp.sum(mine[:, 1] * theirs[:, 0] - mine[:, 0] * theirs[:, 1], axis=0)
                at = pl.ds(pl.multiple_of(row * 8, 8), 8)
                cross_ref[at, :] = jnp.concatenate([real, imag], -1)
                energy_ref[at, :] = jnp.sum(theirs * theirs, axis=(0, 1))
                alive = jnp.where(slot < live, jnp.float32(2.0 / SCALE_WIDTH), jnp.float32(0))
                factor_ref[0, row] = power[half][event]
                factor_ref[1, row] = jnp.full((8, LANES), alive, jnp.float32)
            return carry

        lax.fori_loop(0, SIDE, one_tile, 0)
        corr = jnp.dot(
            cross_ref[...].astype(jnp.bfloat16), table_ref[...], preferred_element_type=jnp.float32
        ).reshape(rows, 8, 2 * LANES)
        low = lax.broadcasted_iota(jnp.int32, (rows, 8, LANES), 1) < 4
        corr = jnp.where(low, corr[..., :LANES], corr[..., LANES:])
        corr = corr + pltpu.roll(corr, 4, 1)
        energy = jnp.dot(
            energy_ref[...].astype(jnp.bfloat16), ones, preferred_element_type=jnp.float32
        ).reshape(rows, 8, LANES)
        energy = (energy + pltpu.roll(energy, 4, 1)) * (2.0 / SCALE_WIDTH)
        corr = corr * (lax.rsqrt(factor_ref[0] * energy + 1e-06) * factor_ref[1])
        shares = jnp.sum(corr, axis=1) * 0.5
        going = []
        if last:
            send_ref[number] = corr
        for step in range(SIDE):
            of = slice(step * SLOTS, (step + 1) * SLOTS)
            at = pl.ds(pl.multiple_of(tile_at(jnp.int32(step)) * SLOTS, SLOTS), SLOTS)
            stack_ref[at, :] += shares[of]
            if last:
                sem = send_sems.at[number, step]
                going.append(
                    pltpu.make_async_copy(send_ref.at[number, pl.ds(step * SLOTS, SLOTS)], out_ref.at[half, at], sem)
                )
                going[step].start()
            else:
                out_ref[half, at] = corr[of]
        for copy in going:
            copy.wait()

    for number, (half, shift, other, *_) in enumerate(blocks):
        copies[number].wait()
        from_core = lax.rem(core + other, 2)
        if half < 2:
            one_block(number, half, shift, from_core)
            continue
        for fixed in range(2):
            sender = fixed if half == 2 else 1 - fixed
            pl.when(from_core == sender)(functools.partial(one_block, number, fixed, shift, from_core))
    if last:
        turned_ref[...] = stack_ref[...].T


def pairs(blocks, place, local, count, table, own, power, partner, total=None, stack=None):
    rows, slots = SIDE * SLOTS, local.shape[0]
    last = total is not None
    args = [place, local, count, table, *own, *power, *partner]
    shape = lambda *size: jax.ShapeDtypeStruct(size, jnp.float32)
    out_shape = [shape(2, slots, 8, LAGS), shape(LAGS, slots) if last else shape(slots, LAGS)]
    work = [
        pltpu.VMEM((rows * 8, 2 * LANES), jnp.float32),
        pltpu.VMEM((rows * 8, LANES), jnp.float32),
        pltpu.VMEM((2, rows, 8, LANES), jnp.float32),
        pltpu.VMEM((len(blocks), rows, ROWS, LANES), jnp.bfloat16),
        pltpu.SemaphoreType.DMA((len(blocks),)),
    ]
    if last:
        sending = [
            pltpu.VMEM((slots, LAGS), jnp.float32),
            pltpu.VMEM((len(blocks), rows, 8, LAGS), jnp.float32),
            pltpu.SemaphoreType.DMA((len(blocks), SIDE)),
        ]
        work = sending + work
    return pl.pallas_call(
        functools.partial(pair_kernel, blocks, len(partner), last),
        in_specs=[SMEM] * 3 + [VMEM] * 5 + [ANY] * len(partner) + [ANY, VMEM] * last,
        out_specs=[ANY if last else VMEM, VMEM],
        out_shape=out_shape,
        input_output_aliases={len(args): 0} if last else {},
        scratch_shapes=work,
        compiler_params=WHOLE,
        name="pairs",
    )(*args, *([total, stack] if last else []))


def permute(value, rule):
    moves = []
    for y in range(SIDE):
        for x in range(SIDE):
            for core in range(2):
                dy, dx, dcore = rule(core)
                target = ((y + dy) % SIDE * SIDE + (x + dx) % SIDE) * 2 + (core + dcore) % 2
                moves.append(((y * SIDE + x) * 2 + core, target))
    return lax.ppermute(value, "tile", moves)


def hop(value, dy, dx, dcore):
    return permute(value, lambda core: ((1 - 2 * core) * dy, (1 - 2 * core) * dx, dcore))


def far_hop(value, which, dcore):
    return permute(value, lambda core: (2, 0, dcore) if core == which else (0, 2, dcore))


def on_device(waves, station_mask, pair_local, pair_remote, pair_count):
    width, tiles = waves.shape[-1], pair_remote.shape[1]
    events, stations = station_mask.shape
    groups = lax.axis_size("sta")
    here = lax.axis_index("tile")
    place = jnp.stack([here // (2 * SIDE), here // 2 % SIDE, here % 2]).astype(jnp.int32)
    local, count = pair_local.reshape(-1), pair_count.reshape(-1)

    other = hop(pair_remote, 0, 0, 1)
    own = own_spectra(waves, station_mask, jnp.asarray(forward_table(width)), pair_remote, other)
    power = own_power(own)

    along = lambda half, value, hops: hop(value, *((0, hops) if half == 0 else (hops, 0)), 0)
    rings = [(half, hops) for hops in (1, SIDE - 1) for half in range(2)]
    came = [along(half, own[half], hops) for half, hops in rings]
    passed = [along(half, value, hops) for (half, hops), value in zip(rings, split(came))]
    held = [[own[half], *came[half::2], *passed[half::2]] for half in range(2)]
    across = lambda half, value, hops, other: hop(value, *((hops, 0) if half == 0 else (0, hops)), other)

    plan = tuple(((*where, 0), (*where, 1)) for where in rings + [(2, 2)])
    packed = pack(plan, place, held, [power[0], local])
    got = [across(where[0], value, where[1], 0) for value, where in zip(packed, rings)]
    got.append(far_hop(packed[4], 0, 0))
    rest = pack(
        (((0, 0, 0), (1, 0, 0)), ((0, 0, 1), (1, 0, 1)), ((3, 2, 0),), ((3, 2, 1),)),
        place,
        held,
        packed[:1],
    )
    far = [far_hop(rest[2 + other], 1, other) for other in range(2)]
    size = SIDE * SLOTS
    swapped = hop(join(got, rest[1]), 0, 0, 1)

    table = jnp.asarray(lag_table(width))
    calc = functools.partial(pairs, place=place, local=local, count=count, table=table, own=own, power=power)
    near, early = [(0, 0), (1, 0)], rings + [(2, 2)]
    blocks = tuple((*where, 0, 5, number * size) for number, where in enumerate(near))
    blocks += tuple((*where, 0, number, 0) for number, where in enumerate(early))
    blocks += tuple((*where, 1, 6, number * size) for number, where in enumerate(early + near))
    total, stack = calc(blocks, partner=got + [rest[0], swapped])
    blocks = tuple((3, 2, other, other, 0) for other in range(2))
    total, stack = calc(blocks, partner=far, total=total, stack=stack)

    stack = lax.all_to_all(stack, "sta", split_axis=0, concat_axis=0, tiled=True)
    stack = jnp.sum(stack.reshape(groups, LAGS // groups, -1), axis=0).T
    first = lax.broadcasted_iota(jnp.int32, total.shape[1:], 1) < stations // 2
    station_coef = jnp.where(first, total[0], total[1]).astype(jnp.bfloat16)
    station_coef = station_coef.reshape(1, tiles, SLOTS, stations, LAGS)
    return (station_coef, stack.reshape(1, tiles, SLOTS, LAGS // groups))


def solution(mesh):
    placed = (
        P("tile", None, "sta", None),
        P("tile", "sta"),
        P("tile", None, None),
        P("tile", None, None),
        P("tile", None),
    )
    return jax.shard_map(
        on_device,
        mesh=mesh,
        in_specs=placed,
        out_specs=(P("tile", None, None, "sta", None), P("tile", None, None, "sta")),
        check_vma=False,
    )
```

```python
import functools
import math

import jax
import jax.numpy as jnp
import ml_dtypes
import numpy as np
from jax import lax
from jax.experimental import pallas as pl
from jax.experimental.pallas import tpu as pltpu
from jax.sharding import PartitionSpec as P

BAND = 256
LAGS = 128
SLOTS = 8
SIDE = 4
LANES = 128
ROWS = 48
BLOCK_BITS = 4
EVENT_BLOCK = 1 << BLOCK_BITS
BLOCK_ROWS = EVENT_BLOCK * ROWS + 32
SCALE_WIDTH = 1024.0
VMEM = pl.BlockSpec(memory_space=pltpu.VMEM)
ANY = pl.BlockSpec(memory_space=pl.ANY)
SMEM = pl.BlockSpec(memory_space=pltpu.SMEM)
PARAMS = pltpu.CompilerParams(vmem_limit_bytes=24 * 1024 * 1024)


def forward_table(width):
    phase = np.arange(width)[:, None] * np.arange(1, BAND + 1)[None, :] % width * (2.0 * math.pi / width)
    return np.concatenate([np.cos(phase), -np.sin(phase)], 1).astype(ml_dtypes.bfloat16)


def lag_table(width):
    phase = np.arange(1, BAND + 1)[:, None] * (np.arange(LAGS)[None, :] - LAGS // 2) % width
    phase = phase * (2.0 * math.pi / width)
    table = np.concatenate([np.cos(phase), -np.sin(phase)], 0).astype(ml_dtypes.bfloat16)
    low_re, high_re, low_im, high_im = (table[i * LANES : (i + 1) * LANES] for i in range(4))
    return np.concatenate(
        [np.concatenate([low_re, high_re], 1), np.concatenate([low_im, high_im], 1)], 0
    )


def spectra_kernel(waves_ref, mask_ref, table_ref, mine_ref, other_ref, *refs):
    outs, (came_ref, factors_ref, sems) = refs[:2], refs[2:]
    rows = EVENT_BLOCK * 24
    blocks = waves_ref.shape[0] // rows
    copies = [pltpu.make_async_copy(table_ref, factors_ref, sems.at[blocks])]
    copies += [
        pltpu.make_async_copy(waves_ref.at[pl.ds(i * rows, rows), :], came_ref.at[i], sems.at[i])
        for i in range(blocks)
    ]
    for copy in copies:
        copy.start()
    def tiles_first(ref):
        blank = jnp.zeros((SLOTS, LANES - ref.shape[2]), jnp.float32)
        return jnp.concatenate([ref[0].astype(jnp.float32), blank], 1).T[: ref.shape[2]]

    blank = jnp.zeros((mine_ref.shape[2], LANES - 2 * SLOTS), jnp.float32)
    asked = jnp.concatenate([tiles_first(mine_ref), tiles_first(other_ref), blank], 1)
    asked = asked.astype(jnp.bfloat16)
    masks = mask_ref[...].astype(jnp.float32)
    copies[0].wait()
    low = lax.broadcasted_iota(jnp.int32, (EVENT_BLOCK * 3, 8, LANES), 1) < 4
    for block in range(blocks):
        events = range(block * EVENT_BLOCK, (block + 1) * EVENT_BLOCK)
        mask = jnp.stack([masks[:, event : event + 1] for event in events])[:, None]
        copies[block + 1].wait()
        flat = jnp.dot(came_ref[block], factors_ref[...], preferred_element_type=jnp.float32)
        flat = flat.reshape(EVENT_BLOCK, 3, 8, 4 * LANES) * mask
        part = [
            flat[..., i * LANES : (i + 1) * LANES].reshape(EVENT_BLOCK * 3, 8, LANES)
            for i in range(4)
        ]
        turned = [pltpu.roll(value, 4, 1) for value in part]
        halves = (
            (jnp.where(low, part[0], turned[1]), jnp.where(low, part[2], turned[3])),
            (jnp.where(low, turned[0], part[1]), jnp.where(low, turned[2], part[3])),
        )
        first, last = block * BLOCK_ROWS, block * BLOCK_ROWS + EVENT_BLOCK * ROWS
        for (real, imag), out_ref in zip(halves, outs):
            packed = jnp.concatenate([real, imag], 1).astype(jnp.bfloat16)
            out_ref[first:last, :] = packed.reshape(EVENT_BLOCK * ROWS, LANES)
            out_ref[last : first + BLOCK_ROWS, :] = asked


def own_spectra(waves, mask, table, mine, other):
    flat = waves.reshape(-1, waves.shape[-1])
    blocks = mask.shape[1] // EVENT_BLOCK
    half = jax.ShapeDtypeStruct((blocks * BLOCK_ROWS, LANES), jnp.bfloat16)
    return pl.pallas_call(
        spectra_kernel,
        in_specs=[ANY, VMEM, ANY, VMEM, VMEM],
        out_specs=[VMEM] * 2,
        out_shape=[half, half],
        scratch_shapes=[
            pltpu.VMEM((blocks, flat.shape[0] // blocks, flat.shape[1]), flat.dtype),
            pltpu.VMEM(table.shape, table.dtype),
            pltpu.SemaphoreType.DMA((blocks + 1,)),
        ],
        compiler_params=PARAMS,
        name="spectra",
    )(flat, mask, table, mine, other)


def power_kernel(first_ref, second_ref, *outs):
    for spectra_ref, out_ref in zip((first_ref, second_ref), outs):
        for block in range(out_ref.shape[0] // EVENT_BLOCK):
            start = block * BLOCK_ROWS
            values = spectra_ref[start : start + EVENT_BLOCK * ROWS, :].astype(jnp.float32)
            values = values.reshape(EVENT_BLOCK, 3, 2, 8, LANES)
            total = jnp.sum(jnp.sum(values * values, axis=(1, 2)), axis=-1, keepdims=True)
            total = jnp.broadcast_to(total, (EVENT_BLOCK, 8, LANES))
            total = (total + pltpu.roll(total, 4, 1)) * (2.0 / SCALE_WIDTH)
            out_ref[block * EVENT_BLOCK : (block + 1) * EVENT_BLOCK] = total


def own_power(own):
    events = own[0].shape[0] // BLOCK_ROWS * EVENT_BLOCK
    return pl.pallas_call(
        power_kernel,
        in_specs=[VMEM] * 2,
        out_specs=[VMEM] * 2,
        out_shape=[jax.ShapeDtypeStruct((events, 8, LANES), jnp.float32)] * 2,
        compiler_params=PARAMS,
        name="power",
    )(*own)


def split(values):
    rows = values[0].shape[0]
    part = lambda i: pl.BlockSpec((rows // 2, LANES), lambda _: (2 * i // len(values), 0))
    whole = pl.BlockSpec((rows // 2, LANES), lambda _: (0, 0))

    def kernel(*refs):
        for in_ref, out_ref in zip(refs[: len(values)], refs[len(values) :]):
            out_ref[...] = in_ref[...]

    return pl.pallas_call(
        kernel,
        grid=(1,),
        in_specs=[part(i) for i in range(len(values))],
        out_specs=[whole] * len(values),
        out_shape=[jax.ShapeDtypeStruct((rows // 2, LANES), values[0].dtype)] * len(values),
        compiler_params=PARAMS,
        name="split",
    )(*values)


def event_rows(event):
    start = event * ROWS + (event >> BLOCK_BITS) * (BLOCK_ROWS - EVENT_BLOCK * ROWS)
    return pl.ds(pl.multiple_of(start, 16), ROWS)


def tile_of(y, x, core):
    return (lax.rem(y + SIDE, SIDE) * SIDE + lax.rem(x + SIDE, SIDE)) * 2 + core


def pack_kernel(plan, asks, halves, later, place_ref, *refs):
    sources, refs = refs[: len(asks)], refs[len(asks) :]
    held, outs = refs[: 5 * len(halves)], refs[5 * len(halves) + later : -8]
    near_ref, full_ref, words_ref, chosen_ref, asked_ref, in_sems, out_sems, sem = refs[-8:]
    y, x, core = place_ref[0], place_ref[1], place_ref[2]
    tiles, size = near_ref.shape[1], full_ref.shape[2]
    asking = [
        pltpu.make_async_copy(
            source.at[pl.ds(EVENT_BLOCK * ROWS, tiles), :], near_ref.at[i], in_sems.at[i]
        )
        for i, source in enumerate(sources)
    ]
    coming = []
    for i in range(len(halves)):
        steps = ((0, 0, size), (1, 0, size), (3, 0, size), (2, 0, size // 2), (2, size // 2, size // 2))
        for number, (step, start, length) in enumerate(steps):
            target = full_ref.at[i, step, pl.ds(start, length), :]
            which = 5 * i + number
            coming.append(pltpu.make_async_copy(held[which], target, in_sems.at[len(asks) + which]))
    for copy in asking + coming:
        copy.start()
    for i, ((half, _), copy) in enumerate(zip(asks, asking)):
        copy.wait()
        event = near_ref[i].astype(jnp.float32).astype(jnp.int32)
        words_ref[i] = event * ROWS + (event >> BLOCK_BITS) * (BLOCK_ROWS - EVENT_BLOCK * ROWS)
        for step in range(SIDE):
            back = step * (1 - 2 * core)
            tile = tile_of(y, x - back, core) if half == 0 else tile_of(y - back, x, core)
            at = i * SIDE + step
            chosen_ref[at : at + 1, :] = words_ref[i, pl.ds(tile, 1), :]
    copy = pltpu.make_async_copy(chosen_ref, asked_ref, sem)
    copy.start()
    copy.wait()
    going = []
    for i, (out_ref, blocks) in enumerate(zip(outs[: len(plan)], plan)):
        packed_ref = outs[len(plan) + i]
        for place, (half, hops, other) in enumerate(blocks):
            which, first = asks.index((half, hops)), halves.index(half)
            while len(coming) > 5 * (len(halves) - 1 - first):
                coming.pop(0).wait()
            for step in range(SIDE):
                for slot in range(SLOTS):
                    row = (place * SIDE + step) * SLOTS + slot
                    start = asked_ref[which * SIDE + step, other * SLOTS + slot]
                    packed_ref[row] = full_ref[first, step, pl.ds(pl.multiple_of(start, 16), ROWS), :]
        going.append(pltpu.make_async_copy(packed_ref, out_ref, out_sems.at[i]))
        going[i].start()
    for copy in going:
        copy.wait()


def pack(plan, place, held, after=()):
    asks = tuple(sorted({block[:2] for blocks in plan for block in blocks}))
    halves = tuple(sorted({half for half, _ in asks}))
    sources = [held[1 - half][{0: 0, 1: 2, 2: 3, 3: 1}[hops]] for half, hops in asks]
    pieces = [piece for half in halves for piece in held[half]]
    shape = lambda blocks: (len(blocks) * SIDE * SLOTS, ROWS, LANES)
    tiles = BLOCK_ROWS - EVENT_BLOCK * ROWS
    chosen = ((len(asks) * SIDE + 7) // 8 * 8, LANES)
    return pl.pallas_call(
        functools.partial(pack_kernel, plan, asks, halves, len(after)),
        in_specs=[SMEM] + [ANY] * (len(asks) + len(pieces) + len(after)),
        out_specs=[ANY] * len(plan),
        out_shape=[jax.ShapeDtypeStruct(shape(blocks), jnp.bfloat16) for blocks in plan],
        scratch_shapes=[pltpu.VMEM(shape(blocks), jnp.bfloat16) for blocks in plan]
        + [
            pltpu.VMEM((len(asks), tiles, LANES), jnp.bfloat16),
            pltpu.VMEM((len(halves), SIDE) + pieces[0].shape, jnp.bfloat16),
            pltpu.VMEM((len(asks), tiles, LANES), jnp.int32),
            pltpu.VMEM(chosen, jnp.int32),
            pltpu.SMEM(chosen, jnp.int32),
            pltpu.SemaphoreType.DMA((len(asks) + len(pieces),)),
            pltpu.SemaphoreType.DMA((len(plan),)),
            pltpu.SemaphoreType.DMA,
        ],
        compiler_params=PARAMS,
        name="pack",
    )(place, *sources, *pieces, *after)


def join_kernel(*refs):
    *parts, more_ref, out_ref = refs
    size = parts[0].shape[0] // 2
    for i, part in enumerate(parts):
        out_ref[i * size : (i + 1) * size] = part[size:]
    out_ref[len(parts) * size :] = more_ref[...]


def join(parts, more):
    length = parts[0].shape[0] // 2 * len(parts) + more.shape[0]
    return pl.pallas_call(
        join_kernel,
        in_specs=[VMEM] * (len(parts) + 1),
        out_specs=VMEM,
        out_shape=jax.ShapeDtypeStruct((length,) + more.shape[1:], more.dtype),
        compiler_params=PARAMS,
        name="join",
    )(*parts, more)


def pair_kernel(blocks, arrays, first, last, place_ref, local_ref, count_ref, table_ref, *refs):
    own, power = refs[:2], refs[2:4]
    partner = refs[4 : 4 + arrays]
    refs = refs[4 + arrays :]
    if not first:
        before_ref, refs = refs[0], refs[1:]
    out_ref, refs = refs[0], refs[1:]
    if last:
        turned_ref, refs = refs[0], refs[1:]
    cross_ref, energy_ref, factor_ref, came_ref, sems = refs
    y, x, core = place_ref[0], place_ref[1], place_ref[2]
    rows = SIDE * SLOTS
    copies = [
        pltpu.make_async_copy(partner[array].at[pl.ds(offset, rows)], came_ref.at[i], sems.at[i])
        for i, (*_, array, offset) in enumerate(blocks)
    ]
    for copy in copies:
        copy.start()
    if not first:
        out_ref[...] = before_ref[...]
    for number, (half, shift, other, *_) in enumerate(blocks):
        copies[number].wait()
        from_core = lax.rem(core + other, 2)

        def tile_at(step):
            way = 1 - 2 * from_core
            if half == 0:
                return tile_of(y - way * shift, x - way * step, from_core)
            return tile_of(y - way * step, x - way * shift, from_core)

        def one_tile(step, carry):
            tile = tile_at(step)
            live = count_ref[tile]
            for slot in range(SLOTS):
                event = local_ref[tile * SLOTS + slot]
                mine = own[half][event_rows(event), :].astype(jnp.float32)
                mine = mine.reshape(3, 2, 8, LANES)
                row = step * SLOTS + slot
                theirs = came_ref[number, row].astype(jnp.float32).reshape(3, 2, 8, LANES)
                real = jnp.sum(mine * theirs, axis=(0, 1))
                imag = jnp.sum(mine[:, 1] * theirs[:, 0] - mine[:, 0] * theirs[:, 1], axis=0)
                cross = jnp.concatenate([real, imag], -1)
                cross_ref[pl.ds(pl.multiple_of(row * 8, 8), 8), :] = cross
                energy_ref[row] = jnp.sum(theirs * theirs, axis=(0, 1))
                alive = jnp.where(slot < live, jnp.float32(2.0 / SCALE_WIDTH), jnp.float32(0))
                factor_ref[0, row] = power[half][event]
                factor_ref[1, row] = jnp.full((8, LANES), alive, jnp.float32)
            return carry

        lax.fori_loop(0, SIDE, one_tile, 0)
        corr = jnp.dot(
            cross_ref[...].astype(jnp.bfloat16), table_ref[...], preferred_element_type=jnp.float32
        ).reshape(rows, 8, 2 * LANES)
        low = lax.broadcasted_iota(jnp.int32, (rows, 8, LANES), 1) < 4
        corr = jnp.where(low, corr[..., :LANES], corr[..., LANES:])
        corr = corr + pltpu.roll(corr, 4, 1)
        energy = jnp.broadcast_to(
            jnp.sum(energy_ref[...], axis=-1, keepdims=True), (rows, 8, LANES)
        )
        energy = (energy + pltpu.roll(energy, 4, 1)) * (2.0 / SCALE_WIDTH)
        corr = corr * (lax.rsqrt(factor_ref[0] * energy + 1e-06) * factor_ref[1])
        for step in range(SIDE):
            at = pl.ds(pl.multiple_of(tile_at(jnp.int32(step)) * SLOTS, SLOTS), SLOTS)
            out_ref[at, 4 * half : 4 * half + 4, :] = corr[
                step * SLOTS : (step + 1) * SLOTS, 4 * half : 4 * half + 4
            ]
    if last:
        turned_ref[...] = jnp.sum(out_ref[...], axis=1).T


def pairs(blocks, place, local, count, table, own, power, partner, total, last):
    rows, slots = SIDE * SLOTS, local.shape[0]
    first = total is None
    out_shape = [jax.ShapeDtypeStruct((slots, 8, LAGS), jnp.float32)]
    if last:
        out_shape += [jax.ShapeDtypeStruct((LAGS, slots), jnp.float32)]
    args = [place, local, count, table, *own, *power, *partner] + ([] if first else [total])
    return pl.pallas_call(
        functools.partial(pair_kernel, blocks, len(partner), first, last),
        in_specs=[SMEM] * 3 + [VMEM] * 5 + [ANY] * len(partner) + [VMEM] * (not first),
        out_specs=[VMEM] * len(out_shape),
        out_shape=out_shape,
        scratch_shapes=[
            pltpu.VMEM((rows * 8, 2 * LANES), jnp.float32),
            pltpu.VMEM((rows, 8, LANES), jnp.float32),
            pltpu.VMEM((2, rows, 8, LANES), jnp.float32),
            pltpu.VMEM((len(blocks), rows, ROWS, LANES), jnp.bfloat16),
            pltpu.SemaphoreType.DMA((len(blocks),)),
        ],
        compiler_params=PARAMS,
        name="pairs",
    )(*args)


def hop(value, dy, dx, dcore):
    moves = []
    for y in range(SIDE):
        for x in range(SIDE):
            for core in range(2):
                way = 1 - 2 * core
                target = ((y + way * dy) % SIDE * SIDE + (x + way * dx) % SIDE) * 2 + (core + dcore) % 2
                moves.append(((y * SIDE + x) * 2 + core, target))
    return lax.ppermute(value, "tile", moves)


def on_device(waves, station_mask, pair_local, pair_remote, pair_count):
    width, tiles = waves.shape[-1], pair_remote.shape[1]
    events, stations = station_mask.shape
    groups = lax.axis_size("sta")
    here = lax.axis_index("tile")
    place = jnp.stack([here // (2 * SIDE), here // 2 % SIDE, here % 2]).astype(jnp.int32)
    local, count = pair_local.reshape(-1), pair_count.reshape(-1)

    mine = pair_remote.transpose(0, 2, 1)
    other = hop(mine, 0, 0, 1)
    own = own_spectra(waves, station_mask.T, jnp.asarray(forward_table(width)), mine, other)
    power = own_power(own)

    along = lambda half, value, hops: hop(value, *((0, hops) if half == 0 else (hops, 0)), 0)
    rings = [(half, hops) for hops in (1, SIDE - 1) for half in range(2)]
    came = [along(half, own[half], hops) for half, hops in rings]
    passed = [along(half, value, hops) for (half, hops), value in zip(rings, split(came))]
    held = [[own[half], *came[half::2], *passed[half::2]] for half in range(2)]
    across = lambda half, value, hops, other: hop(value, *((hops, 0) if half == 0 else (0, hops)), other)

    plan = tuple(((*where, 0), (*where, 1)) for where in rings)
    packed = pack(plan, place, held, [local])
    got = [across(where[0], value, where[1], 0) for value, where in zip(packed, rings)]
    distant = [(half, 2, other) for other in range(2) for half in range(2)]
    rest = pack(
        tuple((where,) for where in distant)
        + (((0, 0, 0), (1, 0, 0)), ((0, 0, 1), (1, 0, 1))),
        place,
        held,
        packed[:1],
    )
    far = [across(where[0], value, *where[1:]) for value, where in zip(rest, distant)]
    size = SIDE * SLOTS
    swapped = hop(join(got, rest[5]), 0, 0, 1)

    table = jnp.asarray(lag_table(width))
    calc = functools.partial(pairs, place=place, local=local, count=count, table=table, own=own, power=power)
    near = [(half, 0) for half in range(2)]
    blocks = tuple((half, 0, 0, 4, half * size) for half in range(2))
    blocks += tuple((*where, 0, number, 0) for number, where in enumerate(rings))
    total = calc(blocks, partner=got + [rest[4]], total=None, last=False)[0]
    blocks = tuple((*where, 1, 0, number * size) for number, where in enumerate(rings + near))
    total = calc(blocks, partner=[swapped], total=total, last=False)[0]
    blocks = tuple((*where, number, 0) for number, where in enumerate(distant))
    total, stack = calc(blocks, partner=far, total=total, last=True)

    stack = lax.all_to_all(stack, "sta", split_axis=0, concat_axis=0, tiled=True)
    stack = jnp.sum(stack.reshape(groups, LAGS // groups, -1), axis=0).T
    station_coef = total.astype(jnp.bfloat16).reshape(1, tiles, SLOTS, stations, LAGS)
    return (station_coef, stack.reshape(1, tiles, SLOTS, LAGS // groups))


def solution(mesh):
    placed = (
        P("tile", None, "sta", None),
        P("tile", "sta"),
        P("tile", None, None),
        P("tile", None, None),
        P("tile", None),
    )
    return jax.shard_map(
        on_device,
        mesh=mesh,
        in_specs=placed,
        out_specs=(P("tile", None, None, "sta", None), P("tile", None, None, "sta")),
        check_vma=False,
    )
```

```python
import functools
import math

import jax
import jax.numpy as jnp
import ml_dtypes
import numpy as np
from jax import lax
from jax.experimental import pallas as pl
from jax.experimental.pallas import tpu as pltpu
from jax.sharding import PartitionSpec as P

BAND = 256
LAGS = 128
SLOTS = 8
SIDE = 4
LANES = 128
ROWS = 48
BLOCK_BITS = 4
EVENT_BLOCK = 1 << BLOCK_BITS
BLOCK_ROWS = EVENT_BLOCK * ROWS + 32
SCALE_WIDTH = 1024.0
VMEM = pl.BlockSpec(memory_space=pltpu.VMEM)
ANY = pl.BlockSpec(memory_space=pl.ANY)
SMEM = pl.BlockSpec(memory_space=pltpu.SMEM)
PARAMS = pltpu.CompilerParams(vmem_limit_bytes=24 * 1024 * 1024)


def forward_table(width):
    phase = np.arange(width)[:, None] * np.arange(1, BAND + 1)[None, :] % width * (2.0 * math.pi / width)
    return np.concatenate([np.cos(phase), -np.sin(phase)], 1).astype(ml_dtypes.bfloat16)


def lag_table(width):
    phase = np.arange(1, BAND + 1)[:, None] * (np.arange(LAGS)[None, :] - LAGS // 2) % width
    phase = phase * (2.0 * math.pi / width)
    table = np.concatenate([np.cos(phase), -np.sin(phase)], 0).astype(ml_dtypes.bfloat16)
    low_re, high_re, low_im, high_im = (table[i * LANES : (i + 1) * LANES] for i in range(4))
    return np.concatenate(
        [np.concatenate([low_re, high_re], 1), np.concatenate([low_im, high_im], 1)], 0
    )


def spectra_kernel(waves_ref, mask_ref, table_ref, mine_ref, other_ref, *refs):
    outs, (came_ref, factors_ref, sems) = refs[:2], refs[2:]
    rows = EVENT_BLOCK * 24
    blocks = waves_ref.shape[0] // rows
    copies = [pltpu.make_async_copy(table_ref, factors_ref, sems.at[blocks])]
    copies += [
        pltpu.make_async_copy(waves_ref.at[pl.ds(i * rows, rows), :], came_ref.at[i], sems.at[i])
        for i in range(blocks)
    ]
    for copy in copies:
        copy.start()
    same = lax.broadcasted_iota(jnp.int32, (1, 8, 8), 1) == lax.broadcasted_iota(jnp.int32, (1, 8, 8), 2)
    mine, other = mine_ref[0], other_ref[0]
    blank = jnp.zeros((mine.shape[0], LANES - 2 * SLOTS), mine.dtype)
    asked = jnp.concatenate([mine, other, blank], 1).astype(jnp.float32).astype(jnp.bfloat16)
    copies[0].wait()
    low = lax.broadcasted_iota(jnp.int32, (EVENT_BLOCK * 3, 8, LANES), 1) < 4
    for block in range(blocks):
        mask = mask_ref[block * EVENT_BLOCK : (block + 1) * EVENT_BLOCK, :].astype(jnp.float32)
        mask = jnp.sum(jnp.where(same, mask[:, None, :], 0.0), axis=-1, keepdims=True)[:, None]
        copies[block + 1].wait()
        flat = jnp.dot(came_ref[block], factors_ref[...], preferred_element_type=jnp.float32)
        flat = flat.reshape(EVENT_BLOCK, 3, 8, 4 * LANES) * mask
        part = [
            flat[..., i * LANES : (i + 1) * LANES].reshape(EVENT_BLOCK * 3, 8, LANES)
            for i in range(4)
        ]
        turned = [pltpu.roll(value, 4, 1) for value in part]
        halves = (
            (jnp.where(low, part[0], turned[1]), jnp.where(low, part[2], turned[3])),
            (jnp.where(low, turned[0], part[1]), jnp.where(low, turned[2], part[3])),
        )
        first, last = block * BLOCK_ROWS, block * BLOCK_ROWS + EVENT_BLOCK * ROWS
        for (real, imag), out_ref in zip(halves, outs):
            packed = jnp.concatenate([real, imag], 1).astype(jnp.bfloat16)
            out_ref[first:last, :] = packed.reshape(EVENT_BLOCK * ROWS, LANES)
            out_ref[last : first + BLOCK_ROWS, :] = asked


def own_spectra(waves, mask, table, mine, other):
    flat = waves.reshape(-1, waves.shape[-1])
    blocks = mask.shape[0] // EVENT_BLOCK
    half = jax.ShapeDtypeStruct((blocks * BLOCK_ROWS, LANES), jnp.bfloat16)
    return pl.pallas_call(
        spectra_kernel,
        in_specs=[ANY, VMEM, ANY, VMEM, VMEM],
        out_specs=[VMEM] * 2,
        out_shape=[half, half],
        scratch_shapes=[
            pltpu.VMEM((blocks, flat.shape[0] // blocks, flat.shape[1]), flat.dtype),
            pltpu.VMEM(table.shape, table.dtype),
            pltpu.SemaphoreType.DMA((blocks + 1,)),
        ],
        compiler_params=PARAMS,
        name="spectra",
    )(flat, mask, table, mine, other)


def power_kernel(first_ref, second_ref, *outs):
    for spectra_ref, out_ref in zip((first_ref, second_ref), outs):
        for block in range(out_ref.shape[0] // EVENT_BLOCK):
            start = block * BLOCK_ROWS
            values = spectra_ref[start : start + EVENT_BLOCK * ROWS, :].astype(jnp.float32)
            values = values.reshape(EVENT_BLOCK, 3, 2, 8, LANES)
            total = jnp.sum(jnp.sum(values * values, axis=(1, 2)), axis=-1, keepdims=True)
            total = jnp.broadcast_to(total, (EVENT_BLOCK, 8, LANES))
            total = (total + pltpu.roll(total, 4, 1)) * (2.0 / SCALE_WIDTH)
            out_ref[block * EVENT_BLOCK : (block + 1) * EVENT_BLOCK] = total


def own_power(own):
    events = own[0].shape[0] // BLOCK_ROWS * EVENT_BLOCK
    return pl.pallas_call(
        power_kernel,
        in_specs=[VMEM] * 2,
        out_specs=[VMEM] * 2,
        out_shape=[jax.ShapeDtypeStruct((events, 8, LANES), jnp.float32)] * 2,
        compiler_params=PARAMS,
        name="power",
    )(*own)


def split(values):
    rows = values[0].shape[0]
    part = lambda i: pl.BlockSpec((rows // 2, LANES), lambda _: (2 * i // len(values), 0))
    whole = pl.BlockSpec((rows // 2, LANES), lambda _: (0, 0))

    def kernel(*refs):
        for in_ref, out_ref in zip(refs[: len(values)], refs[len(values) :]):
            out_ref[...] = in_ref[...]

    return pl.pallas_call(
        kernel,
        grid=(1,),
        in_specs=[part(i) for i in range(len(values))],
        out_specs=[whole] * len(values),
        out_shape=[jax.ShapeDtypeStruct((rows // 2, LANES), values[0].dtype)] * len(values),
        compiler_params=PARAMS,
        name="split",
    )(*values)


def event_rows(event):
    start = event * ROWS + (event >> BLOCK_BITS) * (BLOCK_ROWS - EVENT_BLOCK * ROWS)
    return pl.ds(pl.multiple_of(start, 16), ROWS)


def tile_of(y, x, core):
    return (lax.rem(y + SIDE, SIDE) * SIDE + lax.rem(x + SIDE, SIDE)) * 2 + core


def pack_kernel(plan, asks, halves, later, place_ref, *refs):
    sources, refs = refs[: len(asks)], refs[len(asks) :]
    held, outs = refs[: 5 * len(halves)], refs[5 * len(halves) + later : -8]
    near_ref, full_ref, words_ref, chosen_ref, asked_ref, in_sems, out_sems, sem = refs[-8:]
    y, x, core = place_ref[0], place_ref[1], place_ref[2]
    tiles, size = near_ref.shape[1], full_ref.shape[2]
    asking = [
        pltpu.make_async_copy(
            source.at[pl.ds(EVENT_BLOCK * ROWS, tiles), :], near_ref.at[i], in_sems.at[i]
        )
        for i, source in enumerate(sources)
    ]
    coming = []
    for i in range(len(halves)):
        steps = ((0, 0, size), (1, 0, size), (3, 0, size), (2, 0, size // 2), (2, size // 2, size // 2))
        for number, (step, start, length) in enumerate(steps):
            target = full_ref.at[i, step, pl.ds(start, length), :]
            which = 5 * i + number
            coming.append(pltpu.make_async_copy(held[which], target, in_sems.at[len(asks) + which]))
    for copy in asking + coming:
        copy.start()
    for i, ((half, _), copy) in enumerate(zip(asks, asking)):
        copy.wait()
        event = near_ref[i].astype(jnp.float32).astype(jnp.int32)
        words_ref[i] = event * ROWS + (event >> BLOCK_BITS) * (BLOCK_ROWS - EVENT_BLOCK * ROWS)
        for step in range(SIDE):
            back = step * (1 - 2 * core)
            tile = tile_of(y, x - back, core) if half == 0 else tile_of(y - back, x, core)
            at = i * SIDE + step
            chosen_ref[at : at + 1, :] = words_ref[i, pl.ds(tile, 1), :]
    copy = pltpu.make_async_copy(chosen_ref, asked_ref, sem)
    copy.start()
    copy.wait()
    going = []
    for i, (out_ref, blocks) in enumerate(zip(outs[: len(plan)], plan)):
        packed_ref = outs[len(plan) + i]
        for place, (half, hops, other) in enumerate(blocks):
            which, first = asks.index((half, hops)), halves.index(half)
            while len(coming) > 5 * (len(halves) - 1 - first):
                coming.pop(0).wait()
            for step in range(SIDE):
                for slot in range(SLOTS):
                    row = (place * SIDE + step) * SLOTS + slot
                    start = asked_ref[which * SIDE + step, other * SLOTS + slot]
                    packed_ref[row] = full_ref[first, step, pl.ds(pl.multiple_of(start, 16), ROWS), :]
        going.append(pltpu.make_async_copy(packed_ref, out_ref, out_sems.at[i]))
        going[i].start()
    for copy in going:
        copy.wait()


def pack(plan, place, held, after=()):
    asks = tuple(sorted({block[:2] for blocks in plan for block in blocks}))
    halves = tuple(sorted({half for half, _ in asks}))
    sources = [held[1 - half][{0: 0, 1: 2, 2: 3, 3: 1}[hops]] for half, hops in asks]
    pieces = [piece for half in halves for piece in held[half]]
    shape = lambda blocks: (len(blocks) * SIDE * SLOTS, ROWS, LANES)
    tiles = BLOCK_ROWS - EVENT_BLOCK * ROWS
    chosen = ((len(asks) * SIDE + 7) // 8 * 8, LANES)
    return pl.pallas_call(
        functools.partial(pack_kernel, plan, asks, halves, len(after)),
        in_specs=[SMEM] + [ANY] * (len(asks) + len(pieces) + len(after)),
        out_specs=[ANY] * len(plan),
        out_shape=[jax.ShapeDtypeStruct(shape(blocks), jnp.bfloat16) for blocks in plan],
        scratch_shapes=[pltpu.VMEM(shape(blocks), jnp.bfloat16) for blocks in plan]
        + [
            pltpu.VMEM((len(asks), tiles, LANES), jnp.bfloat16),
            pltpu.VMEM((len(halves), SIDE) + pieces[0].shape, jnp.bfloat16),
            pltpu.VMEM((len(asks), tiles, LANES), jnp.int32),
            pltpu.VMEM(chosen, jnp.int32),
            pltpu.SMEM(chosen, jnp.int32),
            pltpu.SemaphoreType.DMA((len(asks) + len(pieces),)),
            pltpu.SemaphoreType.DMA((len(plan),)),
            pltpu.SemaphoreType.DMA,
        ],
        compiler_params=PARAMS,
        name="pack",
    )(place, *sources, *pieces, *after)


def join_kernel(*refs):
    *parts, more_ref, out_ref = refs
    size = parts[0].shape[0] // 2
    for i, part in enumerate(parts):
        out_ref[i * size : (i + 1) * size] = part[size:]
    out_ref[len(parts) * size :] = more_ref[...]


def join(parts, more):
    length = parts[0].shape[0] // 2 * len(parts) + more.shape[0]
    return pl.pallas_call(
        join_kernel,
        in_specs=[VMEM] * (len(parts) + 1),
        out_specs=VMEM,
        out_shape=jax.ShapeDtypeStruct((length,) + more.shape[1:], more.dtype),
        compiler_params=PARAMS,
        name="join",
    )(*parts, more)


def pair_kernel(blocks, arrays, first, last, place_ref, local_ref, count_ref, table_ref, *refs):
    own, power = refs[:2], refs[2:4]
    partner = refs[4 : 4 + arrays]
    refs = refs[4 + arrays :]
    if not first:
        before_ref, refs = refs[0], refs[1:]
    out_ref, refs = refs[0], refs[1:]
    if last:
        turned_ref, refs = refs[0], refs[1:]
    cross_ref, energy_ref, factor_ref, came_ref, sems = refs
    y, x, core = place_ref[0], place_ref[1], place_ref[2]
    rows = SIDE * SLOTS
    copies = [
        pltpu.make_async_copy(partner[array].at[pl.ds(offset, rows)], came_ref.at[i], sems.at[i])
        for i, (*_, array, offset) in enumerate(blocks)
    ]
    for copy in copies:
        copy.start()
    if not first:
        out_ref[...] = before_ref[...]
    for number, (half, shift, other, *_) in enumerate(blocks):
        copies[number].wait()
        from_core = lax.rem(core + other, 2)

        def tile_at(step):
            way = 1 - 2 * from_core
            if half == 0:
                return tile_of(y - way * shift, x - way * step, from_core)
            return tile_of(y - way * step, x - way * shift, from_core)

        def one_tile(step, carry):
            tile = tile_at(step)
            live = count_ref[tile]
            for slot in range(SLOTS):
                event = local_ref[tile * SLOTS + slot]
                mine = own[half][event_rows(event), :].astype(jnp.float32)
                mine = mine.reshape(3, 2, 8, LANES)
                row = step * SLOTS + slot
                theirs = came_ref[number, row].astype(jnp.float32).reshape(3, 2, 8, LANES)
                real = jnp.sum(mine * theirs, axis=(0, 1))
                imag = jnp.sum(mine[:, 1] * theirs[:, 0] - mine[:, 0] * theirs[:, 1], axis=0)
                cross = jnp.concatenate([real, imag], -1)
                cross_ref[pl.ds(pl.multiple_of(row * 8, 8), 8), :] = cross
                energy_ref[row] = jnp.sum(theirs * theirs, axis=(0, 1))
                alive = jnp.where(slot < live, jnp.float32(2.0 / SCALE_WIDTH), jnp.float32(0))
                factor_ref[0, row] = power[half][event]
                factor_ref[1, row] = jnp.full((8, LANES), alive, jnp.float32)
            return carry

        lax.fori_loop(0, SIDE, one_tile, 0)
        corr = jnp.dot(
            cross_ref[...].astype(jnp.bfloat16), table_ref[...], preferred_element_type=jnp.float32
        ).reshape(rows, 8, 2 * LANES)
        low = lax.broadcasted_iota(jnp.int32, (rows, 8, LANES), 1) < 4
        corr = jnp.where(low, corr[..., :LANES], corr[..., LANES:])
        corr = corr + pltpu.roll(corr, 4, 1)
        energy = jnp.broadcast_to(
            jnp.sum(energy_ref[...], axis=-1, keepdims=True), (rows, 8, LANES)
        )
        energy = (energy + pltpu.roll(energy, 4, 1)) * (2.0 / SCALE_WIDTH)
        corr = corr * (lax.rsqrt(factor_ref[0] * energy + 1e-06) * factor_ref[1])
        for step in range(SIDE):
            at = pl.ds(pl.multiple_of(tile_at(jnp.int32(step)) * SLOTS, SLOTS), SLOTS)
            out_ref[at, 4 * half : 4 * half + 4, :] = corr[
                step * SLOTS : (step + 1) * SLOTS, 4 * half : 4 * half + 4
            ]
    if last:
        turned_ref[...] = jnp.sum(out_ref[...], axis=1).T


def pairs(blocks, place, local, count, table, own, power, partner, total, last):
    rows, slots = SIDE * SLOTS, local.shape[0]
    first = total is None
    out_shape = [jax.ShapeDtypeStruct((slots, 8, LAGS), jnp.float32)]
    if last:
        out_shape += [jax.ShapeDtypeStruct((LAGS, slots), jnp.float32)]
    args = [place, local, count, table, *own, *power, *partner] + ([] if first else [total])
    return pl.pallas_call(
        functools.partial(pair_kernel, blocks, len(partner), first, last),
        in_specs=[SMEM] * 3 + [VMEM] * 5 + [ANY] * len(partner) + [VMEM] * (not first),
        out_specs=[VMEM] * len(out_shape),
        out_shape=out_shape,
        scratch_shapes=[
            pltpu.VMEM((rows * 8, 2 * LANES), jnp.float32),
            pltpu.VMEM((rows, 8, LANES), jnp.float32),
            pltpu.VMEM((2, rows, 8, LANES), jnp.float32),
            pltpu.VMEM((len(blocks), rows, ROWS, LANES), jnp.bfloat16),
            pltpu.SemaphoreType.DMA((len(blocks),)),
        ],
        compiler_params=PARAMS,
        name="pairs",
    )(*args)


def hop(value, dy, dx, dcore):
    moves = []
    for y in range(SIDE):
        for x in range(SIDE):
            for core in range(2):
                way = 1 - 2 * core
                target = ((y + way * dy) % SIDE * SIDE + (x + way * dx) % SIDE) * 2 + (core + dcore) % 2
                moves.append(((y * SIDE + x) * 2 + core, target))
    return lax.ppermute(value, "tile", moves)


def on_device(waves, station_mask, pair_local, pair_remote, pair_count):
    width, tiles = waves.shape[-1], pair_remote.shape[1]
    events, stations = station_mask.shape
    groups = lax.axis_size("sta")
    here = lax.axis_index("tile")
    place = jnp.stack([here // (2 * SIDE), here // 2 % SIDE, here % 2]).astype(jnp.int32)
    local, count = pair_local.reshape(-1), pair_count.reshape(-1)

    other = hop(pair_remote, 0, 0, 1)
    own = own_spectra(waves, station_mask, jnp.asarray(forward_table(width)), pair_remote, other)
    power = own_power(own)

    along = lambda half, value, hops: hop(value, *((0, hops) if half == 0 else (hops, 0)), 0)
    rings = [(half, hops) for hops in (1, SIDE - 1) for half in range(2)]
    came = [along(half, own[half], hops) for half, hops in rings]
    passed = [along(half, value, hops) for (half, hops), value in zip(rings, split(came))]
    held = [[own[half], *came[half::2], *passed[half::2]] for half in range(2)]
    across = lambda half, value, hops, other: hop(value, *((hops, 0) if half == 0 else (0, hops)), other)

    plan = tuple(((*where, 0), (*where, 1)) for where in rings)
    packed = pack(plan, place, held, [local])
    got = [across(where[0], value, where[1], 0) for value, where in zip(packed, rings)]
    distant = [(half, 2, other) for other in range(2) for half in range(2)]
    rest = pack(
        tuple((where,) for where in distant)
        + (((0, 0, 0), (1, 0, 0)), ((0, 0, 1), (1, 0, 1))),
        place,
        held,
        packed[:1],
    )
    far = [across(where[0], value, *where[1:]) for value, where in zip(rest, distant)]
    size = SIDE * SLOTS
    swapped = hop(join(got, rest[5]), 0, 0, 1)

    table = jnp.asarray(lag_table(width))
    calc = functools.partial(pairs, place=place, local=local, count=count, table=table, own=own, power=power)
    near = [(half, 0) for half in range(2)]
    blocks = tuple((half, 0, 0, 4, half * size) for half in range(2))
    blocks += tuple((*where, 0, number, 0) for number, where in enumerate(rings))
    total = calc(blocks, partner=got + [rest[4]], total=None, last=False)[0]
    blocks = tuple((*where, 1, 0, number * size) for number, where in enumerate(rings + near))
    total = calc(blocks, partner=[swapped], total=total, last=False)[0]
    blocks = tuple((*where, number, 0) for number, where in enumerate(distant))
    total, stack = calc(blocks, partner=far, total=total, last=True)

    stack = lax.all_to_all(stack, "sta", split_axis=0, concat_axis=0, tiled=True)
    stack = jnp.sum(stack.reshape(groups, LAGS // groups, -1), axis=0).T
    station_coef = total.astype(jnp.bfloat16).reshape(1, tiles, SLOTS, stations, LAGS)
    return (station_coef, stack.reshape(1, tiles, SLOTS, LAGS // groups))


def solution(mesh):
    placed = (
        P("tile", None, "sta", None),
        P("tile", "sta"),
        P("tile", None, None),
        P("tile", None, None),
        P("tile", None),
    )
    return jax.shard_map(
        on_device,
        mesh=mesh,
        in_specs=placed,
        out_specs=(P("tile", None, None, "sta", None), P("tile", None, None, "sta")),
        check_vma=False,
    )
```

```python
import functools
import math

import jax
import jax.numpy as jnp
import ml_dtypes
import numpy as np
from jax import lax
from jax.experimental import pallas as pl
from jax.experimental.pallas import tpu as pltpu
from jax.sharding import PartitionSpec as P

BAND = 256
LAGS = 128
SLOTS = 8
SIDE = 4
LANES = 128
ROWS = 48
BLOCK_BITS = 5
EVENT_BLOCK = 1 << BLOCK_BITS
BLOCK_ROWS = EVENT_BLOCK * ROWS + 32
SCALE_WIDTH = 1024.0
VMEM = pl.BlockSpec(memory_space=pltpu.VMEM)
ANY = pl.BlockSpec(memory_space=pl.ANY)
SMEM = pl.BlockSpec(memory_space=pltpu.SMEM)
PARAMS = pltpu.CompilerParams(vmem_limit_bytes=24 * 1024 * 1024)


def forward_table(width):
    phase = np.arange(width)[:, None] * np.arange(1, BAND + 1)[None, :] % width * (2.0 * math.pi / width)
    return np.concatenate([np.cos(phase), -np.sin(phase)], 1).astype(ml_dtypes.bfloat16)


def lag_table(width):
    phase = np.arange(1, BAND + 1)[:, None] * (np.arange(LAGS)[None, :] - LAGS // 2) % width
    phase = phase * (2.0 * math.pi / width)
    table = np.concatenate([np.cos(phase), -np.sin(phase)], 0).astype(ml_dtypes.bfloat16)
    low_re, high_re, low_im, high_im = (table[i * LANES : (i + 1) * LANES] for i in range(4))
    return np.concatenate(
        [np.concatenate([low_re, high_re], 1), np.concatenate([low_im, high_im], 1)], 0
    )


def spectra_kernel(waves_ref, mask_ref, table_ref, mine_ref, other_ref, *refs):
    outs, (came_ref, factors_ref, sems) = refs[:2], refs[2:]
    rows = EVENT_BLOCK * 24
    blocks = waves_ref.shape[0] // rows
    copies = [pltpu.make_async_copy(table_ref, factors_ref, sems.at[blocks])]
    copies += [
        pltpu.make_async_copy(waves_ref.at[pl.ds(i * rows, rows), :], came_ref.at[i], sems.at[i])
        for i in range(blocks)
    ]
    for copy in copies:
        copy.start()
    same = lax.broadcasted_iota(jnp.int32, (1, 8, 8), 1) == lax.broadcasted_iota(jnp.int32, (1, 8, 8), 2)
    mine, other = mine_ref[0], other_ref[0]
    blank = jnp.zeros((mine.shape[0], LANES - 2 * SLOTS), mine.dtype)
    asked = jnp.concatenate([mine, other, blank], 1).astype(jnp.float32).astype(jnp.bfloat16)
    copies[0].wait()
    low = lax.broadcasted_iota(jnp.int32, (EVENT_BLOCK * 3, 8, LANES), 1) < 4
    for block in range(blocks):
        mask = mask_ref[block * EVENT_BLOCK : (block + 1) * EVENT_BLOCK, :].astype(jnp.float32)
        mask = jnp.sum(jnp.where(same, mask[:, None, :], 0.0), axis=-1, keepdims=True)[:, None]
        copies[block + 1].wait()
        flat = jnp.dot(came_ref[block], factors_ref[...], preferred_element_type=jnp.float32)
        flat = flat.reshape(EVENT_BLOCK, 3, 8, 4 * LANES) * mask
        part = [
            flat[..., i * LANES : (i + 1) * LANES].reshape(EVENT_BLOCK * 3, 8, LANES)
            for i in range(4)
        ]
        turned = [pltpu.roll(value, 4, 1) for value in part]
        halves = (
            (jnp.where(low, part[0], turned[1]), jnp.where(low, part[2], turned[3])),
            (jnp.where(low, turned[0], part[1]), jnp.where(low, turned[2], part[3])),
        )
        first, last = block * BLOCK_ROWS, block * BLOCK_ROWS + EVENT_BLOCK * ROWS
        for (real, imag), out_ref in zip(halves, outs):
            packed = jnp.concatenate([real, imag], 1).astype(jnp.bfloat16)
            out_ref[first:last, :] = packed.reshape(EVENT_BLOCK * ROWS, LANES)
            out_ref[last : first + BLOCK_ROWS, :] = asked


def own_spectra(waves, mask, table, mine, other):
    flat = waves.reshape(-1, waves.shape[-1])
    blocks = mask.shape[0] // EVENT_BLOCK
    half = jax.ShapeDtypeStruct((blocks * BLOCK_ROWS, LANES), jnp.bfloat16)
    return pl.pallas_call(
        spectra_kernel,
        in_specs=[ANY, VMEM, ANY, VMEM, VMEM],
        out_specs=[VMEM] * 2,
        out_shape=[half, half],
        scratch_shapes=[
            pltpu.VMEM((blocks, flat.shape[0] // blocks, flat.shape[1]), flat.dtype),
            pltpu.VMEM(table.shape, table.dtype),
            pltpu.SemaphoreType.DMA((blocks + 1,)),
        ],
        compiler_params=PARAMS,
        name="spectra",
    )(flat, mask, table, mine, other)


def power_kernel(first_ref, second_ref, *outs):
    for spectra_ref, out_ref in zip((first_ref, second_ref), outs):
        for block in range(out_ref.shape[0] // EVENT_BLOCK):
            start = block * BLOCK_ROWS
            values = spectra_ref[start : start + EVENT_BLOCK * ROWS, :].astype(jnp.float32)
            values = values.reshape(EVENT_BLOCK, 3, 2, 8, LANES)
            total = jnp.sum(jnp.sum(values * values, axis=(1, 2)), axis=-1, keepdims=True)
            total = jnp.broadcast_to(total, (EVENT_BLOCK, 8, LANES))
            total = (total + pltpu.roll(total, 4, 1)) * (2.0 / SCALE_WIDTH)
            out_ref[block * EVENT_BLOCK : (block + 1) * EVENT_BLOCK] = total


def own_power(own):
    events = own[0].shape[0] // BLOCK_ROWS * EVENT_BLOCK
    return pl.pallas_call(
        power_kernel,
        in_specs=[VMEM] * 2,
        out_specs=[VMEM] * 2,
        out_shape=[jax.ShapeDtypeStruct((events, 8, LANES), jnp.float32)] * 2,
        compiler_params=PARAMS,
        name="power",
    )(*own)


def split(values):
    rows = values[0].shape[0]
    part = lambda i: pl.BlockSpec((rows // 2, LANES), lambda _: (2 * i // len(values), 0))
    whole = pl.BlockSpec((rows // 2, LANES), lambda _: (0, 0))

    def kernel(*refs):
        for in_ref, out_ref in zip(refs[: len(values)], refs[len(values) :]):
            out_ref[...] = in_ref[...]

    return pl.pallas_call(
        kernel,
        grid=(1,),
        in_specs=[part(i) for i in range(len(values))],
        out_specs=[whole] * len(values),
        out_shape=[jax.ShapeDtypeStruct((rows // 2, LANES), values[0].dtype)] * len(values),
        compiler_params=PARAMS,
        name="split",
    )(*values)


def event_rows(event):
    start = event * ROWS + (event >> BLOCK_BITS) * (BLOCK_ROWS - EVENT_BLOCK * ROWS)
    return pl.ds(pl.multiple_of(start, 16), ROWS)


def tile_of(y, x, core):
    return (lax.rem(y + SIDE, SIDE) * SIDE + lax.rem(x + SIDE, SIDE)) * 2 + core


def pack_kernel(plan, asks, halves, later, place_ref, *refs):
    sources, refs = refs[: len(asks)], refs[len(asks) :]
    held, outs = refs[: 5 * len(halves)], refs[5 * len(halves) + later : -8]
    near_ref, full_ref, words_ref, chosen_ref, asked_ref, in_sems, out_sems, sem = refs[-8:]
    y, x, core = place_ref[0], place_ref[1], place_ref[2]
    tiles, size = near_ref.shape[1], full_ref.shape[2]
    asking = [
        pltpu.make_async_copy(
            source.at[pl.ds(EVENT_BLOCK * ROWS, tiles), :], near_ref.at[i], in_sems.at[i]
        )
        for i, source in enumerate(sources)
    ]
    coming = []
    for i in range(len(halves)):
        steps = ((0, 0, size), (1, 0, size), (3, 0, size), (2, 0, size // 2), (2, size // 2, size // 2))
        for number, (step, start, length) in enumerate(steps):
            target = full_ref.at[i, step, pl.ds(start, length), :]
            which = 5 * i + number
            coming.append(pltpu.make_async_copy(held[which], target, in_sems.at[len(asks) + which]))
    for copy in asking + coming:
        copy.start()
    for i, ((half, _), copy) in enumerate(zip(asks, asking)):
        copy.wait()
        event = near_ref[i].astype(jnp.float32).astype(jnp.int32)
        words_ref[i] = event * ROWS + (event >> BLOCK_BITS) * (BLOCK_ROWS - EVENT_BLOCK * ROWS)
        for step in range(SIDE):
            back = step * (1 - 2 * core)
            tile = tile_of(y, x - back, core) if half == 0 else tile_of(y - back, x, core)
            at = i * SIDE + step
            chosen_ref[at : at + 1, :] = words_ref[i, pl.ds(tile, 1), :]
    copy = pltpu.make_async_copy(chosen_ref, asked_ref, sem)
    copy.start()
    copy.wait()
    going = []
    for i, (out_ref, blocks) in enumerate(zip(outs[: len(plan)], plan)):
        packed_ref = outs[len(plan) + i]
        for place, (half, hops, other) in enumerate(blocks):
            which, first = asks.index((half, hops)), halves.index(half)
            while len(coming) > 5 * (len(halves) - 1 - first):
                coming.pop(0).wait()
            for step in range(SIDE):
                for slot in range(SLOTS):
                    row = (place * SIDE + step) * SLOTS + slot
                    start = asked_ref[which * SIDE + step, other * SLOTS + slot]
                    packed_ref[row] = full_ref[first, step, pl.ds(pl.multiple_of(start, 16), ROWS), :]
        going.append(pltpu.make_async_copy(packed_ref, out_ref, out_sems.at[i]))
        going[i].start()
    for copy in going:
        copy.wait()


def pack(plan, place, held, after=()):
    asks = tuple(sorted({block[:2] for blocks in plan for block in blocks}))
    halves = tuple(sorted({half for half, _ in asks}))
    sources = [held[1 - half][{0: 0, 1: 2, 2: 3, 3: 1}[hops]] for half, hops in asks]
    pieces = [piece for half in halves for piece in held[half]]
    shape = lambda blocks: (len(blocks) * SIDE * SLOTS, ROWS, LANES)
    tiles = BLOCK_ROWS - EVENT_BLOCK * ROWS
    chosen = ((len(asks) * SIDE + 7) // 8 * 8, LANES)
    return pl.pallas_call(
        functools.partial(pack_kernel, plan, asks, halves, len(after)),
        in_specs=[SMEM] + [ANY] * (len(asks) + len(pieces) + len(after)),
        out_specs=[ANY] * len(plan),
        out_shape=[jax.ShapeDtypeStruct(shape(blocks), jnp.bfloat16) for blocks in plan],
        scratch_shapes=[pltpu.VMEM(shape(blocks), jnp.bfloat16) for blocks in plan]
        + [
            pltpu.VMEM((len(asks), tiles, LANES), jnp.bfloat16),
            pltpu.VMEM((len(halves), SIDE) + pieces[0].shape, jnp.bfloat16),
            pltpu.VMEM((len(asks), tiles, LANES), jnp.int32),
            pltpu.VMEM(chosen, jnp.int32),
            pltpu.SMEM(chosen, jnp.int32),
            pltpu.SemaphoreType.DMA((len(asks) + len(pieces),)),
            pltpu.SemaphoreType.DMA((len(plan),)),
            pltpu.SemaphoreType.DMA,
        ],
        compiler_params=PARAMS,
        name="pack",
    )(place, *sources, *pieces, *after)


def join_kernel(*refs):
    *parts, more_ref, out_ref = refs
    size = parts[0].shape[0] // 2
    for i, part in enumerate(parts):
        out_ref[i * size : (i + 1) * size] = part[size:]
    out_ref[len(parts) * size :] = more_ref[...]


def join(parts, more):
    length = parts[0].shape[0] // 2 * len(parts) + more.shape[0]
    return pl.pallas_call(
        join_kernel,
        in_specs=[VMEM] * (len(parts) + 1),
        out_specs=VMEM,
        out_shape=jax.ShapeDtypeStruct((length,) + more.shape[1:], more.dtype),
        compiler_params=PARAMS,
        name="join",
    )(*parts, more)


def pair_kernel(blocks, arrays, first, last, place_ref, local_ref, count_ref, table_ref, *refs):
    own, power = refs[:2], refs[2:4]
    partner = refs[4 : 4 + arrays]
    refs = refs[4 + arrays :]
    if not first:
        before_ref, refs = refs[0], refs[1:]
    out_ref, refs = refs[0], refs[1:]
    if last:
        turned_ref, refs = refs[0], refs[1:]
    cross_ref, energy_ref, factor_ref, came_ref, sems = refs
    y, x, core = place_ref[0], place_ref[1], place_ref[2]
    rows = SIDE * SLOTS
    copies = [
        pltpu.make_async_copy(partner[array].at[pl.ds(offset, rows)], came_ref.at[i], sems.at[i])
        for i, (*_, array, offset) in enumerate(blocks)
    ]
    for copy in copies:
        copy.start()
    if not first:
        out_ref[...] = before_ref[...]
    for number, (half, shift, other, *_) in enumerate(blocks):
        copies[number].wait()
        from_core = lax.rem(core + other, 2)

        def tile_at(step):
            way = 1 - 2 * from_core
            if half == 0:
                return tile_of(y - way * shift, x - way * step, from_core)
            return tile_of(y - way * step, x - way * shift, from_core)

        def one_tile(step, carry):
            tile = tile_at(step)
            live = count_ref[tile]
            for slot in range(SLOTS):
                event = local_ref[tile * SLOTS + slot]
                mine = own[half][event_rows(event), :].astype(jnp.float32)
                mine = mine.reshape(3, 2, 8, LANES)
                row = step * SLOTS + slot
                theirs = came_ref[number, row].astype(jnp.float32).reshape(3, 2, 8, LANES)
                real = jnp.sum(mine * theirs, axis=(0, 1))
                imag = jnp.sum(mine[:, 1] * theirs[:, 0] - mine[:, 0] * theirs[:, 1], axis=0)
                cross = jnp.concatenate([real, imag], -1)
                cross_ref[pl.ds(pl.multiple_of(row * 8, 8), 8), :] = cross
                energy_ref[row] = jnp.sum(theirs * theirs, axis=(0, 1))
                alive = jnp.where(slot < live, jnp.float32(2.0 / SCALE_WIDTH), jnp.float32(0))
                factor_ref[0, row] = power[half][event]
                factor_ref[1, row] = jnp.full((8, LANES), alive, jnp.float32)
            return carry

        lax.fori_loop(0, SIDE, one_tile, 0)
        corr = jnp.dot(
            cross_ref[...].astype(jnp.bfloat16), table_ref[...], preferred_element_type=jnp.float32
        ).reshape(rows, 8, 2 * LANES)
        low = lax.broadcasted_iota(jnp.int32, (rows, 8, LANES), 1) < 4
        corr = jnp.where(low, corr[..., :LANES], corr[..., LANES:])
        corr = corr + pltpu.roll(corr, 4, 1)
        energy = jnp.broadcast_to(
            jnp.sum(energy_ref[...], axis=-1, keepdims=True), (rows, 8, LANES)
        )
        energy = (energy + pltpu.roll(energy, 4, 1)) * (2.0 / SCALE_WIDTH)
        corr = corr * (lax.rsqrt(factor_ref[0] * energy + 1e-06) * factor_ref[1])
        for step in range(SIDE):
            at = pl.ds(pl.multiple_of(tile_at(jnp.int32(step)) * SLOTS, SLOTS), SLOTS)
            out_ref[at, 4 * half : 4 * half + 4, :] = corr[
                step * SLOTS : (step + 1) * SLOTS, 4 * half : 4 * half + 4
            ]
    if last:
        turned_ref[...] = jnp.sum(out_ref[...], axis=1).T


def pairs(blocks, place, local, count, table, own, power, partner, total, last):
    rows, slots = SIDE * SLOTS, local.shape[0]
    first = total is None
    out_shape = [jax.ShapeDtypeStruct((slots, 8, LAGS), jnp.float32)]
    if last:
        out_shape += [jax.ShapeDtypeStruct((LAGS, slots), jnp.float32)]
    args = [place, local, count, table, *own, *power, *partner] + ([] if first else [total])
    return pl.pallas_call(
        functools.partial(pair_kernel, blocks, len(partner), first, last),
        in_specs=[SMEM] * 3 + [VMEM] * 5 + [ANY] * len(partner) + [VMEM] * (not first),
        out_specs=[VMEM] * len(out_shape),
        out_shape=out_shape,
        scratch_shapes=[
            pltpu.VMEM((rows * 8, 2 * LANES), jnp.float32),
            pltpu.VMEM((rows, 8, LANES), jnp.float32),
            pltpu.VMEM((2, rows, 8, LANES), jnp.float32),
            pltpu.VMEM((len(blocks), rows, ROWS, LANES), jnp.bfloat16),
            pltpu.SemaphoreType.DMA((len(blocks),)),
        ],
        compiler_params=PARAMS,
        name="pairs",
    )(*args)


def hop(value, dy, dx, dcore):
    moves = []
    for y in range(SIDE):
        for x in range(SIDE):
            for core in range(2):
                way = 1 - 2 * core
                target = ((y + way * dy) % SIDE * SIDE + (x + way * dx) % SIDE) * 2 + (core + dcore) % 2
                moves.append(((y * SIDE + x) * 2 + core, target))
    return lax.ppermute(value, "tile", moves)


def on_device(waves, station_mask, pair_local, pair_remote, pair_count):
    width, tiles = waves.shape[-1], pair_remote.shape[1]
    events, stations = station_mask.shape
    groups = lax.axis_size("sta")
    here = lax.axis_index("tile")
    place = jnp.stack([here // (2 * SIDE), here // 2 % SIDE, here % 2]).astype(jnp.int32)
    local, count = pair_local.reshape(-1), pair_count.reshape(-1)

    other = hop(pair_remote, 0, 0, 1)
    own = own_spectra(waves, station_mask, jnp.asarray(forward_table(width)), pair_remote, other)
    power = own_power(own)

    along = lambda half, value, hops: hop(value, *((0, hops) if half == 0 else (hops, 0)), 0)
    rings = [(half, hops) for hops in (1, SIDE - 1) for half in range(2)]
    came = [along(half, own[half], hops) for half, hops in rings]
    passed = [along(half, value, hops) for (half, hops), value in zip(rings, split(came))]
    held = [[own[half], *came[half::2], *passed[half::2]] for half in range(2)]
    across = lambda half, value, hops, other: hop(value, *((hops, 0) if half == 0 else (0, hops)), other)

    plan = tuple(((*where, 0), (*where, 1)) for where in rings)
    packed = pack(plan, place, held, [local])
    got = [across(where[0], value, where[1], 0) for value, where in zip(packed, rings)]
    distant = [(half, 2, other) for other in range(2) for half in range(2)]
    rest = pack(
        tuple((where,) for where in distant)
        + (((0, 0, 0), (1, 0, 0)), ((0, 0, 1), (1, 0, 1))),
        place,
        held,
        packed[:1],
    )
    far = [across(where[0], value, *where[1:]) for value, where in zip(rest, distant)]
    size = SIDE * SLOTS
    swapped = hop(join(got, rest[5]), 0, 0, 1)

    table = jnp.asarray(lag_table(width))
    calc = functools.partial(pairs, place=place, local=local, count=count, table=table, own=own, power=power)
    near = [(half, 0) for half in range(2)]
    blocks = tuple((half, 0, 0, 4, half * size) for half in range(2))
    blocks += tuple((*where, 0, number, 0) for number, where in enumerate(rings))
    total = calc(blocks, partner=got + [rest[4]], total=None, last=False)[0]
    blocks = tuple((*where, 1, 0, number * size) for number, where in enumerate(rings + near))
    total = calc(blocks, partner=[swapped], total=total, last=False)[0]
    blocks = tuple((*where, number, 0) for number, where in enumerate(distant))
    total, stack = calc(blocks, partner=far, total=total, last=True)

    stack = lax.all_to_all(stack, "sta", split_axis=0, concat_axis=0, tiled=True)
    stack = jnp.sum(stack.reshape(groups, LAGS // groups, -1), axis=0).T
    station_coef = total.astype(jnp.bfloat16).reshape(1, tiles, SLOTS, stations, LAGS)
    return (station_coef, stack.reshape(1, tiles, SLOTS, LAGS // groups))


def solution(mesh):
    placed = (
        P("tile", None, "sta", None),
        P("tile", "sta"),
        P("tile", None, None),
        P("tile", None, None),
        P("tile", None),
    )
    return jax.shard_map(
        on_device,
        mesh=mesh,
        in_specs=placed,
        out_specs=(P("tile", None, None, "sta", None), P("tile", None, None, "sta")),
        check_vma=False,
    )
```
